128 devices in a mesh: wide: 16 (over z, y), narrow: 8 (over x, core).
Axes of the slice: x: 4, y: 4, z: 4, core: 2. Of those that a mesh axis runs over, the one named last changes fastest.
Arguments:
- material_flow_vector: float32 [3, 256, 256, 512], P(None, 'wide', 'narrow'), may hold values from -6 to 6
- tool_push_density: float32 [3, 256, 256, 512], P(None, 'wide', 'narrow'), may hold values from -6 to 6
- tool_warmth_excess: float32 [256, 256, 512], P('wide', 'narrow'), may hold values from 0.7 to 1.3
- substrate_warmth_excess: float32 [256, 256, 128], P('wide', 'narrow'), may hold values from -6 to 6
- spread_coefficient: float32 [256, 256, 128], P('wide', 'narrow'), may hold values from 0.02 to 0.08
- source_owner_sheet: int32 [262144, 1], P(('wide', 'narrow')), may hold values from 0 to 15; in each aligned block of 2048 rows (0 to 2047, 2048 to 4095, ...) at most 384 rows name the same one
- source_part_line: int32 [262144], P(('wide', 'narrow')), may hold values from 0 to 511
Outputs:
- corrected_flow_vector: float32 [3, 256, 256, 512], P(None, 'wide', 'narrow')
- part_out: float32 [256, 256, 128], P('wide', 'narrow')
The draws below stay inside these ranges and needn't reach their ends.
Inputs may be any that keep to these rules, and one draw needn't show every extreme that they name: `source_owner_sheet`: among the 2048 blocks of one device, no slab is named by more than 384 of them.
All inputs are finite; a program needn't handle non-finite values.
Results may differ from the reference program's by a relative error of at most 0.00012.
Values sent between devices are 32-bit elements; how exact they have to be, the bound alone decides.
A program may use at most 128 MiB of HBM per device.

```python
import math
import jax
import jax.numpy as jnp
import numpy as np

NX = 256
NY = 256
NZ = 512
PASSES = 2
STEPS = 3
SPAN_DEPTH = 128
PZD = 16
PYD = 32
XL = 16
YL = 32
NZB = 4
HBLK = 2048
CAP = 384
PR = 512
SPAN_ALTITUDE = 256
SPAN_BREADTH = 256
N_WIDE = 16
N_NARROW = 8


def place_ends(result, stream_key, low, top_value):
    spot = [jax.random.randint(jax.random.fold_in(stream_key, axis), (), 0, length) for axis, length in enumerate(result.shape)]
    main_axis = result.shape.index(max(result.shape))
    neighbour = spot[:main_axis] + [(spot[main_axis] + 1) % result.shape[main_axis]] + spot[main_axis + 1:]
    return result.at[tuple(spot)].set(low).at[tuple(neighbour)].set(top_value)


def block_levels(stream_key, extent, split, low, largest):
    def one(dim, parts):
        heights = jax.random.uniform(jax.random.fold_in(jax.random.fold_in(stream_key, 6), dim), (parts,), jnp.float32, low / len(split), largest / len(split))
        return jnp.repeat(jnp.exp(heights), extent[dim] // parts).reshape((-1,) + (1,) * (len(extent) - dim - 1))

    level = one(*split[0])
    for cut in split[1:]:
        level = level * one(*cut)
    return level


def routed_block(rng, own, number, rows, count, top, most, slope):
    ranking = jax.random.permutation(rng, count)
    heavy_load, common = load_shares(count, rows * top, most, slope, True), load_shares(count, rows * top, most, slope, False)
    places = jnp.arange(count)

    def named(tallies, offset_by):
        used = int((tallies > 0).sum())
        fixed = max(1, used // 4)
        shifted = fixed + (places - fixed + offset_by * (used - fixed)) % max(1, count - fixed)
        return jnp.zeros((count,), jnp.int32).at[ranking[jnp.where(places < fixed, places, shifted)]].set(jnp.asarray(tallies, jnp.int32))

    tallies = jnp.where(number % 4 == 0, named(heavy_load, number // 4), named(common, number - number // 4 - 1))
    mixed = jax.random.permutation(jax.random.fold_in(own, 3), count)
    donor, sink = mixed[0:count // 2 * 2:2], mixed[1:count // 2 * 2:2]
    room = jnp.minimum(tallies[donor] - 1, most - tallies[sink]) // 2
    room = jnp.where((donor == ranking[0]) | (sink == ranking[0]) | (tallies[sink] == 0), 0, jnp.maximum(room, 0))
    shifted = jax.random.randint(jax.random.fold_in(own, 4), (count // 2,), 0, 1 << 20) % (room + 1)
    tallies = tallies.at[donor].add(-shifted).at[sink].add(shifted)
    items = jnp.searchsorted(jnp.cumsum(tallies), jnp.arange(rows * top), side="right").astype(jnp.int32)
    listing = items.reshape(top, rows).T
    listing = listing[jax.random.permutation(jax.random.fold_in(own, 1), rows)]
    offset_by = jax.random.randint(jax.random.fold_in(own, 2), (rows, 1), 0, top)
    return jnp.take_along_axis(listing, (jnp.arange(top)[None, :] + offset_by) % top, axis=1)


def load_shares(number_of, total, limit, slope, full):
    weights = [(1 << 20) // math.isqrt(standing ** slope) + 1 for standing in range(1, number_of + 1)]
    largest = limit if full else min(limit, max(-(-total // number_of), total * weights[0] // sum(weights)))
    least = 1 if total - largest >= number_of - 1 else 0
    given, spare = [largest] + [least] * (number_of - 1), total - largest - least * (number_of - 1)
    while spare > 0:
        candidates = [i for i in range(1, number_of) if given[i] < largest] or [i for i in range(1, number_of) if given[i] < limit]
        mass, budget = sum([weights[i] for i in candidates]), spare
        for i in candidates:
            addition = min(limit - given[i], max(1, budget * weights[i] // mass), spare)
            given[i] = given[i] + addition
            spare = spare - addition
    return np.array(given)


def scatter_about(stream_key, dims, deviation, bound, cuts=(), held_as=jnp.bfloat16):
    loudness = block_levels(stream_key, dims, cuts, -0.22, 0.18) if cuts else 1.0
    drawn = jax.random.normal(stream_key, dims, jnp.float32) * deviation * loudness
    return jnp.minimum(jnp.maximum(drawn, -bound), bound).astype(held_as)


def setup_inputs(seed: int = 0) -> dict:
    keys = jax.random.split(jax.random.key(seed), 8)
    material_flow_vector = scatter_about(keys[0], (3, NX, NY, NZ), 1.0, 6.0, ((1, 16), (2, 8)), jnp.float32)
    tool_push_density = scatter_about(keys[1], (3, NX, NY, NZ), 1.0, 6.0, ((1, 16), (2, 8)), jnp.float32)
    tool_warmth_excess = jnp.clip(0.7 + 0.59999996 * jax.random.uniform(keys[2], (NX, NY, NZ), jnp.float32) ** block_levels(keys[2], (NX, NY, NZ), ((0, 16), (1, 8)), -0.2, 0.2), 0.7, 1.3)
    substrate_warmth_excess = scatter_about(keys[3], (SPAN_ALTITUDE, SPAN_BREADTH, SPAN_DEPTH), 1.0, 6.0, ((0, 16), (1, 8)), jnp.float32)
    spread_coefficient = jnp.clip(jnp.exp(math.log(0.08) - 1.3862944 * jax.random.uniform(keys[4], (SPAN_ALTITUDE, SPAN_BREADTH, SPAN_DEPTH), jnp.float32) ** block_levels(keys[4], (SPAN_ALTITUDE, SPAN_BREADTH, SPAN_DEPTH), ((0, 16), (1, 8)), -0.2, 0.2)), 0.02, 0.08)
    source_owner_sheet_keys = jax.random.split(jax.random.fold_in(keys[5], 1), (N_WIDE * N_NARROW * HBLK) // HBLK)
    source_owner_sheet_turns = jax.random.permutation(jax.random.fold_in(keys[5], 3), (N_WIDE * N_NARROW * HBLK) // HBLK)
    source_owner_sheet = jax.vmap(lambda own, number: routed_block(jax.random.fold_in(keys[5], 2), own, number, HBLK, N_WIDE, 1, CAP, 2))(source_owner_sheet_keys, source_owner_sheet_turns).reshape((N_WIDE * N_NARROW * HBLK, 1))
    source_part_line = place_ends(jax.random.randint(keys[6], (N_WIDE * N_NARROW * HBLK,), 0, PR), jax.random.fold_in(keys[6], 1), 0, PR - 1).astype(jnp.int32)
    return dict(material_flow_vector=material_flow_vector, tool_push_density=tool_push_density, tool_warmth_excess=tool_warmth_excess, substrate_warmth_excess=substrate_warmth_excess, spread_coefficient=spread_coefficient, source_owner_sheet=source_owner_sheet, source_part_line=source_part_line)


time_step = 0.15
rate_base = 0.5
zener_energy = 4.0
stress_exponent = 5.0
penalty = 0.001
dissipation_factor = 0.1

def central(field, axis):
    return (jnp.roll(field, -1, axis) - jnp.roll(field, 1, axis)) * 0.5

def rate_squared(current):
    s_xx = central(current[0], 0)
    s_yy = central(current[1], 1)
    s_zz = central(current[2], 2)
    s_xy = 0.5 * (central(current[0], 1) + central(current[1], 0))
    s_xz = 0.5 * (central(current[0], 2) + central(current[2], 0))
    s_yz = 0.5 * (central(current[1], 2) + central(current[2], 1))
    total = s_xx ** 2 + s_yy ** 2 + s_zz ** 2 + 2.0 * (s_xy ** 2 + s_xz ** 2 + s_yz ** 2)
    return rate_base ** 2 + 2.0 * total

def inverse_sinh(value):
    return jnp.log(value + jnp.sqrt(value * value + 1.0))

def viscosity(rate_sq, zener):
    rate = jnp.sqrt(rate_sq)
    return inverse_sinh((rate * zener) ** (1.0 / stress_exponent)) / (3.0 * rate)

def viscous_term(mu_field, current):
    total = jnp.zeros_like(current)
    for axis in range(3):
        mu_ahead = jnp.roll(mu_field, -1, axis)
        mu_behind = jnp.roll(mu_field, 1, axis)
        vel_ahead = jnp.roll(current, -1, axis + 1)
        vel_behind = jnp.roll(current, 1, axis + 1)
        total = total + 0.5 * (mu_field + mu_ahead) * (vel_ahead - current) - 0.5 * (mu_field + mu_behind) * (current - vel_behind)
    return total

def sine_squared(count):
    waves = jnp.arange(count, dtype=jnp.int32).astype(jnp.float32)
    return jnp.sin(waves * (2.0 * math.pi / count)) ** 2

def reference(material_flow_vector, tool_push_density, tool_warmth_excess, substrate_warmth_excess, spread_coefficient, source_owner_sheet, source_part_line):
    zener = jnp.exp(zener_energy * (1.0 / tool_warmth_excess - 1.0))
    current = material_flow_vector
    rate_sq = rate_squared(current)
    mu_field = viscosity(rate_sq, zener)
    for section in range(PASSES):
        rate_sq = rate_squared(current)
        mu_field = viscosity(rate_sq, zener)
        current = material_flow_vector + time_step * (viscous_term(mu_field, material_flow_vector) + tool_push_density)
    heat = mu_field * (rate_sq - rate_base ** 2)
    divergence = central(current[0], 0) + central(current[1], 1) + central(current[2], 2)
    spectrum = jnp.fft.fftn(divergence)
    symbol = sine_squared(NX)[:, None, None] + sine_squared(NY)[None, :, None] + sine_squared(NZ)[None, None, :]
    pressure = jnp.real(jnp.fft.ifftn(-spectrum / (symbol + penalty)))
    gradient = jnp.stack([central(pressure, 0), central(pressure, 1), central(pressure, 2)])
    corrected_flow_vector = current - gradient
    blocks = heat.reshape(N_WIDE, XL, N_NARROW, YL, NZB, 128).transpose(0, 2, 1, 3, 4, 5).reshape(-1, 128)
    numbers = jnp.arange(N_WIDE * N_NARROW * HBLK, dtype=jnp.int32)
    narrow_of = numbers // HBLK % N_NARROW
    target = (source_owner_sheet[:, 0] * N_NARROW + narrow_of) * PR + source_part_line
    summed = jnp.zeros((N_WIDE * N_NARROW * PR, 128), jnp.float32).at[target].add(blocks)
    substrate_energy_input = summed.reshape(N_WIDE, N_NARROW, PZD, PYD, 128).transpose(0, 2, 1, 3, 4).reshape(SPAN_ALTITUDE, SPAN_BREADTH, SPAN_DEPTH)
    thermal_profile = substrate_warmth_excess + dissipation_factor * substrate_energy_input
    for section in range(STEPS):
        bordered_array = jnp.pad(thermal_profile, 1)
        neighbour_voxels = bordered_array[2:, 1:-1, 1:-1] + bordered_array[:-2, 1:-1, 1:-1]
        neighbour_voxels = neighbour_voxels + bordered_array[1:-1, 2:, 1:-1] + bordered_array[1:-1, :-2, 1:-1]
        neighbour_voxels = neighbour_voxels + bordered_array[1:-1, 1:-1, 2:] + bordered_array[1:-1, 1:-1, :-2]
        thermal_profile = thermal_profile + spread_coefficient * (neighbour_voxels - 6.0 * thermal_profile)
    return (corrected_flow_vector, thermal_profile)
```

```python
import functools
import math

import jax
import jax.numpy as jnp
import ml_dtypes
import numpy as np
from jax import lax
from jax.experimental import pallas as pl
from jax.experimental.pallas import tpu as pltpu
from jax.sharding import PartitionSpec as P

PASSES = 2
STEPS = 3
MESH = pl.DeviceIdType.MESH
F32 = jnp.float32
BF16 = jnp.bfloat16
VM = pl.BlockSpec(memory_space=pltpu.VMEM)

time_step = 0.15
rate_base = 0.5
zener_energy = 4.0
stress_exponent = 5.0
penalty = 0.001
dissipation_factor = 0.1
GROUPS = 2


def shifted(x, axis, up, wrap):
    size = lax.axis_size(axis)
    pairs = [(i, (i + 1) % size) for i in range(size if wrap else size - 1)]
    if not up:
        pairs = [(j, i) for i, j in pairs]
    return lax.ppermute(x, axis, pairs)


def with_halo(x, sides, width, wrap):
    for axis, dim in sides:
        length = x.shape[dim]
        last = lax.slice_in_dim(x, length - width, length, axis=dim)
        initial = lax.slice_in_dim(x, 0, width, axis=dim)
        before = shifted(last, axis, True, wrap)
        after = shifted(initial, axis, False, wrap)
        x = jnp.concatenate([before, x, after], axis=dim)
    return x


def pad_cells(field):
    return with_halo(field, (("wide", 1), ("narrow", 2)), 1, True)


def gradients(bordered_array):
    center = bordered_array[:, 1:-1, 1:-1]
    along_x = (bordered_array[:, 2:, 1:-1] - bordered_array[:, :-2, 1:-1]) * 0.5
    along_y = (bordered_array[:, 1:-1, 2:] - bordered_array[:, 1:-1, :-2]) * 0.5
    along_z = (jnp.roll(center, -1, 3) - jnp.roll(center, 1, 3)) * 0.5
    return (along_x, along_y, along_z)


def rate_squared(bordered_array):
    along_x, along_y, along_z = gradients(bordered_array)
    s_xy = 0.5 * (along_y[0] + along_x[1])
    s_xz = 0.5 * (along_z[0] + along_x[2])
    s_yz = 0.5 * (along_z[1] + along_y[2])
    total = (
        along_x[0] ** 2 + along_y[1] ** 2 + along_z[2] ** 2 + 2.0 * (s_xy**2 + s_xz**2 + s_yz**2)
    )
    return rate_base**2 + 2.0 * total


def inverse_sinh(value):
    return jnp.log(value + jnp.sqrt(value * value + 1.0))


def viscosity(rate_sq, zener):
    rate = jnp.sqrt(rate_sq)
    return inverse_sinh((rate * zener) ** (1.0 / stress_exponent)) / (3.0 * rate)


def viscous_term(mu_padded, vel_padded):
    mu_center = mu_padded[1:-1, 1:-1]
    vel_center = vel_padded[:, 1:-1, 1:-1]
    total = 0.5 * (mu_center + mu_padded[2:, 1:-1]) * (
        vel_padded[:, 2:, 1:-1] - vel_center
    ) - 0.5 * (mu_center + mu_padded[:-2, 1:-1]) * (vel_center - vel_padded[:, :-2, 1:-1])
    total = (
        total
        + 0.5 * (mu_center + mu_padded[1:-1, 2:]) * (vel_padded[:, 1:-1, 2:] - vel_center)
        - 0.5 * (mu_center + mu_padded[1:-1, :-2]) * (vel_center - vel_padded[:, 1:-1, :-2])
    )
    total = (
        total
        + 0.5
        * (mu_center + jnp.roll(mu_center, -1, 2))
        * (jnp.roll(vel_center, -1, 3) - vel_center)
        - 0.5 * (mu_center + jnp.roll(mu_center, 1, 2)) * (vel_center - jnp.roll(vel_center, 1, 3))
    )
    return total


def real_basis(length):
    cells = np.arange(length, dtype=np.float64)
    rows = [np.full(length, 1.0 / math.sqrt(length)), (-1.0) ** cells / math.sqrt(length)]
    waves = [0, length // 2]
    for k in range(1, length // 2):
        angle = 2.0 * math.pi * k * cells / length
        rows.append(np.cos(angle) * math.sqrt(2.0 / length))
        rows.append(np.sin(angle) * math.sqrt(2.0 / length))
        waves += [k, k]
    waves = np.array(waves)
    symbol = np.sin(2.0 * math.pi * (waves % (length // 2)) / length) ** 2
    return np.stack(rows), symbol


def split_table(table):
    high = table.astype(np.float32).astype(ml_dtypes.bfloat16)
    low = (table - high.astype(np.float64)).astype(np.float32).astype(ml_dtypes.bfloat16)
    return [high, low]


def pressure_tables(n_y, n_z, n_narrow):
    basis_z, symbol_z = real_basis(n_z)
    basis_y, symbol_y = real_basis(n_y)
    forward = basis_z.T
    swapped = forward.reshape(n_z, n_z // 128, 2, 64)[:, :, ::-1].reshape(n_z, n_z)
    tables = []
    for table in (forward, swapped, forward.T, swapped.T, basis_y, basis_y.T):
        tables += split_table(np.ascontiguousarray(table))
    s_y = np.broadcast_to(symbol_y[:, None], (n_y, 128)).astype(np.float32)
    s_z = np.tile(symbol_z.reshape(n_narrow, 1, 64), (1, 8, 2)).astype(np.float32)
    return tables + [s_y, s_z]


def split_value(x):
    high = x.astype(BF16)
    return high, (x - high.astype(F32)).astype(BF16)


def dot_left(x, high, low):
    x_high, x_low = split_value(x)
    dot = functools.partial(jnp.dot, preferred_element_type=F32)
    return dot(x_high, high) + (dot(x_high, low) + dot(x_low, high))


def dot_right(high, low, x):
    x_high, x_low = split_value(x)
    dot = functools.partial(jnp.dot, preferred_element_type=F32)
    return dot(high, x_high) + (dot(low, x_high) + dot(high, x_low))


def pressure_kernel(
    n_wide, n_narrow,
    div, fe_h, fe_l, fo_h, fo_l, ie_h, ie_l, io_h, io_l, cy_h, cy_l, iy_h, iy_l, s_y, s_z,
    press, y_halo,
    zsend, rbuf, ubuf, vsend, zrecv, rtab, mom, mrecv, absend, ab, xrecv, yrecv, ysend,
    nf_send, nf_recv, nb_send, nb_recv, wf_send, wf_recv, wb_send, wb_recv, h_send, h_recv,
):
    w = lax.axis_index("wide")
    n = lax.axis_index("narrow")
    xps, _, rows, n_z = div.shape
    n_y = s_y.shape[0]
    per = xps // GROUPS
    chunk_rows = n_y // n_wide

    def across(k):
        return lax.rem(n + k, n_narrow)

    def along(k):
        return lax.rem(w + k, n_wide)

    barrier = pltpu.get_barrier_semaphore()

    def greet_n(k, c):
        pl.semaphore_signal(barrier, inc=1, device_id=(w, across(k)), device_id_type=MESH)
        return c

    def greet_w(k, c):
        pl.semaphore_signal(barrier, inc=1, device_id=(along(k), n), device_id_type=MESH)
        return c

    lax.fori_loop(1, n_narrow, greet_n, 0)
    lax.fori_loop(1, n_wide, greet_w, 0)

    lane = lax.broadcasted_iota(jnp.int32, (per * rows, 128), 1)
    low_half = lane < 64

    def forward_copy(g, k):
        to = across(k)
        return pltpu.make_async_remote_copy(
            src_ref=zsend.at[to, pl.ds(g * per, per)],
            dst_ref=rbuf.at[pl.ds(g * per, per), pl.ds(pl.multiple_of(n * rows, rows), rows)],
            send_sem=nf_send.at[g, k],
            recv_sem=nf_recv.at[g, k],
            device_id=(w, to),
            device_id_type=MESH,
        )

    def forward_arrival(g, k):
        source = across(n_narrow - k)
        here = rbuf.at[pl.ds(g * per, per), pl.ds(pl.multiple_of(source * rows, rows), rows)]
        return pltpu.make_async_remote_copy(
            src_ref=here, dst_ref=here, send_sem=nf_send.at[g, k], recv_sem=nf_recv.at[g, k],
            device_id=(w, source), device_id_type=MESH,
        )

    for g in range(GROUPS):
        even = div[g * per:(g + 1) * per, 0].reshape(per * rows, n_z)
        odd = div[g * per:(g + 1) * per, 1].reshape(per * rows, n_z)
        even = dot_left(even, fe_h[...], fe_l[...])
        odd = dot_left(odd, fo_h[...], fo_l[...])
        for m in range(n_z // 128):
            e = even[:, 128 * m:128 * (m + 1)]
            o = odd[:, 128 * m:128 * (m + 1)]
            first = jnp.where(low_half, e, o)
            second = jnp.where(low_half, o, e)
            zsend[2 * m, g * per:(g + 1) * per] = first.reshape(per, rows, 128)
            zsend[2 * m + 1, g * per:(g + 1) * per] = second.reshape(per, rows, 128)
        if g == 0:
            pl.semaphore_wait(barrier, n_narrow - 1 + n_wide - 1)

        def launch(k, c):
            forward_copy(g, k).start()
            return c

        lax.fori_loop(1, n_narrow, launch, 0)

    s = s_y[...] + s_z[n][0:1, :] + penalty
    root = jnp.sqrt(s * (1.0 + s))
    rtab[0] = 1.0 / (1.0 + 2.0 * s + 2.0 * root)
    rtab[1] = -1.0 / root

    for g in range(GROUPS):
        span = slice(g * per, (g + 1) * per)
        rbuf[span, pl.ds(pl.multiple_of(n * rows, rows), rows)] = zsend[n, span]

        def arrive(k, c):
            forward_arrival(g, k).wait_recv()
            return c

        lax.fori_loop(1, n_narrow, arrive, 0)
        lines = jnp.concatenate([rbuf[xp] for xp in range(g * per, (g + 1) * per)], axis=1)
        lines = dot_right(cy_h[...], cy_l[...], lines)
        for i in range(per):
            ubuf[g * per + i] = lines[:, 128 * i:128 * (i + 1)]

    block = 16

    def moments(i, c):
        here = pl.ds(pl.multiple_of(i * block, block), block)
        r = rtab[0, here]
        f = ubuf[0, here]
        b = ubuf[xps - 1, here]
        for xp in range(1, xps):
            f = f * r + ubuf[xp, here]
            b = b * r + ubuf[xps - 1 - xp, here]
        mom[0, here] = f
        mom[1, here] = b
        return c

    lax.fori_loop(0, n_y // block, moments, 0)

    def chunk(index):
        return pl.ds(pl.multiple_of(index * chunk_rows, chunk_rows), chunk_rows)

    def out_copy(k):
        to = along(k)
        return pltpu.make_async_remote_copy(
            src_ref=mom.at[:, chunk(to)], dst_ref=mrecv.at[w],
            send_sem=wf_send.at[k], recv_sem=wf_recv.at[k],
            device_id=(to, n), device_id_type=MESH,
        )

    def out_arrival(k):
        here = mrecv.at[along(n_wide - k)]
        return pltpu.make_async_remote_copy(
            src_ref=here, dst_ref=here, send_sem=wf_send.at[k], recv_sem=wf_recv.at[k],
            device_id=(along(n_wide - k), n), device_id_type=MESH,
        )

    def back_copy(k):
        to = along(k)
        return pltpu.make_async_remote_copy(
            src_ref=absend.at[to], dst_ref=ab.at[:, chunk(w)],
            send_sem=wb_send.at[k], recv_sem=wb_recv.at[k],
            device_id=(to, n), device_id_type=MESH,
        )

    def back_arrival(k):
        here = ab.at[:, chunk(along(n_wide - k))]
        return pltpu.make_async_remote_copy(
            src_ref=here, dst_ref=here, send_sem=wb_send.at[k], recv_sem=wb_recv.at[k],
            device_id=(along(n_wide - k), n), device_id_type=MESH,
        )

    def each(count, action):
        def body(k, c):
            action(k)
            return c

        lax.fori_loop(1, count, body, 0)

    each(n_wide, lambda k: out_copy(k).start())
    mrecv[w] = mom[:, chunk(w)]
    r = rtab[0, chunk(w)]
    q = r
    for _ in range(int(math.log2(xps))):
        q = q * q
    total = q
    for _ in range(int(math.log2(n_wide))):
        total = total * total
    closing = 1.0 / (1.0 - total)
    each(n_wide, lambda k: out_arrival(k).wait_recv())
    f = mrecv[0, 0]
    b = mrecv[n_wide - 1, 1]
    for j in range(1, n_wide):
        f = f * q + mrecv[j, 0]
        b = b * q + mrecv[n_wide - 1 - j, 1]
    f = f * closing
    b = b * closing
    for j in range(n_wide):
        absend[j, 0] = f
        absend[n_wide - 1 - j, 1] = b
        f = f * q + mrecv[j, 0]
        b = b * q + mrecv[n_wide - 1 - j, 1]
    each(n_wide, lambda k: back_copy(k).start())
    ab[:, chunk(w)] = absend[w]
    each(n_wide, lambda k: back_arrival(k).wait_recv())

    def solve(i, c):
        here = pl.ds(pl.multiple_of(i * block, block), block)
        r = rtab[0, here]
        scale = rtab[1, here]
        f = ab[0, here]
        b = ab[1, here]
        behind = []
        for xp in range(xps - 1, -1, -1):
            rb = b * r
            behind.append(rb)
            b = rb + ubuf[xp, here]
        for xp in range(xps):
            f = f * r + ubuf[xp, here]
            ubuf[xp, here] = scale * (f + behind[xps - 1 - xp])
        return c

    lax.fori_loop(0, n_y // block, solve, 0)

    def backward_copy(g, k):
        to = across(k)
        return pltpu.make_async_remote_copy(
            src_ref=vsend.at[to, pl.ds(g * per, per)],
            dst_ref=zrecv.at[n, pl.ds(g * per, per)],
            send_sem=nb_send.at[g, k],
            recv_sem=nb_recv.at[g, k],
            device_id=(w, to),
            device_id_type=MESH,
        )

    def backward_arrival(g, k):
        source = across(n_narrow - k)
        here = zrecv.at[source, pl.ds(g * per, per)]
        return pltpu.make_async_remote_copy(
            src_ref=here, dst_ref=here, send_sem=nb_send.at[g, k], recv_sem=nb_recv.at[g, k],
            device_id=(w, source), device_id_type=MESH,
        )

    for g in range(GROUPS):
        span = slice(g * per, (g + 1) * per)
        lines = jnp.concatenate([ubuf[xp] for xp in range(g * per, (g + 1) * per)], axis=1)
        lines = dot_right(iy_h[...], iy_l[...], lines)
        for to in range(n_narrow):
            for i in range(per):
                vsend[to, g * per + i] = lines[to * rows:(to + 1) * rows, 128 * i:128 * (i + 1)]
        each(n_narrow, lambda k: backward_copy(g, k).start())
        zrecv[n, span] = vsend[n, span]

    wide_to = {0: along(n_wide - 1), 1: along(1)}
    narrow_to = {0: across(n_narrow - 1), 1: across(1)}

    def x_halo(side):
        source = 2 * xps if side else 1
        return pltpu.make_async_remote_copy(
            src_ref=press.at[source], dst_ref=xrecv.at[1 - side],
            send_sem=h_send.at[side], recv_sem=h_recv.at[1 - side],
            device_id=(wide_to[side], n), device_id_type=MESH,
        )

    def y_halo_copy(side):
        return pltpu.make_async_remote_copy(
            src_ref=ysend.at[side], dst_ref=yrecv.at[1 - side],
            send_sem=h_send.at[2 + side], recv_sem=h_recv.at[3 - side],
            device_id=(w, narrow_to[side]), device_id_type=MESH,
        )

    for g in range(GROUPS):
        each(n_narrow, lambda k: backward_arrival(g, k).wait_recv())
        evens, odds = [], []
        for m in range(n_z // 128):
            first = zrecv[2 * m, g * per:(g + 1) * per].reshape(per * rows, 128)
            second = zrecv[2 * m + 1, g * per:(g + 1) * per].reshape(per * rows, 128)
            evens.append(jnp.where(low_half, first, second))
            odds.append(jnp.where(low_half, second, first))
        even = dot_left(jnp.concatenate(evens, axis=1), ie_h[...], ie_l[...])
        odd = dot_left(jnp.concatenate(odds, axis=1), io_h[...], io_l[...])
        for i in range(per):
            for parity, part in ((0, even), (1, odd)):
                x = 2 * (g * per + i) + parity
                plane = part[i * rows:(i + 1) * rows]
                press[x + 1] = plane
                ysend[0, x] = plane[0]
                ysend[1, x] = plane[rows - 1]
        if g == 0:
            x_halo(0).start()
    x_halo(1).start()
    y_halo_copy(0).start()
    y_halo_copy(1).start()

    for g in range(GROUPS):
        each(n_narrow, lambda k: forward_copy(g, k).wait_send())
        each(n_narrow, lambda k: backward_copy(g, k).wait_send())
    each(n_wide, lambda k: out_copy(k).wait_send())
    each(n_wide, lambda k: back_copy(k).wait_send())
    for side in (0, 1):
        x_halo(side).wait()
        y_halo_copy(side).wait()
    press[0] = xrecv[0]
    press[2 * xps + 1] = xrecv[1]
    y_halo[...] = yrecv[...]


def solve_pressure(divergence):
    n_wide, n_narrow = lax.axis_size("wide"), lax.axis_size("narrow")
    x_local, rows, n_z = divergence.shape
    n_y = rows * n_narrow
    xps = x_local // 2
    tables = [jnp.asarray(t) for t in pressure_tables(n_y, n_z, n_narrow)]
    dma = pltpu.SemaphoreType.DMA
    field = (xps, n_y, 128)
    turned = (n_narrow, xps, rows, 128)
    chunk_rows = n_y // n_wide
    return pl.pallas_call(
        functools.partial(pressure_kernel, n_wide, n_narrow),
        out_shape=[
            jax.ShapeDtypeStruct((x_local + 2, rows, n_z), F32),
            jax.ShapeDtypeStruct((2, x_local, n_z), F32),
        ],
        in_specs=[VM] * (1 + len(tables)),
        out_specs=[VM, VM],
        scratch_shapes=[
            pltpu.VMEM(turned, F32),
            pltpu.VMEM(field, F32),
            pltpu.VMEM(field, F32),
            pltpu.VMEM(turned, F32),
            pltpu.VMEM(turned, F32),
            pltpu.VMEM((2, n_y, 128), F32),
            pltpu.VMEM((2, n_y, 128), F32),
            pltpu.VMEM((n_wide, 2, chunk_rows, 128), F32),
            pltpu.VMEM((n_wide, 2, chunk_rows, 128), F32),
            pltpu.VMEM((2, n_y, 128), F32),
            pltpu.VMEM((2, rows, n_z), F32),
            pltpu.VMEM((2, x_local, n_z), F32),
            pltpu.VMEM((2, x_local, n_z), F32),
            dma((GROUPS, n_narrow)),
            dma((GROUPS, n_narrow)),
            dma((GROUPS, n_narrow)),
            dma((GROUPS, n_narrow)),
            dma((n_wide,)),
            dma((n_wide,)),
            dma((n_wide,)),
            dma((n_wide,)),
            dma((4,)),
            dma((4,)),
        ],
        compiler_params=pltpu.CompilerParams(
            collective_id=1, has_side_effects=True, vmem_limit_bytes=40 * 2**20
        ),
        name="pressure",
    )(divergence.reshape(xps, 2, rows, n_z), *tables)


def y_step(plane, before, after, ahead):
    rows = plane.shape[0]
    row = lax.broadcasted_iota(jnp.int32, plane.shape, 0)
    if ahead:
        return jnp.where(row == rows - 1, after, pltpu.roll(plane, rows - 1, 0))
    return jnp.where(row == 0, before, pltpu.roll(plane, 1, 0))


def project_kernel(press, y_halo, current, out):
    step = pl.program_id(0)
    n_z = press.shape[2]
    for i in range(current.shape[1]):
        x = step * current.shape[1] + i
        p = press[x + 1]
        before = y_halo[0, pl.ds(x, 1)]
        after = y_halo[1, pl.ds(x, 1)]
        out[0, i] = current[0, i] - (press[x + 2] - press[x]) * 0.5
        out[1, i] = current[1, i] - 0.5 * (
            y_step(p, before, after, True) - y_step(p, before, after, False)
        )
        out[2, i] = current[2, i] - 0.5 * (pltpu.roll(p, n_z - 1, 1) - pltpu.roll(p, 1, 1))


def project(current, divergence):
    press, y_halo = solve_pressure(divergence)
    _, x_local, rows, n_z = current.shape
    planes = 2
    spec = pl.BlockSpec((3, planes, rows, n_z), lambda i: (0, i, 0, 0))
    return pl.pallas_call(
        project_kernel,
        grid=(x_local // planes,),
        out_shape=jax.ShapeDtypeStruct(current.shape, F32),
        in_specs=[VM, VM, spec],
        out_specs=spec,
        compiler_params=pltpu.CompilerParams(vmem_limit_bytes=20 * 2**20),
        name="projection",
    )(press, y_halo, current)


def conduct(thermal_profile, spread_wide):
    sides = (("wide", 0), ("narrow", 1))
    t = with_halo(thermal_profile, sides, STEPS, False)
    coefficient = spread_wide
    for _ in range(STEPS):
        center = t[1:-1, 1:-1]
        coefficient = coefficient[1:-1, 1:-1]
        around = t[2:, 1:-1] + t[:-2, 1:-1] + t[1:-1, 2:] + t[1:-1, :-2]
        ahead = jnp.pad(center[:, :, 1:], ((0, 0), (0, 0), (0, 1)))
        behind = jnp.pad(center[:, :, :-1], ((0, 0), (0, 0), (1, 0)))
        t = center + coefficient * (around + ahead + behind - 6.0 * center)
    return t


def per_device(
    material_flow_vector,
    tool_push_density,
    tool_warmth_excess,
    substrate_warmth_excess,
    spread_coefficient,
    source_owner_sheet,
    source_part_line,
):
    zener = jnp.exp(zener_energy * (1.0 / tool_warmth_excess - 1.0))
    base_pad = pad_cells(material_flow_vector)
    current_pad = base_pad
    current = material_flow_vector
    for section in range(PASSES):
        rate_sq = rate_squared(current_pad)
        mu_field = viscosity(rate_sq, zener)
        mu_padded = pad_cells(mu_field[None])[0]
        current = material_flow_vector + time_step * (
            viscous_term(mu_padded, base_pad) + tool_push_density
        )
        if section + 1 < PASSES:
            current_pad = pad_cells(current)
    heat_cells = mu_field * (rate_sq - rate_base**2)
    along_x, along_y, along_z = gradients(pad_cells(current))
    divergence = along_x[0] + along_y[1] + along_z[2]
    corrected_flow_vector = project(current, divergence)
    spread_wide = with_halo(spread_coefficient, (("wide", 0), ("narrow", 1)), STEPS, False)
    blocks = heat_cells.reshape(-1, 128)
    slab_ids = source_owner_sheet[:, 0]
    slab_count = lax.axis_size("wide")
    component_lines = substrate_warmth_excess.shape[0] * substrate_warmth_excess.shape[1]
    partial_value = (
        jnp.zeros((slab_count * component_lines, 128), jnp.float32)
        .at[slab_ids * component_lines + source_part_line]
        .add(blocks)
    )
    substrate_energy_input = lax.psum_scatter(
        partial_value.reshape(slab_count, component_lines, 128),
        "wide",
        scatter_dimension=0,
        tiled=True,
    )
    thermal_profile = substrate_warmth_excess + dissipation_factor * substrate_energy_input.reshape(
        substrate_warmth_excess.shape
    )
    return (corrected_flow_vector, conduct(thermal_profile, spread_wide))


def solution(mesh):
    return jax.shard_map(
        per_device,
        mesh=mesh,
        in_specs=(
            P(None, "wide", "narrow", None),
            P(None, "wide", "narrow", None),
            P("wide", "narrow", None),
            P("wide", "narrow", None),
            P("wide", "narrow", None),
            P(("wide", "narrow"), None),
            P(("wide", "narrow")),
        ),
        out_specs=(P(None, "wide", "narrow", None), P("wide", "narrow", None)),
        check_vma=False,
    )
```

```python
import functools
import math

import jax
import jax.numpy as jnp
import ml_dtypes
import numpy as np
from jax import lax
from jax.experimental import pallas as pl
from jax.experimental.pallas import tpu as pltpu
from jax.sharding import PartitionSpec as P

STEPS = 3
MESH = pl.DeviceIdType.MESH
F32 = jnp.float32
BF16 = jnp.bfloat16
VM = pl.BlockSpec(memory_space=pltpu.VMEM)

time_step = 0.15
rate_base = 0.5
zener_energy = 4.0
stress_exponent = 5.0
penalty = 0.001
dissipation_factor = 0.1
GROUPS = 2


def shifted(x, axis, up, wrap):
    size = lax.axis_size(axis)
    pairs = [(i, (i + 1) % size) for i in range(size if wrap else size - 1)]
    if not up:
        pairs = [(j, i) for i, j in pairs]
    return lax.ppermute(x, axis, pairs)


def with_halo(x, sides, width, wrap):
    for axis, dim in sides:
        length = x.shape[dim]
        last = lax.slice_in_dim(x, length - width, length, axis=dim)
        initial = lax.slice_in_dim(x, 0, width, axis=dim)
        before = shifted(last, axis, True, wrap)
        after = shifted(initial, axis, False, wrap)
        x = jnp.concatenate([before, x, after], axis=dim)
    return x


PAD = 8
STRIP = 8


def flow_kernel(
    n_wide, n_narrow,
    vel_in, push_in, warmth_in,
    mom, div, heat,
    velp, provp, mup0, mup1, lz, push,
    vel_ys, vel_yr, mu_ys0, mu_yr0, prov_ys, prov_yr, mu_ys1, mu_yr1, mom_ys, mom_yr, mom_xr,
    load_sem, h_send, h_recv,
):
    w = lax.axis_index("wide")
    n = lax.axis_index("narrow")
    _, planes, rows, n_z = vel_in.shape
    strips = rows // STRIP
    wide_to = (lax.rem(w + n_wide - 1, n_wide), lax.rem(w + 1, n_wide))
    narrow_to = (lax.rem(n + n_narrow - 1, n_narrow), lax.rem(n + 1, n_narrow))
    body = pl.ds(PAD, rows)

    barrier = pltpu.get_barrier_semaphore()
    for side in (0, 1):
        pl.semaphore_signal(barrier, inc=1, device_id=(wide_to[side], n), device_id_type=MESH)
        pl.semaphore_signal(barrier, inc=1, device_id=(w, narrow_to[side]), device_id_type=MESH)

    loads = [
        pltpu.make_async_copy(vel_in, velp.at[:, pl.ds(1, planes), body], load_sem.at[0]),
        pltpu.make_async_copy(warmth_in, lz, load_sem.at[1]),
        pltpu.make_async_copy(push_in, push, load_sem.at[2]),
    ]
    for load in loads:
        load.start()

    def wide_copy(e, side, source, target):
        return pltpu.make_async_remote_copy(
            src_ref=source, dst_ref=target,
            send_sem=h_send.at[e, side], recv_sem=h_recv.at[e, 1 - side],
            device_id=(wide_to[side], n), device_id_type=MESH,
        )

    def narrow_copy(e, side, sends, lands):
        return pltpu.make_async_remote_copy(
            src_ref=sends.at[side], dst_ref=lands.at[1 - side],
            send_sem=h_send.at[e, 2 + side], recv_sem=h_recv.at[e, 3 - side],
            device_id=(w, narrow_to[side]), device_id_type=MESH,
        )

    def x_pair(e, field, lead=()):
        return [
            wide_copy(e, 0, field.at[lead + (1, body)], field.at[lead + (planes + 1, body)]),
            wide_copy(e, 1, field.at[lead + (planes, body)], field.at[lead + (0, body)]),
        ]

    def y_pair(e, sends, lands):
        return [narrow_copy(e, side, sends, lands) for side in (0, 1)]

    def all_x(action, first=0, last=None):
        def step(x, c):
            action(x)
            return c

        lax.fori_loop(first, planes if last is None else last, step, 0)

    def y_fill(field, lands, comps):
        def fill(x):
            here = pl.ds(x, 1)
            if comps is None:
                field[x + 1, PAD - 1:PAD] = lands[0, here]
                field[x + 1, PAD + rows:PAD + rows + 1] = lands[1, here]
                return
            for i, c in enumerate(comps):
                field[c, x + 1, PAD - 1:PAD] = lands[0, i, here]
                field[c, x + 1, PAD + rows:PAD + rows + 1] = lands[1, i, here]

        all_x(fill)

    def z_ahead(a):
        return pltpu.roll(a, n_z - 1, 1)

    def z_behind(a):
        return pltpu.roll(a, 1, 1)

    loads[0].wait()

    def vel_rows(x):
        for c in range(3):
            vel_ys[0, c, pl.ds(x, 1)] = velp[c, x + 1, PAD:PAD + 1]
            vel_ys[1, c, pl.ds(x, 1)] = velp[c, x + 1, PAD + rows - 1:PAD + rows]

    all_x(vel_rows)
    pl.semaphore_wait(barrier, 4)
    every = slice(None)
    vel_x = x_pair(0, velp, (every,))
    vel_y = y_pair(0, vel_ys, vel_yr)
    for copy in vel_x + vel_y:
        copy.start()
    loads[1].wait()

    def zener_log(x):
        lz[x] = (zener_energy / stress_exponent) * (1.0 / lz[x] - 1.0)

    all_x(zener_log)
    loads[2].wait()

    def excess(src, x, r):
        here = slice(PAD + STRIP * r, PAD + STRIP * (r + 1))
        up = slice(PAD + STRIP * r + 1, PAD + STRIP * (r + 1) + 1)
        down = slice(PAD + STRIP * r - 1, PAD + STRIP * (r + 1) - 1)
        dx = [src[c, x + 2, here] - src[c, x, here] for c in range(3)]
        dy = [src[c, x + 1, up] - src[c, x + 1, down] for c in range(3)]
        mid = [src[c, x + 1, here] for c in range(3)]
        dz = [z_ahead(m) - z_behind(m) for m in mid]
        xy, xz, yz = dy[0] + dx[1], dz[0] + dx[2], dz[1] + dy[2]
        diagonal = dx[0] * dx[0] + dy[1] * dy[1] + dz[2] * dz[2]
        return 0.5 * diagonal + 0.25 * (xy * xy + xz * xz + yz * yz)

    def mu_plane(src, mup, ys, with_heat):
        def plane(x):
            for r in range(strips):
                part = slice(STRIP * r, STRIP * (r + 1))
                extra = excess(src, x, r)
                rate_sq = extra + rate_base**2
                v = jnp.exp((0.5 / stress_exponent) * jnp.log(rate_sq) + lz[x, part])
                mu = jnp.log(v + jnp.sqrt(v * v + 1.0)) * lax.rsqrt(rate_sq) * (1.0 / 3.0)
                mup[x + 1, PAD + STRIP * r:PAD + STRIP * (r + 1)] = mu
                if r == 0:
                    ys[0, pl.ds(x, 1)] = mu[0:1]
                if r == strips - 1:
                    ys[1, pl.ds(x, 1)] = mu[STRIP - 1:]
                if with_heat:
                    h = mu * extra
                    to = pl.ds(pl.multiple_of(x * rows + STRIP * r, STRIP), STRIP)
                    for m in range(n_z // 128):
                        heat[m, to] = h[:, 128 * m:128 * (m + 1)]

        return plane

    def advance_plane(mup, final):
        def plane(x):
            for r in range(strips):
                part = slice(STRIP * r, STRIP * (r + 1))
                here = slice(PAD + STRIP * r, PAD + STRIP * (r + 1))
                up = slice(PAD + STRIP * r + 1, PAD + STRIP * (r + 1) + 1)
                down = slice(PAD + STRIP * r - 1, PAD + STRIP * (r + 1) - 1)
                m = mup[x + 1, here]
                m_xp = m + mup[x + 2, here]
                m_xm = m + mup[x, here]
                m_yp = m + mup[x + 1, up]
                m_ym = m + mup[x + 1, down]
                m_z = m + z_ahead(m)
                for c in range(3):
                    u = velp[c, x + 1, here]
                    flux = m_z * (z_ahead(u) - u)
                    total = flux - z_behind(flux)
                    total += m_xp * (velp[c, x + 2, here] - u) - m_xm * (u - velp[c, x, here])
                    total += m_yp * (velp[c, x + 1, up] - u) - m_ym * (u - velp[c, x + 1, down])
                    new = u + (0.5 * time_step) * total + time_step * push[c, x, part]
                    provp[c, x + 1, here] = new
                    if final:
                        mom[c, x, part] = new
                        if c == 1:
                            if r == 0:
                                mom_ys[0, pl.ds(x, 1)] = new[0:1]
                            if r == strips - 1:
                                mom_ys[1, pl.ds(x, 1)] = new[STRIP - 1:]
                    else:
                        if r == 0:
                            prov_ys[0, c, pl.ds(x, 1)] = new[0:1]
                        if r == strips - 1:
                            prov_ys[1, c, pl.ds(x, 1)] = new[STRIP - 1:]

        return plane

    def stage(action, arriving_x, arriving_y, fill):
        for copy in arriving_y:
            copy.wait_recv()
        fill()
        all_x(action, 1, planes - 1)
        for copy in arriving_x:
            copy.wait_recv()
        all_x(lambda i: action(i * (planes - 1)), 0, 2)

    stage(mu_plane(velp, mup0, mu_ys0, False), vel_x, vel_y,
          lambda: y_fill(velp, vel_yr, (0, 1, 2)))
    mu_x0 = x_pair(1, mup0)
    mu_y0 = y_pair(1, mu_ys0, mu_yr0)
    for copy in mu_x0 + mu_y0:
        copy.start()
    stage(advance_plane(mup0, False), mu_x0, mu_y0, lambda: y_fill(mup0, mu_yr0, None))
    prov_x = x_pair(2, provp, (every,))
    prov_y = y_pair(2, prov_ys, prov_yr)
    for copy in prov_x + prov_y:
        copy.start()
    stage(mu_plane(provp, mup1, mu_ys1, True), prov_x, prov_y,
          lambda: y_fill(provp, prov_yr, (0, 1, 2)))
    mu_x1 = x_pair(3, mup1)
    mu_y1 = y_pair(3, mu_ys1, mu_yr1)
    for copy in mu_x1 + mu_y1:
        copy.start()
    for copy in prov_x + prov_y:
        copy.wait_send()
    stage(advance_plane(mup1, True), mu_x1, mu_y1, lambda: y_fill(mup1, mu_yr1, None))
    mom_x = [
        wide_copy(4, 0, mom.at[0, 0], mom_xr.at[1]),
        wide_copy(4, 1, mom.at[0, planes - 1], mom_xr.at[0]),
    ]
    mom_y = y_pair(4, mom_ys, mom_yr)
    for copy in mom_x + mom_y:
        copy.start()
    for copy in vel_x + vel_y + mu_x0 + mu_y0 + mu_x1 + mu_y1:
        copy.wait_send()

    def fill_rows():
        def fill(x):
            here = pl.ds(x, 1)
            provp[1, x + 1, PAD - 1:PAD] = mom_yr[0, here]
            provp[1, x + 1, PAD + rows:PAD + rows + 1] = mom_yr[1, here]

        all_x(fill)

    def div_plane(x):
        for r in range(strips):
            part = slice(STRIP * r, STRIP * (r + 1))
            here = slice(PAD + STRIP * r, PAD + STRIP * (r + 1))
            up = slice(PAD + STRIP * r + 1, PAD + STRIP * (r + 1) + 1)
            down = slice(PAD + STRIP * r - 1, PAD + STRIP * (r + 1) - 1)
            u = provp[2, x + 1, here]
            total = provp[0, x + 2, here] - provp[0, x, here]
            total += provp[1, x + 1, up] - provp[1, x + 1, down]
            div[x, part] = 0.5 * (total + (z_ahead(u) - z_behind(u)))

    for copy in mom_y:
        copy.wait_recv()
    fill_rows()
    all_x(div_plane, 1, planes - 1)
    for copy in mom_x:
        copy.wait_recv()
    provp[0, 0, body] = mom_xr[0]
    provp[0, planes + 1, body] = mom_xr[1]
    all_x(lambda i: div_plane(i * (planes - 1)), 0, 2)
    for copy in mom_x + mom_y:
        copy.wait_send()


def flow(velocity, push, warmth):
    n_wide, n_narrow = lax.axis_size("wide"), lax.axis_size("narrow")
    _, planes, rows, n_z = velocity.shape
    padded = (planes + 2, PAD + rows + PAD, n_z)
    line = (2, planes, n_z)
    lines = (2, 3, planes, n_z)
    any_space = pl.BlockSpec(memory_space=pl.ANY)
    shapes = [(3,) + padded, (3,) + padded, padded, padded, (planes, rows, n_z), velocity.shape]
    shapes += [lines, lines, line, line, lines, lines, line, line, line, line, (2, rows, n_z)]
    dma = pltpu.SemaphoreType.DMA
    return pl.pallas_call(
        functools.partial(flow_kernel, n_wide, n_narrow),
        out_shape=[
            jax.ShapeDtypeStruct(velocity.shape, F32),
            jax.ShapeDtypeStruct((planes, rows, n_z), F32),
            jax.ShapeDtypeStruct((n_z // 128, planes * rows, 128), F32),
        ],
        in_specs=[any_space] * 3,
        out_specs=[VM] * 3,
        scratch_shapes=[pltpu.VMEM(shape, F32) for shape in shapes]
        + [dma((3,)), dma((5, 4)), dma((5, 4))],
        compiler_params=pltpu.CompilerParams(
            collective_id=2, has_side_effects=True, vmem_limit_bytes=48 * 2**20
        ),
        name="flow",
    )(velocity, push, warmth)


def gather_kernel(target, heat, out, other):
    out[...] = jnp.zeros_like(out)
    other[...] = jnp.zeros_like(other)
    depth = heat.shape[0]

    def cell(i, c):
        for m in range(depth):
            into = out if m % 2 == 0 else other
            row = pl.ds(target[i * depth + m], 1)
            into[row] = into[row] + heat[m, pl.ds(i, 1)]
        return c

    lax.fori_loop(0, heat.shape[1], cell, 0, unroll=4)
    step = 256

    def join(i, c):
        here = pl.ds(pl.multiple_of(i * step, step), step)
        out[here] = out[here] + other[here]
        return c

    lax.fori_loop(0, out.shape[0] // step, join, 0)


def slab_heat(target, heat, lines):
    return pl.pallas_call(
        gather_kernel,
        out_shape=jax.ShapeDtypeStruct((lines, 128), F32),
        in_specs=[pl.BlockSpec(memory_space=pltpu.SMEM), VM],
        out_specs=VM,
        scratch_shapes=[pltpu.VMEM((lines, 128), F32)],
        compiler_params=pltpu.CompilerParams(vmem_limit_bytes=24 * 2**20),
        name="slab_heat",
    )(target, heat)


def real_basis(length):
    cells = np.arange(length, dtype=np.float64)
    rows = [np.full(length, 1.0 / math.sqrt(length)), (-1.0) ** cells / math.sqrt(length)]
    waves = [0, length // 2]
    for k in range(1, length // 2):
        angle = 2.0 * math.pi * k * cells / length
        rows.append(np.cos(angle) * math.sqrt(2.0 / length))
        rows.append(np.sin(angle) * math.sqrt(2.0 / length))
        waves += [k, k]
    waves = np.array(waves)
    symbol = np.sin(2.0 * math.pi * (waves % (length // 2)) / length) ** 2
    return np.stack(rows), symbol


def split_table(table):
    high = table.astype(np.float32).astype(ml_dtypes.bfloat16)
    low = (table - high.astype(np.float64)).astype(np.float32).astype(ml_dtypes.bfloat16)
    return [high, low]


def pressure_tables(n_y, n_z, n_narrow):
    basis_z, symbol_z = real_basis(n_z)
    basis_y, symbol_y = real_basis(n_y)
    forward = basis_z.T
    swapped = forward.reshape(n_z, n_z // 128, 2, 64)[:, :, ::-1].reshape(n_z, n_z)
    tables = []
    for table in (forward, swapped, forward.T, swapped.T, basis_y, basis_y.T):
        tables += split_table(np.ascontiguousarray(table))
    s_y = np.broadcast_to(symbol_y[:, None], (n_y, 128)).astype(np.float32)
    s_z = np.tile(symbol_z.reshape(n_narrow, 1, 64), (1, 8, 2)).astype(np.float32)
    return tables + [s_y, s_z]


def split_value(x):
    high = x.astype(BF16)
    return high, (x - high.astype(F32)).astype(BF16)


def dot_left(x, high, low):
    x_high, x_low = split_value(x)
    dot = functools.partial(jnp.dot, preferred_element_type=F32)
    return dot(x_high, high) + (dot(x_high, low) + dot(x_low, high))


def dot_right(high, low, x):
    x_high, x_low = split_value(x)
    dot = functools.partial(jnp.dot, preferred_element_type=F32)
    return dot(high, x_high) + (dot(low, x_high) + dot(high, x_low))


def pressure_kernel(
    n_wide, n_narrow,
    div, fe_h, fe_l, fo_h, fo_l, ie_h, ie_l, io_h, io_l, cy_h, cy_l, iy_h, iy_l, s_y, s_z,
    press, y_halo,
    zsend, rbuf, ubuf, vsend, zrecv, rtab, mom, mrecv, absend, ab, xrecv, yrecv, ysend,
    nf_send, nf_recv, nb_send, nb_recv, wf_send, wf_recv, wb_send, wb_recv, h_send, h_recv,
):
    w = lax.axis_index("wide")
    n = lax.axis_index("narrow")
    xps, _, rows, n_z = div.shape
    n_y = s_y.shape[0]
    per = xps // GROUPS
    chunk_rows = n_y // n_wide

    def across(k):
        return lax.rem(n + k, n_narrow)

    def along(k):
        return lax.rem(w + k, n_wide)

    barrier = pltpu.get_barrier_semaphore()

    def greet_n(k, c):
        pl.semaphore_signal(barrier, inc=1, device_id=(w, across(k)), device_id_type=MESH)
        return c

    def greet_w(k, c):
        pl.semaphore_signal(barrier, inc=1, device_id=(along(k), n), device_id_type=MESH)
        return c

    lax.fori_loop(1, n_narrow, greet_n, 0)
    lax.fori_loop(1, n_wide, greet_w, 0)

    lane = lax.broadcasted_iota(jnp.int32, (per * rows, 128), 1)
    low_half = lane < 64

    def forward_copy(g, k):
        to = across(k)
        return pltpu.make_async_remote_copy(
            src_ref=zsend.at[to, pl.ds(g * per, per)],
            dst_ref=rbuf.at[pl.ds(g * per, per), pl.ds(pl.multiple_of(n * rows, rows), rows)],
            send_sem=nf_send.at[g, k],
            recv_sem=nf_recv.at[g, k],
            device_id=(w, to),
            device_id_type=MESH,
        )

    def forward_arrival(g, k):
        source = across(n_narrow - k)
        here = rbuf.at[pl.ds(g * per, per), pl.ds(pl.multiple_of(source * rows, rows), rows)]
        return pltpu.make_async_remote_copy(
            src_ref=here, dst_ref=here, send_sem=nf_send.at[g, k], recv_sem=nf_recv.at[g, k],
            device_id=(w, source), device_id_type=MESH,
        )

    for g in range(GROUPS):
        even = div[g * per:(g + 1) * per, 0].reshape(per * rows, n_z)
        odd = div[g * per:(g + 1) * per, 1].reshape(per * rows, n_z)
        even = dot_left(even, fe_h[...], fe_l[...])
        odd = dot_left(odd, fo_h[...], fo_l[...])
        for m in range(n_z // 128):
            e = even[:, 128 * m:128 * (m + 1)]
            o = odd[:, 128 * m:128 * (m + 1)]
            first = jnp.where(low_half, e, o)
            second = jnp.where(low_half, o, e)
            zsend[2 * m, g * per:(g + 1) * per] = first.reshape(per, rows, 128)
            zsend[2 * m + 1, g * per:(g + 1) * per] = second.reshape(per, rows, 128)
        if g == 0:
            pl.semaphore_wait(barrier, n_narrow - 1 + n_wide - 1)

        def launch(k, c):
            forward_copy(g, k).start()
            return c

        lax.fori_loop(1, n_narrow, launch, 0)

    s = s_y[...] + s_z[n][0:1, :] + penalty
    root = jnp.sqrt(s * (1.0 + s))
    rtab[0] = 1.0 / (1.0 + 2.0 * s + 2.0 * root)
    rtab[1] = -1.0 / root

    for g in range(GROUPS):
        span = slice(g * per, (g + 1) * per)
        rbuf[span, pl.ds(pl.multiple_of(n * rows, rows), rows)] = zsend[n, span]

        def arrive(k, c):
            forward_arrival(g, k).wait_recv()
            return c

        lax.fori_loop(1, n_narrow, arrive, 0)
        lines = jnp.concatenate([rbuf[xp] for xp in range(g * per, (g + 1) * per)], axis=1)
        lines = dot_right(cy_h[...], cy_l[...], lines)
        for i in range(per):
            ubuf[g * per + i] = lines[:, 128 * i:128 * (i + 1)]

    block = 16

    def moments(i, c):
        here = pl.ds(pl.multiple_of(i * block, block), block)
        r = rtab[0, here]
        f = ubuf[0, here]
        b = ubuf[xps - 1, here]
        for xp in range(1, xps):
            f = f * r + ubuf[xp, here]
            b = b * r + ubuf[xps - 1 - xp, here]
        mom[0, here] = f
        mom[1, here] = b
        return c

    lax.fori_loop(0, n_y // block, moments, 0)

    def chunk(index):
        return pl.ds(pl.multiple_of(index * chunk_rows, chunk_rows), chunk_rows)

    def out_copy(k):
        to = along(k)
        return pltpu.make_async_remote_copy(
            src_ref=mom.at[:, chunk(to)], dst_ref=mrecv.at[w],
            send_sem=wf_send.at[k], recv_sem=wf_recv.at[k],
            device_id=(to, n), device_id_type=MESH,
        )

    def out_arrival(k):
        here = mrecv.at[along(n_wide - k)]
        return pltpu.make_async_remote_copy(
            src_ref=here, dst_ref=here, send_sem=wf_send.at[k], recv_sem=wf_recv.at[k],
            device_id=(along(n_wide - k), n), device_id_type=MESH,
        )

    def back_copy(k):
        to = along(k)
        return pltpu.make_async_remote_copy(
            src_ref=absend.at[to], dst_ref=ab.at[:, chunk(w)],
            send_sem=wb_send.at[k], recv_sem=wb_recv.at[k],
            device_id=(to, n), device_id_type=MESH,
        )

    def back_arrival(k):
        here = ab.at[:, chunk(along(n_wide - k))]
        return pltpu.make_async_remote_copy(
            src_ref=here, dst_ref=here, send_sem=wb_send.at[k], recv_sem=wb_recv.at[k],
            device_id=(along(n_wide - k), n), device_id_type=MESH,
        )

    def each(count, action):
        def body(k, c):
            action(k)
            return c

        lax.fori_loop(1, count, body, 0)

    each(n_wide, lambda k: out_copy(k).start())
    mrecv[w] = mom[:, chunk(w)]
    r = rtab[0, chunk(w)]
    q = r
    for _ in range(int(math.log2(xps))):
        q = q * q
    total = q
    for _ in range(int(math.log2(n_wide))):
        total = total * total
    closing = 1.0 / (1.0 - total)
    each(n_wide, lambda k: out_arrival(k).wait_recv())
    f = mrecv[0, 0]
    b = mrecv[n_wide - 1, 1]
    for j in range(1, n_wide):
        f = f * q + mrecv[j, 0]
        b = b * q + mrecv[n_wide - 1 - j, 1]
    f = f * closing
    b = b * closing
    for j in range(n_wide):
        absend[j, 0] = f
        absend[n_wide - 1 - j, 1] = b
        f = f * q + mrecv[j, 0]
        b = b * q + mrecv[n_wide - 1 - j, 1]
    each(n_wide, lambda k: back_copy(k).start())
    ab[:, chunk(w)] = absend[w]
    each(n_wide, lambda k: back_arrival(k).wait_recv())

    def solve(i, c):
        here = pl.ds(pl.multiple_of(i * block, block), block)
        r = rtab[0, here]
        scale = rtab[1, here]
        f = ab[0, here]
        b = ab[1, here]
        behind = []
        for xp in range(xps - 1, -1, -1):
            rb = b * r
            behind.append(rb)
            b = rb + ubuf[xp, here]
        for xp in range(xps):
            f = f * r + ubuf[xp, here]
            ubuf[xp, here] = scale * (f + behind[xps - 1 - xp])
        return c

    lax.fori_loop(0, n_y // block, solve, 0)

    def backward_copy(g, k):
        to = across(k)
        return pltpu.make_async_remote_copy(
            src_ref=vsend.at[to, pl.ds(g * per, per)],
            dst_ref=zrecv.at[n, pl.ds(g * per, per)],
            send_sem=nb_send.at[g, k],
            recv_sem=nb_recv.at[g, k],
            device_id=(w, to),
            device_id_type=MESH,
        )

    def backward_arrival(g, k):
        source = across(n_narrow - k)
        here = zrecv.at[source, pl.ds(g * per, per)]
        return pltpu.make_async_remote_copy(
            src_ref=here, dst_ref=here, send_sem=nb_send.at[g, k], recv_sem=nb_recv.at[g, k],
            device_id=(w, source), device_id_type=MESH,
        )

    for g in range(GROUPS):
        span = slice(g * per, (g + 1) * per)
        lines = jnp.concatenate([ubuf[xp] for xp in range(g * per, (g + 1) * per)], axis=1)
        lines = dot_right(iy_h[...], iy_l[...], lines)
        for to in range(n_narrow):
            for i in range(per):
                vsend[to, g * per + i] = lines[to * rows:(to + 1) * rows, 128 * i:128 * (i + 1)]
        each(n_narrow, lambda k: backward_copy(g, k).start())
        zrecv[n, span] = vsend[n, span]

    wide_to = {0: along(n_wide - 1), 1: along(1)}
    narrow_to = {0: across(n_narrow - 1), 1: across(1)}

    def x_halo(side):
        source = 2 * xps if side else 1
        return pltpu.make_async_remote_copy(
            src_ref=press.at[source], dst_ref=xrecv.at[1 - side],
            send_sem=h_send.at[side], recv_sem=h_recv.at[1 - side],
            device_id=(wide_to[side], n), device_id_type=MESH,
        )

    def y_halo_copy(side):
        return pltpu.make_async_remote_copy(
            src_ref=ysend.at[side], dst_ref=yrecv.at[1 - side],
            send_sem=h_send.at[2 + side], recv_sem=h_recv.at[3 - side],
            device_id=(w, narrow_to[side]), device_id_type=MESH,
        )

    for g in range(GROUPS):
        each(n_narrow, lambda k: backward_arrival(g, k).wait_recv())
        evens, odds = [], []
        for m in range(n_z // 128):
            first = zrecv[2 * m, g * per:(g + 1) * per].reshape(per * rows, 128)
            second = zrecv[2 * m + 1, g * per:(g + 1) * per].reshape(per * rows, 128)
            evens.append(jnp.where(low_half, first, second))
            odds.append(jnp.where(low_half, second, first))
        even = dot_left(jnp.concatenate(evens, axis=1), ie_h[...], ie_l[...])
        odd = dot_left(jnp.concatenate(odds, axis=1), io_h[...], io_l[...])
        for i in range(per):
            for parity, part in ((0, even), (1, odd)):
                x = 2 * (g * per + i) + parity
                plane = part[i * rows:(i + 1) * rows]
                press[x + 1] = plane
                ysend[0, x] = plane[0]
                ysend[1, x] = plane[rows - 1]
        if g == 0:
            x_halo(0).start()
    x_halo(1).start()
    y_halo_copy(0).start()
    y_halo_copy(1).start()

    for g in range(GROUPS):
        each(n_narrow, lambda k: forward_copy(g, k).wait_send())
        each(n_narrow, lambda k: backward_copy(g, k).wait_send())
    each(n_wide, lambda k: out_copy(k).wait_send())
    each(n_wide, lambda k: back_copy(k).wait_send())
    for side in (0, 1):
        x_halo(side).wait()
        y_halo_copy(side).wait()
    press[0] = xrecv[0]
    press[2 * xps + 1] = xrecv[1]
    y_halo[...] = yrecv[...]


def solve_pressure(divergence):
    n_wide, n_narrow = lax.axis_size("wide"), lax.axis_size("narrow")
    x_local, rows, n_z = divergence.shape
    n_y = rows * n_narrow
    xps = x_local // 2
    tables = [jnp.asarray(t) for t in pressure_tables(n_y, n_z, n_narrow)]
    dma = pltpu.SemaphoreType.DMA
    field = (xps, n_y, 128)
    turned = (n_narrow, xps, rows, 128)
    chunk_rows = n_y // n_wide
    return pl.pallas_call(
        functools.partial(pressure_kernel, n_wide, n_narrow),
        out_shape=[
            jax.ShapeDtypeStruct((x_local + 2, rows, n_z), F32),
            jax.ShapeDtypeStruct((2, x_local, n_z), F32),
        ],
        in_specs=[VM] * (1 + len(tables)),
        out_specs=[VM, VM],
        scratch_shapes=[
            pltpu.VMEM(turned, F32),
            pltpu.VMEM(field, F32),
            pltpu.VMEM(field, F32),
            pltpu.VMEM(turned, F32),
            pltpu.VMEM(turned, F32),
            pltpu.VMEM((2, n_y, 128), F32),
            pltpu.VMEM((2, n_y, 128), F32),
            pltpu.VMEM((n_wide, 2, chunk_rows, 128), F32),
            pltpu.VMEM((n_wide, 2, chunk_rows, 128), F32),
            pltpu.VMEM((2, n_y, 128), F32),
            pltpu.VMEM((2, rows, n_z), F32),
            pltpu.VMEM((2, x_local, n_z), F32),
            pltpu.VMEM((2, x_local, n_z), F32),
            dma((GROUPS, n_narrow)),
            dma((GROUPS, n_narrow)),
            dma((GROUPS, n_narrow)),
            dma((GROUPS, n_narrow)),
            dma((n_wide,)),
            dma((n_wide,)),
            dma((n_wide,)),
            dma((n_wide,)),
            dma((4,)),
            dma((4,)),
        ],
        compiler_params=pltpu.CompilerParams(
            collective_id=1, has_side_effects=True, vmem_limit_bytes=40 * 2**20
        ),
        name="pressure",
    )(divergence.reshape(xps, 2, rows, n_z), *tables)


def y_step(plane, before, after, ahead):
    rows = plane.shape[0]
    row = lax.broadcasted_iota(jnp.int32, plane.shape, 0)
    if ahead:
        return jnp.where(row == rows - 1, after, pltpu.roll(plane, rows - 1, 0))
    return jnp.where(row == 0, before, pltpu.roll(plane, 1, 0))


def project_kernel(press, y_halo, current, out):
    step = pl.program_id(0)
    n_z = press.shape[2]
    for i in range(current.shape[1]):
        x = step * current.shape[1] + i
        p = press[x + 1]
        before = y_halo[0, pl.ds(x, 1)]
        after = y_halo[1, pl.ds(x, 1)]
        out[0, i] = current[0, i] - (press[x + 2] - press[x]) * 0.5
        out[1, i] = current[1, i] - 0.5 * (
            y_step(p, before, after, True) - y_step(p, before, after, False)
        )
        out[2, i] = current[2, i] - 0.5 * (pltpu.roll(p, n_z - 1, 1) - pltpu.roll(p, 1, 1))


def project(current, divergence):
    press, y_halo = solve_pressure(divergence)
    _, x_local, rows, n_z = current.shape
    planes = 2
    spec = pl.BlockSpec((3, planes, rows, n_z), lambda i: (0, i, 0, 0))
    return pl.pallas_call(
        project_kernel,
        grid=(x_local // planes,),
        out_shape=jax.ShapeDtypeStruct(current.shape, F32),
        in_specs=[VM, VM, spec],
        out_specs=spec,
        compiler_params=pltpu.CompilerParams(vmem_limit_bytes=20 * 2**20),
        name="projection",
    )(press, y_halo, current)


def conduct(thermal_profile, spread_wide):
    sides = (("wide", 0), ("narrow", 1))
    t = with_halo(thermal_profile, sides, STEPS, False)
    coefficient = spread_wide
    for _ in range(STEPS):
        center = t[1:-1, 1:-1]
        coefficient = coefficient[1:-1, 1:-1]
        around = t[2:, 1:-1] + t[:-2, 1:-1] + t[1:-1, 2:] + t[1:-1, :-2]
        ahead = jnp.pad(center[:, :, 1:], ((0, 0), (0, 0), (0, 1)))
        behind = jnp.pad(center[:, :, :-1], ((0, 0), (0, 0), (1, 0)))
        t = center + coefficient * (around + ahead + behind - 6.0 * center)
    return t


def per_device(
    material_flow_vector,
    tool_push_density,
    tool_warmth_excess,
    substrate_warmth_excess,
    spread_coefficient,
    source_owner_sheet,
    source_part_line,
):
    current, divergence, heat = flow(material_flow_vector, tool_push_density, tool_warmth_excess)
    corrected_flow_vector = project(current, divergence)
    spread_wide = with_halo(spread_coefficient, (("wide", 0), ("narrow", 1)), STEPS, False)
    slab_ids = source_owner_sheet[:, 0]
    slab_count = lax.axis_size("wide")
    component_lines = substrate_warmth_excess.shape[0] * substrate_warmth_excess.shape[1]
    target = slab_ids * component_lines + source_part_line
    partial_value = slab_heat(target, heat, slab_count * component_lines)
    substrate_energy_input = lax.psum_scatter(
        partial_value.reshape(slab_count, component_lines, 128),
        "wide",
        scatter_dimension=0,
        tiled=True,
    )
    thermal_profile = substrate_warmth_excess + dissipation_factor * substrate_energy_input.reshape(
        substrate_warmth_excess.shape
    )
    return (corrected_flow_vector, conduct(thermal_profile, spread_wide))


def solution(mesh):
    return jax.shard_map(
        per_device,
        mesh=mesh,
        in_specs=(
            P(None, "wide", "narrow", None),
            P(None, "wide", "narrow", None),
            P("wide", "narrow", None),
            P("wide", "narrow", None),
            P("wide", "narrow", None),
            P(("wide", "narrow"), None),
            P(("wide", "narrow")),
        ),
        out_specs=(P(None, "wide", "narrow", None), P("wide", "narrow", None)),
        check_vma=False,
    )
```

```python
import functools
import math

import jax
import jax.numpy as jnp
import ml_dtypes
import numpy as np
from jax import lax
from jax.experimental import pallas as pl
from jax.experimental.pallas import tpu as pltpu
from jax.sharding import PartitionSpec as P

STEPS = 3
MESH = pl.DeviceIdType.MESH
F32 = jnp.float32
BF16 = jnp.bfloat16
VM = pl.BlockSpec(memory_space=pltpu.VMEM)

time_step = 0.15
rate_base = 0.5
zener_energy = 4.0
stress_exponent = 5.0
penalty = 0.001
dissipation_factor = 0.1
GROUPS = 2
DEEP = STEPS


PAD = 8
STRIP = 8


def flow_kernel(
    n_wide, n_narrow,
    vel_in, push_in, warmth_in,
    mom, div, heat,
    velp, provp, mup0, mup1, lz, push,
    vel_ys, vel_yr, mu_ys0, mu_yr0, prov_ys, prov_yr, mu_ys1, mu_yr1, mom_ys, mom_yr, mom_xr,
    load_sem, h_send, h_recv,
):
    w = lax.axis_index("wide")
    n = lax.axis_index("narrow")
    _, planes, rows, n_z = vel_in.shape
    strips = rows // STRIP
    wide_to = (lax.rem(w + n_wide - 1, n_wide), lax.rem(w + 1, n_wide))
    narrow_to = (lax.rem(n + n_narrow - 1, n_narrow), lax.rem(n + 1, n_narrow))
    body = pl.ds(PAD, rows)

    barrier = pltpu.get_barrier_semaphore()
    for side in (0, 1):
        pl.semaphore_signal(barrier, inc=1, device_id=(wide_to[side], n), device_id_type=MESH)
        pl.semaphore_signal(barrier, inc=1, device_id=(w, narrow_to[side]), device_id_type=MESH)

    loads = [
        pltpu.make_async_copy(vel_in, velp.at[:, pl.ds(1, planes), body], load_sem.at[0]),
        pltpu.make_async_copy(warmth_in, lz, load_sem.at[1]),
        pltpu.make_async_copy(push_in, push, load_sem.at[2]),
    ]
    for load in loads:
        load.start()

    def wide_copy(e, side, source, target):
        return pltpu.make_async_remote_copy(
            src_ref=source, dst_ref=target,
            send_sem=h_send.at[e, side], recv_sem=h_recv.at[e, 1 - side],
            device_id=(wide_to[side], n), device_id_type=MESH,
        )

    def narrow_copy(e, side, sends, lands):
        return pltpu.make_async_remote_copy(
            src_ref=sends.at[side], dst_ref=lands.at[1 - side],
            send_sem=h_send.at[e, 2 + side], recv_sem=h_recv.at[e, 3 - side],
            device_id=(w, narrow_to[side]), device_id_type=MESH,
        )

    def x_pair(e, field, lead=()):
        return [
            wide_copy(e, 0, field.at[lead + (1, body)], field.at[lead + (planes + 1, body)]),
            wide_copy(e, 1, field.at[lead + (planes, body)], field.at[lead + (0, body)]),
        ]

    def y_pair(e, sends, lands):
        return [narrow_copy(e, side, sends, lands) for side in (0, 1)]

    def all_x(action, first=0, last=None):
        def step(x, c):
            action(x)
            return c

        lax.fori_loop(first, planes if last is None else last, step, 0)

    def y_fill(field, lands, comps):
        def fill(x):
            here = pl.ds(x, 1)
            if comps is None:
                field[x + 1, PAD - 1:PAD] = lands[0, here]
                field[x + 1, PAD + rows:PAD + rows + 1] = lands[1, here]
                return
            for i, c in enumerate(comps):
                field[c, x + 1, PAD - 1:PAD] = lands[0, i, here]
                field[c, x + 1, PAD + rows:PAD + rows + 1] = lands[1, i, here]

        all_x(fill)

    def z_ahead(a):
        return pltpu.roll(a, n_z - 1, 1)

    def z_behind(a):
        return pltpu.roll(a, 1, 1)

    loads[0].wait()

    def vel_rows(x):
        for c in range(3):
            vel_ys[0, c, pl.ds(x, 1)] = velp[c, x + 1, PAD:PAD + 1]
            vel_ys[1, c, pl.ds(x, 1)] = velp[c, x + 1, PAD + rows - 1:PAD + rows]

    all_x(vel_rows)
    pl.semaphore_wait(barrier, 4)
    every = slice(None)
    vel_x = x_pair(0, velp, (every,))
    vel_y = y_pair(0, vel_ys, vel_yr)
    for copy in vel_x + vel_y:
        copy.start()
    loads[1].wait()

    def zener_log(x):
        lz[x] = (zener_energy / stress_exponent) * (1.0 / lz[x] - 1.0)

    all_x(zener_log)
    loads[2].wait()

    def excess(src, x, r):
        here = slice(PAD + STRIP * r, PAD + STRIP * (r + 1))
        up = slice(PAD + STRIP * r + 1, PAD + STRIP * (r + 1) + 1)
        down = slice(PAD + STRIP * r - 1, PAD + STRIP * (r + 1) - 1)
        dx = [src[c, x + 2, here] - src[c, x, here] for c in range(3)]
        dy = [src[c, x + 1, up] - src[c, x + 1, down] for c in range(3)]
        mid = [src[c, x + 1, here] for c in range(3)]
        dz = [z_ahead(m) - z_behind(m) for m in mid]
        xy, xz, yz = dy[0] + dx[1], dz[0] + dx[2], dz[1] + dy[2]
        diagonal = dx[0] * dx[0] + dy[1] * dy[1] + dz[2] * dz[2]
        return 0.5 * diagonal + 0.25 * (xy * xy + xz * xz + yz * yz)

    def mu_plane(src, mup, ys, with_heat):
        def plane(x):
            for r in range(strips):
                part = slice(STRIP * r, STRIP * (r + 1))
                extra = excess(src, x, r)
                rate_sq = extra + rate_base**2
                v = jnp.exp((0.5 / stress_exponent) * jnp.log(rate_sq) + lz[x, part])
                mu = jnp.log(v + jnp.sqrt(v * v + 1.0)) * lax.rsqrt(rate_sq) * (1.0 / 3.0)
                mup[x + 1, PAD + STRIP * r:PAD + STRIP * (r + 1)] = mu
                if r == 0:
                    ys[0, pl.ds(x, 1)] = mu[0:1]
                if r == strips - 1:
                    ys[1, pl.ds(x, 1)] = mu[STRIP - 1:]
                if with_heat:
                    h = mu * extra
                    to = pl.ds(pl.multiple_of(x * rows + STRIP * r, STRIP), STRIP)
                    for m in range(n_z // 128):
                        heat[m, to] = h[:, 128 * m:128 * (m + 1)]

        return plane

    def advance_plane(mup, final):
        def plane(x):
            for r in range(strips):
                part = slice(STRIP * r, STRIP * (r + 1))
                here = slice(PAD + STRIP * r, PAD + STRIP * (r + 1))
                up = slice(PAD + STRIP * r + 1, PAD + STRIP * (r + 1) + 1)
                down = slice(PAD + STRIP * r - 1, PAD + STRIP * (r + 1) - 1)
                m = mup[x + 1, here]
                m_xp = m + mup[x + 2, here]
                m_xm = m + mup[x, here]
                m_yp = m + mup[x + 1, up]
                m_ym = m + mup[x + 1, down]
                m_z = m + z_ahead(m)
                for c in range(3):
                    u = velp[c, x + 1, here]
                    flux = m_z * (z_ahead(u) - u)
                    total = flux - z_behind(flux)
                    total += m_xp * (velp[c, x + 2, here] - u) - m_xm * (u - velp[c, x, here])
                    total += m_yp * (velp[c, x + 1, up] - u) - m_ym * (u - velp[c, x + 1, down])
                    new = u + (0.5 * time_step) * total + time_step * push[c, x, part]
                    provp[c, x + 1, here] = new
                    if final:
                        mom[c, x, part] = new
                        if c == 1:
                            if r == 0:
                                mom_ys[0, pl.ds(x, 1)] = new[0:1]
                            if r == strips - 1:
                                mom_ys[1, pl.ds(x, 1)] = new[STRIP - 1:]
                    else:
                        if r == 0:
                            prov_ys[0, c, pl.ds(x, 1)] = new[0:1]
                        if r == strips - 1:
                            prov_ys[1, c, pl.ds(x, 1)] = new[STRIP - 1:]

        return plane

    def stage(action, arriving_x, arriving_y, fill):
        for copy in arriving_y:
            copy.wait_recv()
        fill()
        all_x(action, 1, planes - 1)
        for copy in arriving_x:
            copy.wait_recv()
        all_x(lambda i: action(i * (planes - 1)), 0, 2)

    stage(mu_plane(velp, mup0, mu_ys0, False), vel_x, vel_y,
          lambda: y_fill(velp, vel_yr, (0, 1, 2)))
    mu_x0 = x_pair(1, mup0)
    mu_y0 = y_pair(1, mu_ys0, mu_yr0)
    for copy in mu_x0 + mu_y0:
        copy.start()
    stage(advance_plane(mup0, False), mu_x0, mu_y0, lambda: y_fill(mup0, mu_yr0, None))
    prov_x = x_pair(2, provp, (every,))
    prov_y = y_pair(2, prov_ys, prov_yr)
    for copy in prov_x + prov_y:
        copy.start()
    stage(mu_plane(provp, mup1, mu_ys1, True), prov_x, prov_y,
          lambda: y_fill(provp, prov_yr, (0, 1, 2)))
    mu_x1 = x_pair(3, mup1)
    mu_y1 = y_pair(3, mu_ys1, mu_yr1)
    for copy in mu_x1 + mu_y1:
        copy.start()
    for copy in prov_x + prov_y:
        copy.wait_send()
    stage(advance_plane(mup1, True), mu_x1, mu_y1, lambda: y_fill(mup1, mu_yr1, None))
    mom_x = [
        wide_copy(4, 0, mom.at[0, 0], mom_xr.at[1]),
        wide_copy(4, 1, mom.at[0, planes - 1], mom_xr.at[0]),
    ]
    mom_y = y_pair(4, mom_ys, mom_yr)
    for copy in mom_x + mom_y:
        copy.start()
    for copy in vel_x + vel_y + mu_x0 + mu_y0 + mu_x1 + mu_y1:
        copy.wait_send()

    def fill_rows():
        def fill(x):
            here = pl.ds(x, 1)
            provp[1, x + 1, PAD - 1:PAD] = mom_yr[0, here]
            provp[1, x + 1, PAD + rows:PAD + rows + 1] = mom_yr[1, here]

        all_x(fill)

    def div_plane(x):
        for r in range(strips):
            part = slice(STRIP * r, STRIP * (r + 1))
            here = slice(PAD + STRIP * r, PAD + STRIP * (r + 1))
            up = slice(PAD + STRIP * r + 1, PAD + STRIP * (r + 1) + 1)
            down = slice(PAD + STRIP * r - 1, PAD + STRIP * (r + 1) - 1)
            u = provp[2, x + 1, here]
            total = provp[0, x + 2, here] - provp[0, x, here]
            total += provp[1, x + 1, up] - provp[1, x + 1, down]
            div[x, part] = 0.5 * (total + (z_ahead(u) - z_behind(u)))

    for copy in mom_y:
        copy.wait_recv()
    fill_rows()
    all_x(div_plane, 1, planes - 1)
    for copy in mom_x:
        copy.wait_recv()
    provp[0, 0, body] = mom_xr[0]
    provp[0, planes + 1, body] = mom_xr[1]
    all_x(lambda i: div_plane(i * (planes - 1)), 0, 2)
    for copy in mom_x + mom_y:
        copy.wait_send()


def flow(velocity, push, warmth):
    n_wide, n_narrow = lax.axis_size("wide"), lax.axis_size("narrow")
    _, planes, rows, n_z = velocity.shape
    padded = (planes + 2, PAD + rows + PAD, n_z)
    line = (2, planes, n_z)
    lines = (2, 3, planes, n_z)
    any_space = pl.BlockSpec(memory_space=pl.ANY)
    shapes = [(3,) + padded, (3,) + padded, padded, padded, (planes, rows, n_z), velocity.shape]
    shapes += [lines, lines, line, line, lines, lines, line, line, line, line, (2, rows, n_z)]
    dma = pltpu.SemaphoreType.DMA
    return pl.pallas_call(
        functools.partial(flow_kernel, n_wide, n_narrow),
        out_shape=[
            jax.ShapeDtypeStruct(velocity.shape, F32),
            jax.ShapeDtypeStruct((planes, rows, n_z), F32),
            jax.ShapeDtypeStruct((n_z // 128, planes * rows, 128), F32),
        ],
        in_specs=[any_space] * 3,
        out_specs=[VM] * 3,
        scratch_shapes=[pltpu.VMEM(shape, F32) for shape in shapes]
        + [dma((3,)), dma((5, 4)), dma((5, 4))],
        compiler_params=pltpu.CompilerParams(
            collective_id=2, has_side_effects=True, vmem_limit_bytes=48 * 2**20
        ),
        name="flow",
    )(velocity, push, warmth)


def gather_kernel(target, heat, out, other):
    out[...] = jnp.zeros_like(out)
    other[...] = jnp.zeros_like(other)
    depth = heat.shape[0]

    def cell(i, c):
        for m in range(depth):
            into = out if m % 2 == 0 else other
            row = pl.ds(target[i * depth + m], 1)
            into[row] = into[row] + heat[m, pl.ds(i, 1)]
        return c

    lax.fori_loop(0, heat.shape[1], cell, 0, unroll=4)
    step = 256

    def join(i, c):
        here = pl.ds(pl.multiple_of(i * step, step), step)
        out[here] = out[here] + other[here]
        return c

    lax.fori_loop(0, out.shape[0] // step, join, 0)


def slab_heat(target, heat, lines):
    return pl.pallas_call(
        gather_kernel,
        out_shape=jax.ShapeDtypeStruct((lines, 128), F32),
        in_specs=[pl.BlockSpec(memory_space=pltpu.SMEM), VM],
        out_specs=VM,
        scratch_shapes=[pltpu.VMEM((lines, 128), F32)],
        compiler_params=pltpu.CompilerParams(vmem_limit_bytes=24 * 2**20),
        name="slab_heat",
    )(target, heat)


def real_basis(length):
    cells = np.arange(length, dtype=np.float64)
    rows = [np.full(length, 1.0 / math.sqrt(length)), (-1.0) ** cells / math.sqrt(length)]
    waves = [0, length // 2]
    for k in range(1, length // 2):
        angle = 2.0 * math.pi * k * cells / length
        rows.append(np.cos(angle) * math.sqrt(2.0 / length))
        rows.append(np.sin(angle) * math.sqrt(2.0 / length))
        waves += [k, k]
    waves = np.array(waves)
    symbol = np.sin(2.0 * math.pi * (waves % (length // 2)) / length) ** 2
    return np.stack(rows), symbol


def split_table(table):
    high = table.astype(np.float32).astype(ml_dtypes.bfloat16)
    low = (table - high.astype(np.float64)).astype(np.float32).astype(ml_dtypes.bfloat16)
    return [high, low]


def pressure_tables(n_y, n_z, n_narrow):
    basis_z, symbol_z = real_basis(n_z)
    basis_y, symbol_y = real_basis(n_y)
    forward = basis_z.T
    swapped = forward.reshape(n_z, n_z // 128, 2, 64)[:, :, ::-1].reshape(n_z, n_z)
    tables = []
    for table in (forward, swapped, forward.T, swapped.T, basis_y, basis_y.T):
        tables += split_table(np.ascontiguousarray(table))
    s_y = np.broadcast_to(symbol_y[:, None], (n_y, 128)).astype(np.float32)
    s_z = np.tile(symbol_z.reshape(n_narrow, 1, 64), (1, 8, 2)).astype(np.float32)
    return tables + [s_y, s_z]


def split_value(x):
    high = x.astype(BF16)
    return high, (x - high.astype(F32)).astype(BF16)


def dot_left(x, high, low):
    x_high, x_low = split_value(x)
    dot = functools.partial(jnp.dot, preferred_element_type=F32)
    return dot(x_high, high) + (dot(x_high, low) + dot(x_low, high))


def dot_right(high, low, x):
    x_high, x_low = split_value(x)
    dot = functools.partial(jnp.dot, preferred_element_type=F32)
    return dot(high, x_high) + (dot(low, x_high) + dot(high, x_low))


def pressure_kernel(
    n_wide, n_narrow,
    div, slab, substrate, spread, *rest,
):
    table_refs, rest = rest[:12], rest[12:]
    s_y, s_z, press, y_halo, tp, cp = rest[:6]
    tables, rest = rest[6:18], rest[18:]
    (
        zsend, rbuf, ubuf, vsend, zrecv, rtab, mom, mrecv, absend, ab, xrecv, yrecv, ysend,
        first_in, first_sum, second_in, part_xr,
        nf_send, nf_recv, nb_send, nb_recv, wf_send, wf_recv, wb_send, wb_recv, h_send, h_recv,
        f_send, f_recv, q_send, q_recv, p_send, p_recv, table_sem, own_sem,
    ) = rest
    fe_h, fe_l, fo_h, fo_l, ie_h, ie_l, io_h, io_l, cy_h, cy_l, iy_h, iy_l = tables
    loads = [
        pltpu.make_async_copy(table_refs[i], tables[i], table_sem.at[i]) for i in range(12)
    ]

    def loaded(*which):
        for i in which:
            loads[i].wait()

    for i in (0, 1, 2, 3, 8, 9, 10, 11, 4, 5, 6, 7):
        loads[i].start()
    w = lax.axis_index("wide")
    n = lax.axis_index("narrow")
    xps, _, rows, n_z = div.shape
    n_y = s_y.shape[0]
    per = xps // GROUPS
    chunk_rows = n_y // n_wide

    def across(k):
        return lax.rem(n + k, n_narrow)

    def along(k):
        return lax.rem(w + k, n_wide)

    side = math.isqrt(n_wide)
    half = slab.shape[2] // 2
    own = (w // side, lax.rem(w, side))

    def peer(way, k):
        to = lax.rem(own[way] + k, side)
        return (to, to * side + own[1] if way == 0 else own[0] * side + to)

    def first_source(way, to):
        return slab.at[to, :, pl.ds(0, half)] if way == 0 else slab.at[:, to, pl.ds(half, half)]

    def first_copy(way, k):
        to, device = peer(way, k)
        return pltpu.make_async_remote_copy(
            src_ref=first_source(way, to), dst_ref=first_in.at[way, k],
            send_sem=f_send.at[way, k], recv_sem=f_recv.at[way, k],
            device_id=(device, n), device_id_type=MESH,
        )

    def own_first(way):
        return pltpu.make_async_copy(
            first_source(way, own[way]), first_in.at[way, 0], own_sem.at[way]
        )

    def second_copy(way, k):
        to, device = peer(1 - way, k)
        return pltpu.make_async_remote_copy(
            src_ref=first_sum.at[way, to], dst_ref=second_in.at[way, k],
            send_sem=q_send.at[way, k], recv_sem=q_recv.at[way, k],
            device_id=(device, n), device_id_type=MESH,
        )

    halves = [(way, k) for way in (0, 1) for k in range(1, side)]

    def first_total():
        for way in (0, 1):
            own_first(way).wait()
        for way, k in halves:
            first_copy(way, k).wait_recv()
        step = 32
        per_slab = half // step

        def add(i, c):
            at = i // per_slab
            here = pl.ds(pl.multiple_of(lax.rem(i, per_slab) * step, step), step)
            for way in (0, 1):
                total = first_in[way, 0, at, here]
                for k in range(1, side):
                    total = total + first_in[way, k, at, here]
                first_sum[way, at, here] = total
            return c

        lax.fori_loop(0, side * per_slab, add, 0)
        for way, k in halves:
            second_copy(way, k).start()

    planes = substrate.shape[0]
    part_rows = substrate.shape[1]
    inside = pl.ds(PAD, part_rows)
    last_w, last_n = n_wide - 1, n_narrow - 1
    wide_near = (lax.rem(w + last_w, n_wide), lax.rem(w + 1, n_wide))
    narrow_near = (lax.rem(n + last_n, n_narrow), lax.rem(n + 1, n_narrow))

    def part_x(field, e, side_):
        start = planes if side_ else DEEP
        return pltpu.make_async_remote_copy(
            src_ref=field.at[pl.ds(start, DEEP), inside], dst_ref=part_xr.at[e, 1 - side_],
            send_sem=p_send.at[e, side_], recv_sem=p_recv.at[e, 1 - side_],
            device_id=(wide_near[side_], n), device_id_type=MESH,
        )

    def part_y(field, e, side_):
        start = part_rows if side_ else PAD
        land = 0 if side_ else PAD + part_rows
        return pltpu.make_async_remote_copy(
            src_ref=field.at[:, pl.ds(start, PAD)], dst_ref=field.at[:, pl.ds(land, PAD)],
            send_sem=p_send.at[e, 2 + side_], recv_sem=p_recv.at[e, 3 - side_],
            device_id=(w, narrow_near[side_]), device_id_type=MESH,
        )

    def part_x_start(field, e):
        for i in (0, 1):
            part_x(field, e, i).start()

    def part_x_end(field, e):
        for i in (0, 1):
            part_x(field, e, i).wait_recv()
        field[0:DEEP, PAD:PAD + part_rows] = jnp.where(w == 0, 0.0, part_xr[e, 0])
        field[planes + DEEP:, PAD:PAD + part_rows] = jnp.where(w == last_w, 0.0, part_xr[e, 1])
        for i in (0, 1):
            part_y(field, e, i).start()

    def part_y_end(field, e):
        for i in (0, 1):
            part_y(field, e, i).wait_recv()

        @pl.when(n == 0)
        def _():
            field[:, 0:PAD] = jnp.zeros_like(field[:, 0:PAD])

        @pl.when(n == last_n)
        def _():
            field[:, PAD + part_rows:] = jnp.zeros_like(field[:, PAD + part_rows:])

        for i in (0, 1):
            part_x(field, e, i).wait_send()
            part_y(field, e, i).wait_send()

    def part_start():
        for way, k in halves:
            second_copy(way, k).wait_recv()
        per_half = planes // 2
        for way in (0, 1):
            mine = own[1 - way]
            for i in range(per_half):
                here = slice(i * part_rows, (i + 1) * part_rows)
                total = first_sum[way, mine, here]
                for k in range(1, side):
                    total = total + second_in[way, k, here]
                x = way * per_half + i
                tp[DEEP + x, PAD:PAD + part_rows] = substrate[x] + dissipation_factor * total
        part_x_start(tp, 0)

    barrier = pltpu.get_barrier_semaphore()

    def greet_n(k, c):
        pl.semaphore_signal(barrier, inc=1, device_id=(w, across(k)), device_id_type=MESH)
        return c

    def greet_w(k, c):
        pl.semaphore_signal(barrier, inc=1, device_id=(along(k), n), device_id_type=MESH)
        return c

    lax.fori_loop(1, n_narrow, greet_n, 0)
    lax.fori_loop(1, n_wide, greet_w, 0)

    lane = lax.broadcasted_iota(jnp.int32, (per * rows, 128), 1)
    low_half = lane < 64

    def forward_copy(g, k):
        to = across(k)
        return pltpu.make_async_remote_copy(
            src_ref=zsend.at[to, pl.ds(g * per, per)],
            dst_ref=rbuf.at[pl.ds(g * per, per), pl.ds(pl.multiple_of(n * rows, rows), rows)],
            send_sem=nf_send.at[g, k],
            recv_sem=nf_recv.at[g, k],
            device_id=(w, to),
            device_id_type=MESH,
        )

    def forward_arrival(g, k):
        source = across(n_narrow - k)
        here = rbuf.at[pl.ds(g * per, per), pl.ds(pl.multiple_of(source * rows, rows), rows)]
        return pltpu.make_async_remote_copy(
            src_ref=here, dst_ref=here, send_sem=nf_send.at[g, k], recv_sem=nf_recv.at[g, k],
            device_id=(w, source), device_id_type=MESH,
        )

    for way in (0, 1):
        own_first(way).start()
    loaded(0, 1, 2, 3)
    for g in range(GROUPS):
        even = div[g * per:(g + 1) * per, 0].reshape(per * rows, n_z)
        odd = div[g * per:(g + 1) * per, 1].reshape(per * rows, n_z)
        even = dot_left(even, fe_h[...], fe_l[...])
        odd = dot_left(odd, fo_h[...], fo_l[...])
        for m in range(n_z // 128):
            e = even[:, 128 * m:128 * (m + 1)]
            o = odd[:, 128 * m:128 * (m + 1)]
            first = jnp.where(low_half, e, o)
            second = jnp.where(low_half, o, e)
            zsend[2 * m, g * per:(g + 1) * per] = first.reshape(per, rows, 128)
            zsend[2 * m + 1, g * per:(g + 1) * per] = second.reshape(per, rows, 128)
        if g == 0:
            pl.semaphore_wait(barrier, n_narrow - 1 + n_wide - 1)

        def launch(k, c):
            forward_copy(g, k).start()
            return c

        lax.fori_loop(1, n_narrow, launch, 0)
        if g == 0:
            for way, k in halves:
                first_copy(way, k).start()
            cp[DEEP:DEEP + planes, PAD:PAD + part_rows] = spread[...]
            part_x_start(cp, 1)

    s = s_y[...] + s_z[n][0:1, :] + penalty
    root = jnp.sqrt(s * (1.0 + s))
    rtab[0] = 1.0 / (1.0 + 2.0 * s + 2.0 * root)
    rtab[1] = -1.0 / root

    for g in range(GROUPS):
        span = slice(g * per, (g + 1) * per)
        rbuf[span, pl.ds(pl.multiple_of(n * rows, rows), rows)] = zsend[n, span]
        if g == 0:
            part_x_end(cp, 1)
            loaded(8, 9)

        def arrive(k, c):
            forward_arrival(g, k).wait_recv()
            return c

        lax.fori_loop(1, n_narrow, arrive, 0)
        lines = jnp.concatenate([rbuf[xp] for xp in range(g * per, (g + 1) * per)], axis=1)
        lines = dot_right(cy_h[...], cy_l[...], lines)
        for i in range(per):
            ubuf[g * per + i] = lines[:, 128 * i:128 * (i + 1)]

    block = 16

    def moments(i, c):
        here = pl.ds(pl.multiple_of(i * block, block), block)
        r = rtab[0, here]
        f = ubuf[0, here]
        b = ubuf[xps - 1, here]
        for xp in range(1, xps):
            f = f * r + ubuf[xp, here]
            b = b * r + ubuf[xps - 1 - xp, here]
        mom[0, here] = f
        mom[1, here] = b
        return c

    lax.fori_loop(0, n_y // block, moments, 0)

    def chunk(index):
        return pl.ds(pl.multiple_of(index * chunk_rows, chunk_rows), chunk_rows)

    def out_copy(k):
        to = along(k)
        return pltpu.make_async_remote_copy(
            src_ref=mom.at[:, chunk(to)], dst_ref=mrecv.at[w],
            send_sem=wf_send.at[k], recv_sem=wf_recv.at[k],
            device_id=(to, n), device_id_type=MESH,
        )

    def out_arrival(k):
        here = mrecv.at[along(n_wide - k)]
        return pltpu.make_async_remote_copy(
            src_ref=here, dst_ref=here, send_sem=wf_send.at[k], recv_sem=wf_recv.at[k],
            device_id=(along(n_wide - k), n), device_id_type=MESH,
        )

    def back_copy(k):
        to = along(k)
        return pltpu.make_async_remote_copy(
            src_ref=absend.at[to], dst_ref=ab.at[:, chunk(w)],
            send_sem=wb_send.at[k], recv_sem=wb_recv.at[k],
            device_id=(to, n), device_id_type=MESH,
        )

    def back_arrival(k):
        here = ab.at[:, chunk(along(n_wide - k))]
        return pltpu.make_async_remote_copy(
            src_ref=here, dst_ref=here, send_sem=wb_send.at[k], recv_sem=wb_recv.at[k],
            device_id=(along(n_wide - k), n), device_id_type=MESH,
        )

    def each(count, action):
        def body(k, c):
            action(k)
            return c

        lax.fori_loop(1, count, body, 0)

    each(n_wide, lambda k: out_copy(k).start())
    mrecv[w] = mom[:, chunk(w)]
    r = rtab[0, chunk(w)]
    q = r
    for _ in range(int(math.log2(xps))):
        q = q * q
    total = q
    for _ in range(int(math.log2(n_wide))):
        total = total * total
    closing = 1.0 / (1.0 - total)
    each(n_wide, lambda k: out_arrival(k).wait_recv())
    f = mrecv[0, 0]
    b = mrecv[n_wide - 1, 1]
    for j in range(1, n_wide):
        f = f * q + mrecv[j, 0]
        b = b * q + mrecv[n_wide - 1 - j, 1]
    f = f * closing
    b = b * closing
    for j in range(n_wide):
        absend[j, 0] = f
        absend[n_wide - 1 - j, 1] = b
        f = f * q + mrecv[j, 0]
        b = b * q + mrecv[n_wide - 1 - j, 1]
    each(n_wide, lambda k: back_copy(k).start())
    ab[:, chunk(w)] = absend[w]
    each(n_wide, lambda k: back_arrival(k).wait_recv())

    def solve(i, c):
        here = pl.ds(pl.multiple_of(i * block, block), block)
        r = rtab[0, here]
        scale = rtab[1, here]
        f = ab[0, here]
        b = ab[1, here]
        behind = []
        for xp in range(xps - 1, -1, -1):
            rb = b * r
            behind.append(rb)
            b = rb + ubuf[xp, here]
        for xp in range(xps):
            f = f * r + ubuf[xp, here]
            ubuf[xp, here] = scale * (f + behind[xps - 1 - xp])
        return c

    lax.fori_loop(0, n_y // block, solve, 0)

    def backward_copy(g, k):
        to = across(k)
        return pltpu.make_async_remote_copy(
            src_ref=vsend.at[to, pl.ds(g * per, per)],
            dst_ref=zrecv.at[n, pl.ds(g * per, per)],
            send_sem=nb_send.at[g, k],
            recv_sem=nb_recv.at[g, k],
            device_id=(w, to),
            device_id_type=MESH,
        )

    def backward_arrival(g, k):
        source = across(n_narrow - k)
        here = zrecv.at[source, pl.ds(g * per, per)]
        return pltpu.make_async_remote_copy(
            src_ref=here, dst_ref=here, send_sem=nb_send.at[g, k], recv_sem=nb_recv.at[g, k],
            device_id=(w, source), device_id_type=MESH,
        )

    loaded(10, 11)
    for g in range(GROUPS):
        span = slice(g * per, (g + 1) * per)
        lines = jnp.concatenate([ubuf[xp] for xp in range(g * per, (g + 1) * per)], axis=1)
        lines = dot_right(iy_h[...], iy_l[...], lines)
        for to in range(n_narrow):
            for i in range(per):
                vsend[to, g * per + i] = lines[to * rows:(to + 1) * rows, 128 * i:128 * (i + 1)]
        each(n_narrow, lambda k: backward_copy(g, k).start())
        zrecv[n, span] = vsend[n, span]

    first_total()
    part_y_end(cp, 1)
    loaded(4, 5, 6, 7)

    def x_halo(side):
        source = 2 * xps if side else 1
        return pltpu.make_async_remote_copy(
            src_ref=press.at[source], dst_ref=xrecv.at[1 - side],
            send_sem=h_send.at[side], recv_sem=h_recv.at[1 - side],
            device_id=(wide_near[side], n), device_id_type=MESH,
        )

    def y_halo_copy(side):
        return pltpu.make_async_remote_copy(
            src_ref=ysend.at[side], dst_ref=yrecv.at[1 - side],
            send_sem=h_send.at[2 + side], recv_sem=h_recv.at[3 - side],
            device_id=(w, narrow_near[side]), device_id_type=MESH,
        )

    for g in range(GROUPS):
        each(n_narrow, lambda k: backward_arrival(g, k).wait_recv())
        evens, odds = [], []
        for m in range(n_z // 128):
            first = zrecv[2 * m, g * per:(g + 1) * per].reshape(per * rows, 128)
            second = zrecv[2 * m + 1, g * per:(g + 1) * per].reshape(per * rows, 128)
            evens.append(jnp.where(low_half, first, second))
            odds.append(jnp.where(low_half, second, first))
        even = dot_left(jnp.concatenate(evens, axis=1), ie_h[...], ie_l[...])
        odd = dot_left(jnp.concatenate(odds, axis=1), io_h[...], io_l[...])
        for i in range(per):
            for parity, part in ((0, even), (1, odd)):
                x = 2 * (g * per + i) + parity
                plane = part[i * rows:(i + 1) * rows]
                press[x + 1] = plane
                ysend[0, x] = plane[0]
                ysend[1, x] = plane[rows - 1]
        if g == 0:
            x_halo(0).start()
            part_start()
    x_halo(1).start()
    y_halo_copy(0).start()
    y_halo_copy(1).start()
    part_x_end(tp, 0)

    for way, k in halves:
        first_copy(way, k).wait_send()
        second_copy(way, k).wait_send()
    for g in range(GROUPS):
        each(n_narrow, lambda k: forward_copy(g, k).wait_send())
        each(n_narrow, lambda k: backward_copy(g, k).wait_send())
    each(n_wide, lambda k: out_copy(k).wait_send())
    each(n_wide, lambda k: back_copy(k).wait_send())
    for side in (0, 1):
        x_halo(side).wait()
        y_halo_copy(side).wait()
    press[0] = xrecv[0]
    press[2 * xps + 1] = xrecv[1]
    y_halo[...] = yrecv[...]
    part_y_end(tp, 0)


def solve_pressure(divergence, slab, substrate, spread):
    n_wide, n_narrow = lax.axis_size("wide"), lax.axis_size("narrow")
    x_local, rows, n_z = divergence.shape
    n_y = rows * n_narrow
    xps = x_local // 2
    tables = [jnp.asarray(t) for t in pressure_tables(n_y, n_z, n_narrow)]
    dma = pltpu.SemaphoreType.DMA
    field = (xps, n_y, 128)
    turned = (n_narrow, xps, rows, 128)
    chunk_rows = n_y // n_wide
    side = math.isqrt(n_wide)
    planes, part_rows, depth = substrate.shape
    half = planes * part_rows // 2
    part = (planes + 2 * DEEP, part_rows + 2 * PAD, depth)
    any_space = pl.BlockSpec(memory_space=pl.ANY)
    return pl.pallas_call(
        functools.partial(pressure_kernel, n_wide, n_narrow),
        out_shape=[
            jax.ShapeDtypeStruct((x_local + 2, rows, n_z), F32),
            jax.ShapeDtypeStruct((2, x_local, n_z), F32),
            jax.ShapeDtypeStruct(part, F32),
            jax.ShapeDtypeStruct(part, F32),
        ],
        in_specs=[VM, any_space, VM, VM] + [any_space] * 12 + [VM, VM],
        out_specs=[VM] * 4,
        scratch_shapes=[pltpu.VMEM(t.shape, BF16) for t in tables[:12]]
        + [
            pltpu.VMEM(turned, F32),
            pltpu.VMEM(field, F32),
            pltpu.VMEM(field, F32),
            pltpu.VMEM(turned, F32),
            pltpu.VMEM(turned, F32),
            pltpu.VMEM((2, n_y, 128), F32),
            pltpu.VMEM((2, n_y, 128), F32),
            pltpu.VMEM((n_wide, 2, chunk_rows, 128), F32),
            pltpu.VMEM((n_wide, 2, chunk_rows, 128), F32),
            pltpu.VMEM((2, n_y, 128), F32),
            pltpu.VMEM((2, rows, n_z), F32),
            pltpu.VMEM((2, x_local, n_z), F32),
            pltpu.VMEM((2, x_local, n_z), F32),
            pltpu.VMEM((2, side, side, half, depth), F32),
            pltpu.VMEM((2, side, half, depth), F32),
            pltpu.VMEM((2, side, half, depth), F32),
            pltpu.VMEM((2, 2, DEEP, part_rows, depth), F32),
            dma((GROUPS, n_narrow)),
            dma((GROUPS, n_narrow)),
            dma((GROUPS, n_narrow)),
            dma((GROUPS, n_narrow)),
            dma((n_wide,)),
            dma((n_wide,)),
            dma((n_wide,)),
            dma((n_wide,)),
            dma((4,)),
            dma((4,)),
            dma((2, side)),
            dma((2, side)),
            dma((2, side)),
            dma((2, side)),
            dma((2, 4)),
            dma((2, 4)),
            dma((12,)),
            dma((2,)),
        ],
        compiler_params=pltpu.CompilerParams(
            collective_id=1, has_side_effects=True, vmem_limit_bytes=52 * 2**20
        ),
        name="pressure",
    )(
        divergence.reshape(xps, 2, rows, n_z),
        slab.reshape(side, side, 2 * half, depth),
        substrate, spread, *tables,
    )


def conduct(step, source, coefficient, target):
    planes, rows, depth = coefficient.shape
    lane = lax.broadcasted_iota(jnp.int32, (rows, depth), 1)

    def plane(x, below):
        p = source[x]
        above = source[x + 1]
        around = above + below + pltpu.roll(p, 1, 0) + pltpu.roll(p, rows - 1, 0)
        around += jnp.where(lane == 0, 0.0, pltpu.roll(p, 1, 1))
        around += jnp.where(lane == depth - 1, 0.0, pltpu.roll(p, depth - 1, 1))
        new = p + coefficient[x] * (around - 6.0 * p)
        if step == STEPS - 1:
            target[x - DEEP] = new[PAD:rows - PAD]
        else:
            target[x] = new
        return p

    lax.fori_loop(step + 1, planes - step - 1, plane, source[step])


def y_step(plane, before, after, ahead):
    rows = plane.shape[0]
    row = lax.broadcasted_iota(jnp.int32, plane.shape, 0)
    if ahead:
        return jnp.where(row == rows - 1, after, pltpu.roll(plane, rows - 1, 0))
    return jnp.where(row == 0, before, pltpu.roll(plane, 1, 0))


def project_kernel(press, y_halo, tp, cp, current, out, part, tq):
    step = pl.program_id(0)
    n_z = press.shape[2]
    for i in range(STEPS):

        @pl.when(step == i)
        def _():
            conduct(i, (tp, tq, tq)[i], cp, (tq, tq, part)[i])

    for i in range(current.shape[1]):
        x = step * current.shape[1] + i
        p = press[x + 1]
        before = y_halo[0, pl.ds(x, 1)]
        after = y_halo[1, pl.ds(x, 1)]
        out[0, i] = current[0, i] - (press[x + 2] - press[x]) * 0.5
        out[1, i] = current[1, i] - 0.5 * (
            y_step(p, before, after, True) - y_step(p, before, after, False)
        )
        out[2, i] = current[2, i] - 0.5 * (pltpu.roll(p, n_z - 1, 1) - pltpu.roll(p, 1, 1))


def project(current, press, y_halo, tp, cp):
    _, x_local, rows, n_z = current.shape
    planes = 2
    spec = pl.BlockSpec((3, planes, rows, n_z), lambda i: (0, i, 0, 0))
    part = (tp.shape[0] - 2 * DEEP, tp.shape[1] - 2 * PAD, tp.shape[2])
    return pl.pallas_call(
        project_kernel,
        grid=(x_local // planes,),
        out_shape=[jax.ShapeDtypeStruct(current.shape, F32), jax.ShapeDtypeStruct(part, F32)],
        in_specs=[VM, VM, VM, VM, spec],
        out_specs=[spec, pl.BlockSpec(part, lambda i: (0, 0, 0))],
        scratch_shapes=[pltpu.VMEM(tp.shape, F32)],
        compiler_params=pltpu.CompilerParams(vmem_limit_bytes=20 * 2**20),
        name="projection",
    )(press, y_halo, tp, cp, current)


def per_device(
    material_flow_vector,
    tool_push_density,
    tool_warmth_excess,
    substrate_warmth_excess,
    spread_coefficient,
    source_owner_sheet,
    source_part_line,
):
    current, divergence, heat = flow(material_flow_vector, tool_push_density, tool_warmth_excess)
    slab_ids = source_owner_sheet[:, 0]
    slab_count = lax.axis_size("wide")
    component_lines = substrate_warmth_excess.shape[0] * substrate_warmth_excess.shape[1]
    target = slab_ids * component_lines + source_part_line
    partial_value = slab_heat(target, heat, slab_count * component_lines)
    solved = solve_pressure(
        divergence, partial_value, substrate_warmth_excess, spread_coefficient
    )
    return tuple(project(current, *solved))


def solution(mesh):
    return jax.shard_map(
        per_device,
        mesh=mesh,
        in_specs=(
            P(None, "wide", "narrow", None),
            P(None, "wide", "narrow", None),
            P("wide", "narrow", None),
            P("wide", "narrow", None),
            P("wide", "narrow", None),
            P(("wide", "narrow"), None),
            P(("wide", "narrow")),
        ),
        out_specs=(P(None, "wide", "narrow", None), P("wide", "narrow", None)),
        check_vma=False,
    )
```

```python
import functools
import math

import jax
import jax.numpy as jnp
import ml_dtypes
import numpy as np
from jax import lax
from jax.experimental import pallas as pl
from jax.experimental.pallas import tpu as pltpu
from jax.sharding import PartitionSpec as P

STEPS = 3
MESH = pl.DeviceIdType.MESH
F32 = jnp.float32
BF16 = jnp.bfloat16
VM = pl.BlockSpec(memory_space=pltpu.VMEM)

time_step = 0.15
rate_base = 0.5
zener_energy = 4.0
stress_exponent = 5.0
penalty = 0.001
dissipation_factor = 0.1
GROUPS = 2
DEEP = STEPS


PAD = 8
STRIP = 8


def flow_kernel(
    n_wide, n_narrow,
    vel_in, push_in, warmth_in,
    mom, div, heat,
    velp, provp, mup0, mup1, lz, push,
    vel_ys, vel_yr, mu_ys0, mu_yr0, prov_ys, prov_yr, mu_ys1, mu_yr1, mom_ys, mom_yr, mom_xr,
    load_sem, h_send, h_recv,
):
    w = lax.axis_index("wide")
    n = lax.axis_index("narrow")
    _, planes, rows, n_z = vel_in.shape
    strips = rows // STRIP
    wide_to = (lax.rem(w + n_wide - 1, n_wide), lax.rem(w + 1, n_wide))
    narrow_to = (lax.rem(n + n_narrow - 1, n_narrow), lax.rem(n + 1, n_narrow))
    body = pl.ds(PAD, rows)

    barrier = pltpu.get_barrier_semaphore()
    for side in (0, 1):
        pl.semaphore_signal(barrier, inc=1, device_id=(wide_to[side], n), device_id_type=MESH)
        pl.semaphore_signal(barrier, inc=1, device_id=(w, narrow_to[side]), device_id_type=MESH)

    loads = [
        pltpu.make_async_copy(vel_in, velp.at[:, pl.ds(1, planes), body], load_sem.at[0]),
        pltpu.make_async_copy(push_in, push, load_sem.at[1]),
    ]
    for load in loads:
        load.start()

    def wide_copy(e, side, source, target):
        return pltpu.make_async_remote_copy(
            src_ref=source, dst_ref=target,
            send_sem=h_send.at[e, side], recv_sem=h_recv.at[e, 1 - side],
            device_id=(wide_to[side], n), device_id_type=MESH,
        )

    def narrow_copy(e, side, sends, lands):
        return pltpu.make_async_remote_copy(
            src_ref=sends.at[side], dst_ref=lands.at[1 - side],
            send_sem=h_send.at[e, 2 + side], recv_sem=h_recv.at[e, 3 - side],
            device_id=(w, narrow_to[side]), device_id_type=MESH,
        )

    def x_pair(e, field, lead=()):
        return [
            wide_copy(e, 0, field.at[lead + (1, body)], field.at[lead + (planes + 1, body)]),
            wide_copy(e, 1, field.at[lead + (planes, body)], field.at[lead + (0, body)]),
        ]

    def y_pair(e, sends, lands):
        return [narrow_copy(e, side, sends, lands) for side in (0, 1)]

    def all_x(action, first=0, last=None):
        def step(x, c):
            action(x)
            return c

        lax.fori_loop(first, planes if last is None else last, step, 0)

    def y_fill(field, lands, comps):
        def fill(x):
            here = pl.ds(x, 1)
            if comps is None:
                field[x + 1, PAD - 1:PAD] = lands[0, here]
                field[x + 1, PAD + rows:PAD + rows + 1] = lands[1, here]
                return
            for i, c in enumerate(comps):
                field[c, x + 1, PAD - 1:PAD] = lands[0, i, here]
                field[c, x + 1, PAD + rows:PAD + rows + 1] = lands[1, i, here]

        all_x(fill)

    def z_ahead(a):
        return pltpu.roll(a, n_z - 1, 1)

    def z_behind(a):
        return pltpu.roll(a, 1, 1)

    loads[0].wait()

    def vel_rows(x):
        for c in range(3):
            vel_ys[0, c, pl.ds(x, 1)] = velp[c, x + 1, PAD:PAD + 1]
            vel_ys[1, c, pl.ds(x, 1)] = velp[c, x + 1, PAD + rows - 1:PAD + rows]

    all_x(vel_rows)
    pl.semaphore_wait(barrier, 4)
    every = slice(None)
    vel_x = x_pair(0, velp, (every,))
    vel_y = y_pair(0, vel_ys, vel_yr)
    for copy in vel_x + vel_y:
        copy.start()

    def zener_log(x):
        lz[x] = (zener_energy / stress_exponent) * (1.0 / warmth_in[x] - 1.0)

    all_x(zener_log)
    loads[1].wait()

    def excess(src, x, r):
        here = slice(PAD + STRIP * r, PAD + STRIP * (r + 1))
        up = slice(PAD + STRIP * r + 1, PAD + STRIP * (r + 1) + 1)
        down = slice(PAD + STRIP * r - 1, PAD + STRIP * (r + 1) - 1)
        dx = [src[c, x + 2, here] - src[c, x, here] for c in range(3)]
        dy = [src[c, x + 1, up] - src[c, x + 1, down] for c in range(3)]
        mid = [src[c, x + 1, here] for c in range(3)]
        dz = [z_ahead(m) - z_behind(m) for m in mid]
        xy, xz, yz = dy[0] + dx[1], dz[0] + dx[2], dz[1] + dy[2]
        diagonal = dx[0] * dx[0] + dy[1] * dy[1] + dz[2] * dz[2]
        return 0.5 * diagonal + 0.25 * (xy * xy + xz * xz + yz * yz)

    def mu_plane(src, mup, ys, with_heat):
        def plane(x, which):
            for r in which:
                part = slice(STRIP * r, STRIP * (r + 1))
                extra = excess(src, x, r)
                rate_sq = extra + rate_base**2
                v = jnp.exp((0.5 / stress_exponent) * jnp.log(rate_sq) + lz[x, part])
                mu = jnp.log(v + jnp.sqrt(v * v + 1.0)) * lax.rsqrt(rate_sq) * (1.0 / 3.0)
                mup[x + 1, PAD + STRIP * r:PAD + STRIP * (r + 1)] = mu
                if r == 0:
                    ys[0, pl.ds(x, 1)] = mu[0:1]
                if r == strips - 1:
                    ys[1, pl.ds(x, 1)] = mu[STRIP - 1:]
                if with_heat:
                    h = mu * extra
                    to = pl.ds(pl.multiple_of(x * rows + STRIP * r, STRIP), STRIP)
                    for m in range(n_z // 128):
                        heat[m, to] = h[:, 128 * m:128 * (m + 1)]

        return plane

    def advance_plane(mup, final):
        def plane(x, which):
            for r in which:
                part = slice(STRIP * r, STRIP * (r + 1))
                here = slice(PAD + STRIP * r, PAD + STRIP * (r + 1))
                up = slice(PAD + STRIP * r + 1, PAD + STRIP * (r + 1) + 1)
                down = slice(PAD + STRIP * r - 1, PAD + STRIP * (r + 1) - 1)
                m = mup[x + 1, here]
                m_xp = m + mup[x + 2, here]
                m_xm = m + mup[x, here]
                m_yp = m + mup[x + 1, up]
                m_ym = m + mup[x + 1, down]
                m_z = m + z_ahead(m)
                for c in range(3):
                    u = velp[c, x + 1, here]
                    flux = m_z * (z_ahead(u) - u)
                    total = flux - z_behind(flux)
                    total += m_xp * (velp[c, x + 2, here] - u) - m_xm * (u - velp[c, x, here])
                    total += m_yp * (velp[c, x + 1, up] - u) - m_ym * (u - velp[c, x + 1, down])
                    new = u + (0.5 * time_step) * total + time_step * push[c, x, part]
                    provp[c, x + 1, here] = new
                    if final:
                        mom[c, x, part] = new
                        if c == 1:
                            if r == 0:
                                mom_ys[0, pl.ds(x, 1)] = new[0:1]
                            if r == strips - 1:
                                mom_ys[1, pl.ds(x, 1)] = new[STRIP - 1:]
                    else:
                        if r == 0:
                            prov_ys[0, c, pl.ds(x, 1)] = new[0:1]
                        if r == strips - 1:
                            prov_ys[1, c, pl.ds(x, 1)] = new[STRIP - 1:]

        return plane

    def stage(action, arriving_x, arriving_y, fill, fill_x=None):
        all_x(lambda x: action(x, range(1, strips - 1)), 1, planes - 1)
        for copy in arriving_y:
            copy.wait_recv()
        fill()
        all_x(lambda x: action(x, (0, strips - 1)), 1, planes - 1)
        for copy in arriving_x:
            copy.wait_recv()
        if fill_x is not None:
            fill_x()
        all_x(lambda i: action(i * (planes - 1), range(strips)), 0, 2)

    stage(mu_plane(velp, mup0, mu_ys0, False), vel_x, vel_y,
          lambda: y_fill(velp, vel_yr, (0, 1, 2)))
    mu_x0 = x_pair(1, mup0)
    mu_y0 = y_pair(1, mu_ys0, mu_yr0)
    for copy in mu_x0 + mu_y0:
        copy.start()
    stage(advance_plane(mup0, False), mu_x0, mu_y0, lambda: y_fill(mup0, mu_yr0, None))
    prov_x = x_pair(2, provp, (every,))
    prov_y = y_pair(2, prov_ys, prov_yr)
    for copy in prov_x + prov_y:
        copy.start()
    stage(mu_plane(provp, mup1, mu_ys1, True), prov_x, prov_y,
          lambda: y_fill(provp, prov_yr, (0, 1, 2)))
    mu_x1 = x_pair(3, mup1)
    mu_y1 = y_pair(3, mu_ys1, mu_yr1)
    for copy in mu_x1 + mu_y1:
        copy.start()
    for copy in prov_x + prov_y:
        copy.wait_send()
    stage(advance_plane(mup1, True), mu_x1, mu_y1, lambda: y_fill(mup1, mu_yr1, None))
    mom_x = [
        wide_copy(4, 0, mom.at[0, 0], mom_xr.at[1]),
        wide_copy(4, 1, mom.at[0, planes - 1], mom_xr.at[0]),
    ]
    mom_y = y_pair(4, mom_ys, mom_yr)
    for copy in mom_x + mom_y:
        copy.start()
    for copy in vel_x + vel_y + mu_x0 + mu_y0 + mu_x1 + mu_y1:
        copy.wait_send()

    def fill_rows():
        def fill(x):
            here = pl.ds(x, 1)
            provp[1, x + 1, PAD - 1:PAD] = mom_yr[0, here]
            provp[1, x + 1, PAD + rows:PAD + rows + 1] = mom_yr[1, here]

        all_x(fill)

    def div_plane(x, which):
        for r in which:
            part = slice(STRIP * r, STRIP * (r + 1))
            here = slice(PAD + STRIP * r, PAD + STRIP * (r + 1))
            up = slice(PAD + STRIP * r + 1, PAD + STRIP * (r + 1) + 1)
            down = slice(PAD + STRIP * r - 1, PAD + STRIP * (r + 1) - 1)
            u = provp[2, x + 1, here]
            total = provp[0, x + 2, here] - provp[0, x, here]
            total += provp[1, x + 1, up] - provp[1, x + 1, down]
            div[x, part] = 0.5 * (total + (z_ahead(u) - z_behind(u)))

    def fill_planes():
        provp[0, 0, body] = mom_xr[0]
        provp[0, planes + 1, body] = mom_xr[1]

    stage(div_plane, mom_x, mom_y, fill_rows, fill_planes)
    for copy in mom_x + mom_y:
        copy.wait_send()


def flow(velocity, push, warmth):
    n_wide, n_narrow = lax.axis_size("wide"), lax.axis_size("narrow")
    _, planes, rows, n_z = velocity.shape
    padded = (planes + 2, PAD + rows + PAD, n_z)
    line = (2, planes, n_z)
    lines = (2, 3, planes, n_z)
    any_space = pl.BlockSpec(memory_space=pl.ANY)
    shapes = [(3,) + padded, (3,) + padded, padded, padded, (planes, rows, n_z), velocity.shape]
    shapes += [lines, lines, line, line, lines, lines, line, line, line, line, (2, rows, n_z)]
    dma = pltpu.SemaphoreType.DMA
    return pl.pallas_call(
        functools.partial(flow_kernel, n_wide, n_narrow),
        out_shape=[
            jax.ShapeDtypeStruct(velocity.shape, F32),
            jax.ShapeDtypeStruct((planes, rows, n_z), F32),
            jax.ShapeDtypeStruct((n_z // 128, planes * rows, 128), F32),
        ],
        in_specs=[any_space, any_space, VM],
        out_specs=[VM] * 3,
        scratch_shapes=[pltpu.VMEM(shape, F32) for shape in shapes]
        + [dma((2,)), dma((5, 4)), dma((5, 4))],
        compiler_params=pltpu.CompilerParams(
            collective_id=2, has_side_effects=True, vmem_limit_bytes=48 * 2**20
        ),
        name="flow",
    )(velocity, push, warmth)


def gather_kernel(target, heat, out, other):
    out[...] = jnp.zeros_like(out)
    other[...] = jnp.zeros_like(other)
    depth = heat.shape[0]

    def cell(i, c):
        for m in range(depth):
            into = out if m % 2 == 0 else other
            row = pl.ds(target[i * depth + m], 1)
            into[row] = into[row] + heat[m, pl.ds(i, 1)]
        return c

    lax.fori_loop(0, heat.shape[1], cell, 0, unroll=4)
    step = 256

    def join(i, c):
        here = pl.ds(pl.multiple_of(i * step, step), step)
        out[here] = out[here] + other[here]
        return c

    lax.fori_loop(0, out.shape[0] // step, join, 0)


def slab_heat(target, heat, lines):
    return pl.pallas_call(
        gather_kernel,
        out_shape=jax.ShapeDtypeStruct((lines, 128), F32),
        in_specs=[pl.BlockSpec(memory_space=pltpu.SMEM), VM],
        out_specs=VM,
        scratch_shapes=[pltpu.VMEM((lines, 128), F32)],
        compiler_params=pltpu.CompilerParams(vmem_limit_bytes=24 * 2**20),
        name="slab_heat",
    )(target, heat)


def real_basis(length):
    cells = np.arange(length, dtype=np.float64)
    rows = [np.full(length, 1.0 / math.sqrt(length)), (-1.0) ** cells / math.sqrt(length)]
    waves = [0, length // 2]
    for k in range(1, length // 2):
        angle = 2.0 * math.pi * k * cells / length
        rows.append(np.cos(angle) * math.sqrt(2.0 / length))
        rows.append(np.sin(angle) * math.sqrt(2.0 / length))
        waves += [k, k]
    waves = np.array(waves)
    symbol = np.sin(2.0 * math.pi * (waves % (length // 2)) / length) ** 2
    return np.stack(rows), symbol


def split_table(table):
    high = table.astype(np.float32).astype(ml_dtypes.bfloat16)
    low = (table - high.astype(np.float64)).astype(np.float32).astype(ml_dtypes.bfloat16)
    return [high, low]


def pressure_tables(n_y, n_z, n_narrow):
    basis_z, symbol_z = real_basis(n_z)
    basis_y, symbol_y = real_basis(n_y)
    forward = basis_z.T
    tables = []
    for table in (forward, forward.T, basis_y, basis_y.T):
        tables += split_table(np.ascontiguousarray(table))
    s_y = np.broadcast_to(symbol_y[:, None], (n_y, 128)).astype(np.float32)
    s_z = np.tile(symbol_z.reshape(n_narrow, 1, 64), (1, 8, 2)).astype(np.float32)
    return tables + [s_y, s_z]


def split_value(x):
    high = x.astype(BF16)
    return high, (x - high.astype(F32)).astype(BF16)


def dot_left(x, high, low):
    x_high, x_low = split_value(x)
    dot = functools.partial(jnp.dot, preferred_element_type=F32)
    return dot(x_high, high) + (dot(x_high, low) + dot(x_low, high))


def dot_right(high, low, x):
    x_high, x_low = split_value(x)
    dot = functools.partial(jnp.dot, preferred_element_type=F32)
    return dot(high, x_high) + (dot(low, x_high) + dot(high, x_low))


def pressure_kernel(
    n_wide, n_narrow,
    div, slab, substrate, spread, *rest,
):
    table_refs, rest = rest[:8], rest[8:]
    s_y, s_z, press, y_halo, tp, cp = rest[:6]
    tables, rest = rest[6:14], rest[14:]
    (
        zsend, rbuf, ubuf, vsend, zrecv, rtab, mom, mrecv, absend, ab, xrecv, yrecv, ysend,
        relay_in, relay_out, first_in, first_sum, second_in, part_xr,
        nf_send, nf_recv, nb_send, nb_recv, wf_send, wf_recv, wb_send, wb_recv, h_send, h_recv,
        f_send, f_recv, q_send, q_recv, p_send, p_recv, table_sem,
    ) = rest
    fz_h, fz_l, iz_h, iz_l, cy_h, cy_l, iy_h, iy_l = tables
    loads = [
        pltpu.make_async_copy(table_refs[i], tables[i], table_sem.at[i]) for i in range(8)
    ]

    def loaded(*which):
        for i in which:
            loads[i].wait()

    for i in (0, 1, 4, 5, 6, 7, 2, 3):
        loads[i].start()
    w = lax.axis_index("wide")
    n = lax.axis_index("narrow")
    xps, _, rows, n_z = div.shape
    n_y = s_y.shape[0]
    per = xps // GROUPS
    chunk_rows = n_y // n_wide

    def across(k):
        return lax.rem(n + k, n_narrow)

    def along(k):
        return lax.rem(w + k, n_wide)

    side = math.isqrt(n_wide)
    half = slab.shape[2] // 2
    own = (w // side, lax.rem(w, side))

    def peer(way, k):
        to = lax.rem(own[way] + k, side)
        return (to, to * side + own[1] if way == 0 else own[0] * side + to)

    quarter = half // 2

    def chunk_rows_of(way, to, part, start=0, size=None):
        at = pl.ds(way * half + part * quarter + start, quarter if size is None else size)
        return slab.at[to, :, at] if way == 0 else slab.at[:, to, at]

    def hop(way, direction, source, target, slot):
        _, device = peer(way, 1 if direction == 0 else side - 1)
        return pltpu.make_async_remote_copy(
            src_ref=source, dst_ref=target,
            send_sem=f_send.at[way, direction, slot], recv_sem=f_recv.at[way, direction, slot],
            device_id=(device, n), device_id_type=MESH,
        )

    def next_to(way, direction):
        return peer(way, 1 if direction == 0 else side - 1)[0]

    def far_hop(way, direction):
        source = chunk_rows_of(way, peer(way, 2)[0], direction)
        return hop(way, direction, source, relay_in.at[way, direction], 0)

    def near_hop(way, direction):
        source = chunk_rows_of(way, next_to(way, direction), 1 - direction)
        target = first_in.at[way, direction, :, pl.ds((1 - direction) * quarter, quarter)]
        return hop(way, direction, source, target, 1)

    def joint_hop(way, direction):
        target = first_in.at[way, direction, :, pl.ds(direction * quarter, quarter)]
        return hop(way, direction, relay_out.at[way, direction], target, 2)

    hops = [(way, direction) for way in (0, 1) for direction in (0, 1)]
    step = 32

    def relay():
        for hop_ in hops:
            far_hop(*hop_).wait_recv()
        per_slab = quarter // step

        def add(i, c):
            at = i // per_slab
            start = pl.multiple_of(lax.rem(i, per_slab) * step, step)
            here = pl.ds(start, step)
            for way, direction in hops:
                to = next_to(way, direction)
                mine = pl.ds(
                    pl.multiple_of(way * half + direction * quarter + start, step), step
                )
                own_part = slab[to, at, mine] if way == 0 else slab[at, to, mine]
                relay_out[way, direction, at, here] = relay_in[way, direction, at, here] + own_part
            return c

        lax.fori_loop(0, side * per_slab, add, 0)
        for hop_ in hops:
            joint_hop(*hop_).start()

    def second_copy(way, k):
        to, device = peer(1 - way, k)
        return pltpu.make_async_remote_copy(
            src_ref=first_sum.at[way, to], dst_ref=second_in.at[way, k],
            send_sem=q_send.at[way, k], recv_sem=q_recv.at[way, k],
            device_id=(device, n), device_id_type=MESH,
        )

    halves = [(way, k) for way in (0, 1) for k in range(1, side)]

    def first_total():
        for hop_ in hops:
            near_hop(*hop_).wait_recv()
            joint_hop(*hop_).wait_recv()
        per_slab = half // step

        def add(i, c):
            at = i // per_slab
            start = pl.multiple_of(lax.rem(i, per_slab) * step, step)
            here = pl.ds(start, step)
            for way in (0, 1):
                mine = pl.ds(pl.multiple_of(way * half + start, step), step)
                total = slab[own[0], at, mine] if way == 0 else slab[at, own[1], mine]
                first_sum[way, at, here] = (
                    total + first_in[way, 0, at, here] + first_in[way, 1, at, here]
                )
            return c

        lax.fori_loop(0, side * per_slab, add, 0)
        for way, k in halves:
            second_copy(way, k).start()

    planes = substrate.shape[0]
    part_rows = substrate.shape[1]
    inside = pl.ds(PAD, part_rows)
    last_w, last_n = n_wide - 1, n_narrow - 1
    wide_near = (lax.rem(w + last_w, n_wide), lax.rem(w + 1, n_wide))
    narrow_near = (lax.rem(n + last_n, n_narrow), lax.rem(n + 1, n_narrow))

    def part_x(field, e, side_):
        start = planes if side_ else DEEP
        return pltpu.make_async_remote_copy(
            src_ref=field.at[pl.ds(start, DEEP), inside], dst_ref=part_xr.at[e, 1 - side_],
            send_sem=p_send.at[e, side_], recv_sem=p_recv.at[e, 1 - side_],
            device_id=(wide_near[side_], n), device_id_type=MESH,
        )

    def part_y(field, e, side_):
        start = part_rows if side_ else PAD
        land = 0 if side_ else PAD + part_rows
        return pltpu.make_async_remote_copy(
            src_ref=field.at[:, pl.ds(start, PAD)], dst_ref=field.at[:, pl.ds(land, PAD)],
            send_sem=p_send.at[e, 2 + side_], recv_sem=p_recv.at[e, 3 - side_],
            device_id=(w, narrow_near[side_]), device_id_type=MESH,
        )

    def part_x_start(field, e):
        for i in (0, 1):
            part_x(field, e, i).start()

    def part_x_end(field, e):
        for i in (0, 1):
            part_x(field, e, i).wait_recv()
        field[0:DEEP, PAD:PAD + part_rows] = jnp.where(w == 0, 0.0, part_xr[e, 0])
        field[planes + DEEP:, PAD:PAD + part_rows] = jnp.where(w == last_w, 0.0, part_xr[e, 1])
        for i in (0, 1):
            part_y(field, e, i).start()

    def part_y_end(field, e):
        for i in (0, 1):
            part_y(field, e, i).wait_recv()

        @pl.when(n == 0)
        def _():
            field[:, 0:PAD] = jnp.zeros_like(field[:, 0:PAD])

        @pl.when(n == last_n)
        def _():
            field[:, PAD + part_rows:] = jnp.zeros_like(field[:, PAD + part_rows:])

        for i in (0, 1):
            part_x(field, e, i).wait_send()
            part_y(field, e, i).wait_send()

    def part_start():
        for way, k in halves:
            second_copy(way, k).wait_recv()
        per_half = planes // 2
        for way in (0, 1):
            mine = own[1 - way]
            for i in range(per_half):
                here = slice(i * part_rows, (i + 1) * part_rows)
                total = first_sum[way, mine, here]
                for k in range(1, side):
                    total = total + second_in[way, k, here]
                x = way * per_half + i
                tp[DEEP + x, PAD:PAD + part_rows] = substrate[x] + dissipation_factor * total
        part_x_start(tp, 0)

    barrier = pltpu.get_barrier_semaphore()

    def greet_n(k, c):
        pl.semaphore_signal(barrier, inc=1, device_id=(w, across(k)), device_id_type=MESH)
        return c

    def greet_w(k, c):
        pl.semaphore_signal(barrier, inc=1, device_id=(along(k), n), device_id_type=MESH)
        return c

    lax.fori_loop(1, n_narrow, greet_n, 0)
    lax.fori_loop(1, n_wide, greet_w, 0)

    lane = lax.broadcasted_iota(jnp.int32, (per * rows, 128), 1)
    low_half = lane < 64

    def forward_copy(g, k):
        to = across(k)
        return pltpu.make_async_remote_copy(
            src_ref=zsend.at[to, pl.ds(g * per, per)],
            dst_ref=rbuf.at[pl.ds(g * per, per), pl.ds(pl.multiple_of(n * rows, rows), rows)],
            send_sem=nf_send.at[g, k],
            recv_sem=nf_recv.at[g, k],
            device_id=(w, to),
            device_id_type=MESH,
        )

    def forward_arrival(g, k):
        source = across(n_narrow - k)
        here = rbuf.at[pl.ds(g * per, per), pl.ds(pl.multiple_of(source * rows, rows), rows)]
        return pltpu.make_async_remote_copy(
            src_ref=here, dst_ref=here, send_sem=nf_send.at[g, k], recv_sem=nf_recv.at[g, k],
            device_id=(w, source), device_id_type=MESH,
        )

    loaded(0, 1)
    for g in range(GROUPS):
        lines = div[g * per:(g + 1) * per].reshape(per * 2 * rows, n_z)
        lines = dot_left(lines, fz_h[...], fz_l[...]).reshape(per, 2, rows, n_z)
        even = lines[:, 0].reshape(per * rows, n_z)
        odd = lines[:, 1].reshape(per * rows, n_z)
        for m in range(n_z // 128):
            e = even[:, 128 * m:128 * (m + 1)]
            o = pltpu.roll(odd[:, 128 * m:128 * (m + 1)], 64, 1)
            first = jnp.where(low_half, e, o)
            second = jnp.where(low_half, o, e)
            zsend[2 * m, g * per:(g + 1) * per] = first.reshape(per, rows, 128)
            zsend[2 * m + 1, g * per:(g + 1) * per] = second.reshape(per, rows, 128)
        if g == 0:
            pl.semaphore_wait(barrier, n_narrow - 1 + n_wide - 1)

        def launch(k, c):
            forward_copy(g, k).start()
            return c

        lax.fori_loop(1, n_narrow, launch, 0)
        if g == 0:
            for hop_ in hops:
                far_hop(*hop_).start()
            cp[DEEP:DEEP + planes, PAD:PAD + part_rows] = spread[...]
            part_x_start(cp, 1)

    for hop_ in hops:
        near_hop(*hop_).start()
    s = s_y[...] + s_z[n][0:1, :] + penalty
    root = jnp.sqrt(s * (1.0 + s))
    rtab[0] = 1.0 / (1.0 + 2.0 * s + 2.0 * root)
    rtab[1] = -1.0 / root

    for g in range(GROUPS):
        span = slice(g * per, (g + 1) * per)
        rbuf[span, pl.ds(pl.multiple_of(n * rows, rows), rows)] = zsend[n, span]
        if g == 0:
            part_x_end(cp, 1)
            relay()
            loaded(4, 5)

        def arrive(k, c):
            forward_arrival(g, k).wait_recv()
            return c

        lax.fori_loop(1, n_narrow, arrive, 0)
        lines = jnp.concatenate([rbuf[xp] for xp in range(g * per, (g + 1) * per)], axis=1)
        lines = dot_right(cy_h[...], cy_l[...], lines)
        for i in range(per):
            ubuf[g * per + i] = lines[:, 128 * i:128 * (i + 1)]

    block = 16

    def moments(i, c):
        here = pl.ds(pl.multiple_of(i * block, block), block)
        r = rtab[0, here]
        f = ubuf[0, here]
        b = ubuf[xps - 1, here]
        for xp in range(1, xps):
            f = f * r + ubuf[xp, here]
            b = b * r + ubuf[xps - 1 - xp, here]
        mom[0, here] = f
        mom[1, here] = b
        return c

    lax.fori_loop(0, n_y // block, moments, 0)

    def chunk(index):
        return pl.ds(pl.multiple_of(index * chunk_rows, chunk_rows), chunk_rows)

    def out_copy(k):
        to = along(k)
        return pltpu.make_async_remote_copy(
            src_ref=mom.at[:, chunk(to)], dst_ref=mrecv.at[w],
            send_sem=wf_send.at[k], recv_sem=wf_recv.at[k],
            device_id=(to, n), device_id_type=MESH,
        )

    def out_arrival(k):
        here = mrecv.at[along(n_wide - k)]
        return pltpu.make_async_remote_copy(
            src_ref=here, dst_ref=here, send_sem=wf_send.at[k], recv_sem=wf_recv.at[k],
            device_id=(along(n_wide - k), n), device_id_type=MESH,
        )

    def back_copy(k):
        to = along(k)
        return pltpu.make_async_remote_copy(
            src_ref=absend.at[to], dst_ref=ab.at[:, chunk(w)],
            send_sem=wb_send.at[k], recv_sem=wb_recv.at[k],
            device_id=(to, n), device_id_type=MESH,
        )

    def back_arrival(k):
        here = ab.at[:, chunk(along(n_wide - k))]
        return pltpu.make_async_remote_copy(
            src_ref=here, dst_ref=here, send_sem=wb_send.at[k], recv_sem=wb_recv.at[k],
            device_id=(along(n_wide - k), n), device_id_type=MESH,
        )

    def each(count, action):
        def body(k, c):
            action(k)
            return c

        lax.fori_loop(1, count, body, 0)

    each(n_wide, lambda k: out_copy(k).start())
    mrecv[w] = mom[:, chunk(w)]
    r = rtab[0, chunk(w)]
    q = r
    for _ in range(int(math.log2(xps))):
        q = q * q
    total = q
    for _ in range(int(math.log2(n_wide))):
        total = total * total
    closing = 1.0 / (1.0 - total)
    each(n_wide, lambda k: out_arrival(k).wait_recv())
    f = mrecv[0, 0]
    b = mrecv[n_wide - 1, 1]
    for j in range(1, n_wide):
        f = f * q + mrecv[j, 0]
        b = b * q + mrecv[n_wide - 1 - j, 1]
    f = f * closing
    b = b * closing
    for j in range(n_wide):
        absend[j, 0] = f
        absend[n_wide - 1 - j, 1] = b
        f = f * q + mrecv[j, 0]
        b = b * q + mrecv[n_wide - 1 - j, 1]
    each(n_wide, lambda k: back_copy(k).start())
    ab[:, chunk(w)] = absend[w]
    each(n_wide, lambda k: back_arrival(k).wait_recv())

    def solve(i, c):
        here = pl.ds(pl.multiple_of(i * block, block), block)
        r = rtab[0, here]
        scale = rtab[1, here]
        f = ab[0, here]
        b = ab[1, here]
        behind = []
        for xp in range(xps - 1, -1, -1):
            rb = b * r
            behind.append(rb)
            b = rb + ubuf[xp, here]
        for xp in range(xps):
            f = f * r + ubuf[xp, here]
            ubuf[xp, here] = scale * (f + behind[xps - 1 - xp])
        return c

    lax.fori_loop(0, n_y // block, solve, 0)

    def backward_copy(g, k):
        to = across(k)
        return pltpu.make_async_remote_copy(
            src_ref=vsend.at[to, pl.ds(g * per, per)],
            dst_ref=zrecv.at[n, pl.ds(g * per, per)],
            send_sem=nb_send.at[g, k],
            recv_sem=nb_recv.at[g, k],
            device_id=(w, to),
            device_id_type=MESH,
        )

    def backward_arrival(g, k):
        source = across(n_narrow - k)
        here = zrecv.at[source, pl.ds(g * per, per)]
        return pltpu.make_async_remote_copy(
            src_ref=here, dst_ref=here, send_sem=nb_send.at[g, k], recv_sem=nb_recv.at[g, k],
            device_id=(w, source), device_id_type=MESH,
        )

    loaded(6, 7)
    for g in range(GROUPS):
        span = slice(g * per, (g + 1) * per)
        lines = jnp.concatenate([ubuf[xp] for xp in range(g * per, (g + 1) * per)], axis=1)
        lines = dot_right(iy_h[...], iy_l[...], lines)
        for to in range(n_narrow):
            for i in range(per):
                vsend[to, g * per + i] = lines[to * rows:(to + 1) * rows, 128 * i:128 * (i + 1)]
        each(n_narrow, lambda k: backward_copy(g, k).start())
        zrecv[n, span] = vsend[n, span]

    first_total()
    part_y_end(cp, 1)
    loaded(2, 3)

    def x_halo(side):
        source = 2 * xps if side else 1
        return pltpu.make_async_remote_copy(
            src_ref=press.at[source], dst_ref=xrecv.at[1 - side],
            send_sem=h_send.at[side], recv_sem=h_recv.at[1 - side],
            device_id=(wide_near[side], n), device_id_type=MESH,
        )

    def y_halo_copy(side):
        return pltpu.make_async_remote_copy(
            src_ref=ysend.at[side], dst_ref=yrecv.at[1 - side],
            send_sem=h_send.at[2 + side], recv_sem=h_recv.at[3 - side],
            device_id=(w, narrow_near[side]), device_id_type=MESH,
        )

    for g in range(GROUPS):
        each(n_narrow, lambda k: backward_arrival(g, k).wait_recv())
        evens, odds = [], []
        for m in range(n_z // 128):
            first = zrecv[2 * m, g * per:(g + 1) * per].reshape(per * rows, 128)
            second = zrecv[2 * m + 1, g * per:(g + 1) * per].reshape(per * rows, 128)
            evens.append(jnp.where(low_half, first, second))
            odds.append(pltpu.roll(jnp.where(low_half, second, first), 64, 1))
        lines = jnp.concatenate(
            [jnp.concatenate(evens, axis=1), jnp.concatenate(odds, axis=1)], axis=0
        )
        lines = dot_left(lines, iz_h[...], iz_l[...])
        even, odd = lines[:per * rows], lines[per * rows:]
        for i in range(per):
            for parity, part in ((0, even), (1, odd)):
                x = 2 * (g * per + i) + parity
                plane = part[i * rows:(i + 1) * rows]
                press[x + 1] = plane
                ysend[0, x] = plane[0]
                ysend[1, x] = plane[rows - 1]
        if g == 0:
            x_halo(0).start()
            part_start()
    x_halo(1).start()
    y_halo_copy(0).start()
    y_halo_copy(1).start()
    part_x_end(tp, 0)

    for way, k in halves:
        second_copy(way, k).wait_send()
    for hop_ in hops:
        far_hop(*hop_).wait_send()
        near_hop(*hop_).wait_send()
        joint_hop(*hop_).wait_send()
    for g in range(GROUPS):
        each(n_narrow, lambda k: forward_copy(g, k).wait_send())
        each(n_narrow, lambda k: backward_copy(g, k).wait_send())
    each(n_wide, lambda k: out_copy(k).wait_send())
    each(n_wide, lambda k: back_copy(k).wait_send())
    for side in (0, 1):
        x_halo(side).wait()
        y_halo_copy(side).wait()
    press[0] = xrecv[0]
    press[2 * xps + 1] = xrecv[1]
    y_halo[...] = yrecv[...]
    part_y_end(tp, 0)


def solve_pressure(divergence, slab, substrate, spread):
    n_wide, n_narrow = lax.axis_size("wide"), lax.axis_size("narrow")
    x_local, rows, n_z = divergence.shape
    n_y = rows * n_narrow
    xps = x_local // 2
    tables = [jnp.asarray(t) for t in pressure_tables(n_y, n_z, n_narrow)]
    dma = pltpu.SemaphoreType.DMA
    field = (xps, n_y, 128)
    turned = (n_narrow, xps, rows, 128)
    chunk_rows = n_y // n_wide
    side = math.isqrt(n_wide)
    planes, part_rows, depth = substrate.shape
    half = planes * part_rows // 2
    part = (planes + 2 * DEEP, part_rows + 2 * PAD, depth)
    any_space = pl.BlockSpec(memory_space=pl.ANY)
    return pl.pallas_call(
        functools.partial(pressure_kernel, n_wide, n_narrow),
        out_shape=[
            jax.ShapeDtypeStruct((x_local + 2, rows, n_z), F32),
            jax.ShapeDtypeStruct((2, x_local, n_z), F32),
            jax.ShapeDtypeStruct(part, F32),
            jax.ShapeDtypeStruct(part, F32),
        ],
        in_specs=[VM, VM, VM, VM] + [any_space] * 8 + [VM, VM],
        out_specs=[VM] * 4,
        scratch_shapes=[pltpu.VMEM(t.shape, BF16) for t in tables[:8]]
        + [
            pltpu.VMEM(turned, F32),
            pltpu.VMEM(field, F32),
            pltpu.VMEM(field, F32),
            pltpu.VMEM(turned, F32),
            pltpu.VMEM(turned, F32),
            pltpu.VMEM((2, n_y, 128), F32),
            pltpu.VMEM((2, n_y, 128), F32),
            pltpu.VMEM((n_wide, 2, chunk_rows, 128), F32),
            pltpu.VMEM((n_wide, 2, chunk_rows, 128), F32),
            pltpu.VMEM((2, n_y, 128), F32),
            pltpu.VMEM((2, rows, n_z), F32),
            pltpu.VMEM((2, x_local, n_z), F32),
            pltpu.VMEM((2, x_local, n_z), F32),
            pltpu.VMEM((2, 2, side, half // 2, depth), F32),
            pltpu.VMEM((2, 2, side, half // 2, depth), F32),
            pltpu.VMEM((2, 2, side, half, depth), F32),
            pltpu.VMEM((2, side, half, depth), F32),
            pltpu.VMEM((2, side, half, depth), F32),
            pltpu.VMEM((2, 2, DEEP, part_rows, depth), F32),
            dma((GROUPS, n_narrow)),
            dma((GROUPS, n_narrow)),
            dma((GROUPS, n_narrow)),
            dma((GROUPS, n_narrow)),
            dma((n_wide,)),
            dma((n_wide,)),
            dma((n_wide,)),
            dma((n_wide,)),
            dma((4,)),
            dma((4,)),
            dma((2, 2, 3)),
            dma((2, 2, 3)),
            dma((2, side)),
            dma((2, side)),
            dma((2, 4)),
            dma((2, 4)),
            dma((8,)),
        ],
        compiler_params=pltpu.CompilerParams(
            collective_id=1, has_side_effects=True, vmem_limit_bytes=32 * 2**20
        ),
        name="pressure",
    )(
        divergence.reshape(xps, 2, rows, n_z),
        slab.reshape(side, side, 2 * half, depth),
        substrate, spread, *tables,
    )


def conduct(step, span, source, coefficient, target):
    planes, rows, depth = coefficient.shape
    lane = lax.broadcasted_iota(jnp.int32, (rows, depth), 1)

    def plane(x, c):
        p = source[x]
        around = source[x + 1] + source[x - 1] + pltpu.roll(p, 1, 0) + pltpu.roll(p, rows - 1, 0)
        around += jnp.where(lane == 0, 0.0, pltpu.roll(p, 1, 1))
        around += jnp.where(lane == depth - 1, 0.0, pltpu.roll(p, depth - 1, 1))
        new = p + coefficient[x] * (around - 6.0 * p)
        if step == STEPS - 1:
            target[x - DEEP] = new[PAD:rows - PAD]
        else:
            target[x] = new
        return c

    lax.fori_loop(*span, plane, 0, unroll=2)


def y_step(plane, before, after, ahead):
    rows = plane.shape[0]
    row = lax.broadcasted_iota(jnp.int32, plane.shape, 0)
    if ahead:
        return jnp.where(row == rows - 1, after, pltpu.roll(plane, rows - 1, 0))
    return jnp.where(row == 0, before, pltpu.roll(plane, 1, 0))


def project_kernel(lead, trail, y_halo, tp, cp, current, out, part, tq, tr):
    step = pl.program_id(0)
    planes, n_z = current.shape[1], current.shape[3]
    total = tp.shape[0]
    for i in range(2 * STEPS):

        @pl.when(step == i)
        def _():
            first, last = i // 2 + 1, total - i // 2 - 1
            span = (first, total // 2) if i % 2 == 0 else (total // 2, last)
            conduct(i // 2, span, (tp, tq, tr)[i // 2], cp, (tq, tr, part)[i // 2])

    block = [lead[0], lead[1], trail[0], trail[1]]
    for i in range(planes):
        x = step * planes + i
        p = block[i + 1]
        before = y_halo[0, pl.ds(x, 1)]
        after = y_halo[1, pl.ds(x, 1)]
        out[0, i] = current[0, i] - (block[i + 2] - block[i]) * 0.5
        out[1, i] = current[1, i] - 0.5 * (
            y_step(p, before, after, True) - y_step(p, before, after, False)
        )
        out[2, i] = current[2, i] - 0.5 * (pltpu.roll(p, n_z - 1, 1) - pltpu.roll(p, 1, 1))


def project(current, press, y_halo, tp, cp):
    _, x_local, rows, n_z = current.shape
    planes = 2
    spec = pl.BlockSpec((3, planes, rows, n_z), lambda i: (0, i, 0, 0))
    part = (tp.shape[0] - 2 * DEEP, tp.shape[1] - 2 * PAD, tp.shape[2])
    return pl.pallas_call(
        project_kernel,
        grid=(x_local // planes,),
        out_shape=[jax.ShapeDtypeStruct(current.shape, F32), jax.ShapeDtypeStruct(part, F32)],
        in_specs=[
            pl.BlockSpec((planes, rows, n_z), lambda i: (i, 0, 0)),
            pl.BlockSpec((planes, rows, n_z), lambda i: (i + 1, 0, 0)),
            VM, VM, VM, spec,
        ],
        out_specs=[spec, pl.BlockSpec(part, lambda i: (0, 0, 0))],
        scratch_shapes=[pltpu.VMEM(tp.shape, F32), pltpu.VMEM(tp.shape, F32)],
        compiler_params=pltpu.CompilerParams(vmem_limit_bytes=20 * 2**20),
        name="projection",
    )(press, press, y_halo, tp, cp, current)


def per_device(
    material_flow_vector,
    tool_push_density,
    tool_warmth_excess,
    substrate_warmth_excess,
    spread_coefficient,
    source_owner_sheet,
    source_part_line,
):
    current, divergence, heat = flow(material_flow_vector, tool_push_density, tool_warmth_excess)
    slab_ids = source_owner_sheet[:, 0]
    slab_count = lax.axis_size("wide")
    component_lines = substrate_warmth_excess.shape[0] * substrate_warmth_excess.shape[1]
    target = slab_ids * component_lines + source_part_line
    partial_value = slab_heat(target, heat, slab_count * component_lines)
    solved = solve_pressure(
        divergence, partial_value, substrate_warmth_excess, spread_coefficient
    )
    return tuple(project(current, *solved))


def solution(mesh):
    return jax.shard_map(
        per_device,
        mesh=mesh,
        in_specs=(
            P(None, "wide", "narrow", None),
            P(None, "wide", "narrow", None),
            P("wide", "narrow", None),
            P("wide", "narrow", None),
            P("wide", "narrow", None),
            P(("wide", "narrow"), None),
            P(("wide", "narrow")),
        ),
        out_specs=(P(None, "wide", "narrow", None), P("wide", "narrow", None)),
        check_vma=False,
    )
```

```python
import functools
import math

import jax
import jax.numpy as jnp
import ml_dtypes
import numpy as np
from jax import lax
from jax.experimental import pallas as pl
from jax.experimental.pallas import tpu as pltpu
from jax.sharding import PartitionSpec as P

STEPS = 3
MESH = pl.DeviceIdType.MESH
F32 = jnp.float32
BF16 = jnp.bfloat16
VM = pl.BlockSpec(memory_space=pltpu.VMEM)

time_step = 0.15
rate_base = 0.5
zener_energy = 4.0
stress_exponent = 5.0
penalty = 0.001
dissipation_factor = 0.1
GROUPS = 2
DEEP = STEPS


PAD = 8
STRIP = 8


def flow_kernel(
    n_wide, n_narrow,
    vel_in, push_in, warmth_in,
    mom, div, heat,
    velp, provp, mup0, mup1, lz, push,
    vel_ys, vel_yr, mu_ys0, mu_yr0, prov_ys, prov_yr, mu_ys1, mu_yr1, mom_ys, mom_yr, mom_xr,
    load_sem, h_send, h_recv,
):
    w = lax.axis_index("wide")
    n = lax.axis_index("narrow")
    _, planes, rows, n_z = vel_in.shape
    strips = rows // STRIP
    wide_to = (lax.rem(w + n_wide - 1, n_wide), lax.rem(w + 1, n_wide))
    narrow_to = (lax.rem(n + n_narrow - 1, n_narrow), lax.rem(n + 1, n_narrow))
    body = pl.ds(PAD, rows)

    barrier = pltpu.get_barrier_semaphore()
    for side in (0, 1):
        pl.semaphore_signal(barrier, inc=1, device_id=(wide_to[side], n), device_id_type=MESH)
        pl.semaphore_signal(barrier, inc=1, device_id=(w, narrow_to[side]), device_id_type=MESH)

    loads = [
        pltpu.make_async_copy(vel_in, velp.at[:, pl.ds(1, planes), body], load_sem.at[0]),
        pltpu.make_async_copy(push_in, push, load_sem.at[1]),
    ]
    for load in loads:
        load.start()

    def wide_copy(e, side, source, target):
        return pltpu.make_async_remote_copy(
            src_ref=source, dst_ref=target,
            send_sem=h_send.at[e, side], recv_sem=h_recv.at[e, 1 - side],
            device_id=(wide_to[side], n), device_id_type=MESH,
        )

    def narrow_copy(e, side, sends, lands):
        return pltpu.make_async_remote_copy(
            src_ref=sends.at[side], dst_ref=lands.at[1 - side],
            send_sem=h_send.at[e, 2 + side], recv_sem=h_recv.at[e, 3 - side],
            device_id=(w, narrow_to[side]), device_id_type=MESH,
        )

    def x_pair(e, field, lead=()):
        return [
            wide_copy(e, 0, field.at[lead + (1, body)], field.at[lead + (planes + 1, body)]),
            wide_copy(e, 1, field.at[lead + (planes, body)], field.at[lead + (0, body)]),
        ]

    def y_pair(e, sends, lands):
        return [narrow_copy(e, side, sends, lands) for side in (0, 1)]

    def all_x(action, first=0, last=None, unroll=1):
        def step(x, c):
            action(x)
            return c

        lax.fori_loop(first, planes if last is None else last, step, 0, unroll=unroll)

    def y_fill(field, lands, comps):
        def fill(x):
            here = pl.ds(x, 1)
            if comps is None:
                field[x + 1, PAD - 1:PAD] = lands[0, here]
                field[x + 1, PAD + rows:PAD + rows + 1] = lands[1, here]
                return
            for i, c in enumerate(comps):
                field[c, x + 1, PAD - 1:PAD] = lands[0, i, here]
                field[c, x + 1, PAD + rows:PAD + rows + 1] = lands[1, i, here]

        all_x(fill)

    def z_ahead(a):
        return pltpu.roll(a, n_z - 1, 1)

    def z_behind(a):
        return pltpu.roll(a, 1, 1)

    loads[0].wait()

    def vel_rows(x):
        for c in range(3):
            vel_ys[0, c, pl.ds(x, 1)] = velp[c, x + 1, PAD:PAD + 1]
            vel_ys[1, c, pl.ds(x, 1)] = velp[c, x + 1, PAD + rows - 1:PAD + rows]

    all_x(vel_rows)
    pl.semaphore_wait(barrier, 4)
    every = slice(None)
    vel_x = x_pair(0, velp, (every,))
    vel_y = y_pair(0, vel_ys, vel_yr)
    for copy in vel_x + vel_y:
        copy.start()

    def zener_log(x):
        lz[x] = (zener_energy / stress_exponent) * (1.0 / warmth_in[x] - 1.0)

    all_x(zener_log)
    loads[1].wait()

    def excess(src, x, r):
        here = slice(PAD + STRIP * r, PAD + STRIP * (r + 1))
        up = slice(PAD + STRIP * r + 1, PAD + STRIP * (r + 1) + 1)
        down = slice(PAD + STRIP * r - 1, PAD + STRIP * (r + 1) - 1)
        dx = [src[c, x + 2, here] - src[c, x, here] for c in range(3)]
        dy = [src[c, x + 1, up] - src[c, x + 1, down] for c in range(3)]
        mid = [src[c, x + 1, here] for c in range(3)]
        dz = [z_ahead(m) - z_behind(m) for m in mid]
        xy, xz, yz = dy[0] + dx[1], dz[0] + dx[2], dz[1] + dy[2]
        diagonal = dx[0] * dx[0] + dy[1] * dy[1] + dz[2] * dz[2]
        return 0.5 * diagonal + 0.25 * (xy * xy + xz * xz + yz * yz)

    def mu_plane(src, mup, ys, with_heat):
        def plane(x, which):
            for r in which:
                part = slice(STRIP * r, STRIP * (r + 1))
                extra = excess(src, x, r)
                rate_sq = extra + rate_base**2
                v = jnp.exp((0.5 / stress_exponent) * jnp.log(rate_sq) + lz[x, part])
                mu = jnp.log(v + jnp.sqrt(v * v + 1.0)) * lax.rsqrt(rate_sq) * (1.0 / 3.0)
                mup[x + 1, PAD + STRIP * r:PAD + STRIP * (r + 1)] = mu
                if r == 0:
                    ys[0, pl.ds(x, 1)] = mu[0:1]
                if r == strips - 1:
                    ys[1, pl.ds(x, 1)] = mu[STRIP - 1:]
                if with_heat:
                    h = mu * extra
                    to = pl.ds(pl.multiple_of(x * rows + STRIP * r, STRIP), STRIP)
                    for m in range(n_z // 128):
                        heat[m, to] = h[:, 128 * m:128 * (m + 1)]

        return plane

    def advance_plane(mup, final):
        def plane(x, which):
            for r in which:
                part = slice(STRIP * r, STRIP * (r + 1))
                here = slice(PAD + STRIP * r, PAD + STRIP * (r + 1))
                up = slice(PAD + STRIP * r + 1, PAD + STRIP * (r + 1) + 1)
                down = slice(PAD + STRIP * r - 1, PAD + STRIP * (r + 1) - 1)
                m = mup[x + 1, here]
                m_xp = m + mup[x + 2, here]
                m_xm = m + mup[x, here]
                m_yp = m + mup[x + 1, up]
                m_ym = m + mup[x + 1, down]
                m_z = m + z_ahead(m)
                for c in range(3):
                    u = velp[c, x + 1, here]
                    flux = m_z * (z_ahead(u) - u)
                    total = flux - z_behind(flux)
                    total += m_xp * (velp[c, x + 2, here] - u) - m_xm * (u - velp[c, x, here])
                    total += m_yp * (velp[c, x + 1, up] - u) - m_ym * (u - velp[c, x + 1, down])
                    new = u + (0.5 * time_step) * total + time_step * push[c, x, part]
                    provp[c, x + 1, here] = new
                    if final:
                        mom[c, x, part] = new
                        if c == 1:
                            if r == 0:
                                mom_ys[0, pl.ds(x, 1)] = new[0:1]
                            if r == strips - 1:
                                mom_ys[1, pl.ds(x, 1)] = new[STRIP - 1:]
                    else:
                        if r == 0:
                            prov_ys[0, c, pl.ds(x, 1)] = new[0:1]
                        if r == strips - 1:
                            prov_ys[1, c, pl.ds(x, 1)] = new[STRIP - 1:]

        return plane

    def stage(action, arriving_x, arriving_y, fill, fill_x=None):
        all_x(lambda x: action(x, range(1, strips - 1)), 1, planes - 1, 2)
        for copy in arriving_y:
            copy.wait_recv()
        fill()
        all_x(lambda x: action(x, (0, strips - 1)), 1, planes - 1, 2)
        for copy in arriving_x:
            copy.wait_recv()
        if fill_x is not None:
            fill_x()
        all_x(lambda i: action(i * (planes - 1), range(strips)), 0, 2)

    stage(mu_plane(velp, mup0, mu_ys0, False), vel_x, vel_y,
          lambda: y_fill(velp, vel_yr, (0, 1, 2)))
    mu_x0 = x_pair(1, mup0)
    mu_y0 = y_pair(1, mu_ys0, mu_yr0)
    for copy in mu_x0 + mu_y0:
        copy.start()
    stage(advance_plane(mup0, False), mu_x0, mu_y0, lambda: y_fill(mup0, mu_yr0, None))
    prov_x = x_pair(2, provp, (every,))
    prov_y = y_pair(2, prov_ys, prov_yr)
    for copy in prov_x + prov_y:
        copy.start()
    stage(mu_plane(provp, mup1, mu_ys1, True), prov_x, prov_y,
          lambda: y_fill(provp, prov_yr, (0, 1, 2)))
    mu_x1 = x_pair(3, mup1)
    mu_y1 = y_pair(3, mu_ys1, mu_yr1)
    for copy in mu_x1 + mu_y1:
        copy.start()
    for copy in prov_x + prov_y:
        copy.wait_send()
    stage(advance_plane(mup1, True), mu_x1, mu_y1, lambda: y_fill(mup1, mu_yr1, None))
    mom_x = [
        wide_copy(4, 0, mom.at[0, 0], mom_xr.at[1]),
        wide_copy(4, 1, mom.at[0, planes - 1], mom_xr.at[0]),
    ]
    mom_y = y_pair(4, mom_ys, mom_yr)
    for copy in mom_x + mom_y:
        copy.start()
    for copy in vel_x + vel_y + mu_x0 + mu_y0 + mu_x1 + mu_y1:
        copy.wait_send()

    def fill_rows():
        def fill(x):
            here = pl.ds(x, 1)
            provp[1, x + 1, PAD - 1:PAD] = mom_yr[0, here]
            provp[1, x + 1, PAD + rows:PAD + rows + 1] = mom_yr[1, here]

        all_x(fill)

    def div_plane(x, which):
        for r in which:
            part = slice(STRIP * r, STRIP * (r + 1))
            here = slice(PAD + STRIP * r, PAD + STRIP * (r + 1))
            up = slice(PAD + STRIP * r + 1, PAD + STRIP * (r + 1) + 1)
            down = slice(PAD + STRIP * r - 1, PAD + STRIP * (r + 1) - 1)
            u = provp[2, x + 1, here]
            total = provp[0, x + 2, here] - provp[0, x, here]
            total += provp[1, x + 1, up] - provp[1, x + 1, down]
            div[x, part] = 0.5 * (total + (z_ahead(u) - z_behind(u)))

    def fill_planes():
        provp[0, 0, body] = mom_xr[0]
        provp[0, planes + 1, body] = mom_xr[1]

    stage(div_plane, mom_x, mom_y, fill_rows, fill_planes)
    for copy in mom_x + mom_y:
        copy.wait_send()


def flow(velocity, push, warmth):
    n_wide, n_narrow = lax.axis_size("wide"), lax.axis_size("narrow")
    _, planes, rows, n_z = velocity.shape
    padded = (planes + 2, PAD + rows + PAD, n_z)
    line = (2, planes, n_z)
    lines = (2, 3, planes, n_z)
    any_space = pl.BlockSpec(memory_space=pl.ANY)
    shapes = [(3,) + padded, (3,) + padded, padded, padded, (planes, rows, n_z), velocity.shape]
    shapes += [lines, lines, line, line, lines, lines, line, line, line, line, (2, rows, n_z)]
    dma = pltpu.SemaphoreType.DMA
    return pl.pallas_call(
        functools.partial(flow_kernel, n_wide, n_narrow),
        out_shape=[
            jax.ShapeDtypeStruct(velocity.shape, F32),
            jax.ShapeDtypeStruct((planes, rows, n_z), F32),
            jax.ShapeDtypeStruct((n_z // 128, planes * rows, 128), F32),
        ],
        in_specs=[any_space, any_space, VM],
        out_specs=[VM] * 3,
        scratch_shapes=[pltpu.VMEM(shape, F32) for shape in shapes]
        + [dma((2,)), dma((5, 4)), dma((5, 4))],
        compiler_params=pltpu.CompilerParams(
            collective_id=2, has_side_effects=True, vmem_limit_bytes=48 * 2**20
        ),
        name="flow",
    )(velocity, push, warmth)


def gather_kernel(target, heat, out, other):
    out[...] = jnp.zeros_like(out)
    other[...] = jnp.zeros_like(other)
    depth = heat.shape[0]

    def cell(i, c):
        for m in range(depth):
            into = out if m % 2 == 0 else other
            row = pl.ds(target[i * depth + m], 1)
            into[row] = into[row] + heat[m, pl.ds(i, 1)]
        return c

    lax.fori_loop(0, heat.shape[1], cell, 0, unroll=4)
    step = 256

    def join(i, c):
        here = pl.ds(pl.multiple_of(i * step, step), step)
        out[here] = out[here] + other[here]
        return c

    lax.fori_loop(0, out.shape[0] // step, join, 0)


def slab_heat(target, heat, lines):
    return pl.pallas_call(
        gather_kernel,
        out_shape=jax.ShapeDtypeStruct((lines, 128), F32),
        in_specs=[pl.BlockSpec(memory_space=pltpu.SMEM), VM],
        out_specs=VM,
        scratch_shapes=[pltpu.VMEM((lines, 128), F32)],
        compiler_params=pltpu.CompilerParams(vmem_limit_bytes=24 * 2**20),
        name="slab_heat",
    )(target, heat)


def real_basis(length):
    cells = np.arange(length, dtype=np.float64)
    rows = [np.full(length, 1.0 / math.sqrt(length)), (-1.0) ** cells / math.sqrt(length)]
    waves = [0, length // 2]
    for k in range(1, length // 2):
        angle = 2.0 * math.pi * k * cells / length
        rows.append(np.cos(angle) * math.sqrt(2.0 / length))
        rows.append(np.sin(angle) * math.sqrt(2.0 / length))
        waves += [k, k]
    waves = np.array(waves)
    symbol = np.sin(2.0 * math.pi * (waves % (length // 2)) / length) ** 2
    return np.stack(rows), symbol


def split_table(table):
    high = table.astype(np.float32).astype(ml_dtypes.bfloat16)
    low = (table - high.astype(np.float64)).astype(np.float32).astype(ml_dtypes.bfloat16)
    return [high, low]


def pressure_tables(n_y, n_z, n_narrow):
    basis_z, symbol_z = real_basis(n_z)
    basis_y, symbol_y = real_basis(n_y)
    forward = basis_z.T
    tables = []
    for table in (forward, forward.T, basis_y, basis_y.T):
        tables += split_table(np.ascontiguousarray(table))
    s_y = np.broadcast_to(symbol_y[:, None], (n_y, 128)).astype(np.float32)
    s_z = np.tile(symbol_z.reshape(n_narrow, 1, 64), (1, 8, 2)).astype(np.float32)
    return tables + [s_y, s_z]


def split_value(x):
    high = x.astype(BF16)
    return high, (x - high.astype(F32)).astype(BF16)


def dot_left(x, high, low):
    x_high, x_low = split_value(x)
    dot = functools.partial(jnp.dot, preferred_element_type=F32)
    return dot(x_high, high) + (dot(x_high, low) + dot(x_low, high))


def dot_right(high, low, x):
    x_high, x_low = split_value(x)
    dot = functools.partial(jnp.dot, preferred_element_type=F32)
    return dot(high, x_high) + (dot(low, x_high) + dot(high, x_low))


def pressure_kernel(
    n_wide, n_narrow,
    div, slab, substrate, spread, *rest,
):
    table_refs, rest = rest[:8], rest[8:]
    s_y, s_z, press, y_halo, tp, cp = rest[:6]
    tables, rest = rest[6:14], rest[14:]
    (
        zsend, rbuf, ubuf, vsend, zrecv, rtab, halves_, mom, mrecv, absend, ab, xrecv, yrecv, ysend,
        relay_in, relay_out, first_in, first_sum, second_in, part_xr,
        nf_send, nf_recv, nb_send, nb_recv, wf_send, wf_recv, wb_send, wb_recv, h_send, h_recv,
        f_send, f_recv, q_send, q_recv, p_send, p_recv, table_sem,
    ) = rest
    fz_h, fz_l, iz_h, iz_l, cy_h, cy_l, iy_h, iy_l = tables
    loads = [
        pltpu.make_async_copy(table_refs[i], tables[i], table_sem.at[i]) for i in range(8)
    ]

    def loaded(*which):
        for i in which:
            loads[i].wait()

    for i in (0, 1, 4, 5, 6, 7, 2, 3):
        loads[i].start()
    w = lax.axis_index("wide")
    n = lax.axis_index("narrow")
    xps, _, rows, n_z = div.shape
    n_y = s_y.shape[0]
    per = xps // 2
    chunk_rows = n_y // n_wide

    def across(k):
        return lax.rem(n + k, n_narrow)

    def along(k):
        return lax.rem(w + k, n_wide)

    side = math.isqrt(n_wide)
    half = slab.shape[2] // 2
    own = (w // side, lax.rem(w, side))

    def peer(way, k):
        to = lax.rem(own[way] + k, side)
        return (to, to * side + own[1] if way == 0 else own[0] * side + to)

    quarter = half // 2

    def chunk_rows_of(way, to, part, start=0, size=None):
        at = pl.ds(way * half + part * quarter + start, quarter if size is None else size)
        return slab.at[to, :, at] if way == 0 else slab.at[:, to, at]

    def hop(way, direction, source, target, slot):
        _, device = peer(way, 1 if direction == 0 else side - 1)
        return pltpu.make_async_remote_copy(
            src_ref=source, dst_ref=target,
            send_sem=f_send.at[way, direction, slot], recv_sem=f_recv.at[way, direction, slot],
            device_id=(device, n), device_id_type=MESH,
        )

    def next_to(way, direction):
        return peer(way, 1 if direction == 0 else side - 1)[0]

    def far_hop(way, direction):
        source = chunk_rows_of(way, peer(way, 2)[0], direction)
        return hop(way, direction, source, relay_in.at[way, direction], 0)

    def near_hop(way, direction):
        source = chunk_rows_of(way, next_to(way, direction), 1 - direction)
        target = first_in.at[way, direction, :, pl.ds((1 - direction) * quarter, quarter)]
        return hop(way, direction, source, target, 1)

    def joint_hop(way, direction):
        target = first_in.at[way, direction, :, pl.ds(direction * quarter, quarter)]
        return hop(way, direction, relay_out.at[way, direction], target, 2)

    hops = [(way, direction) for way in (0, 1) for direction in (0, 1)]
    step = 32

    def relay():
        for hop_ in hops:
            far_hop(*hop_).wait_recv()
        per_slab = quarter // step

        def add(i, c):
            at = i // per_slab
            start = pl.multiple_of(lax.rem(i, per_slab) * step, step)
            here = pl.ds(start, step)
            for way, direction in hops:
                to = next_to(way, direction)
                mine = pl.ds(
                    pl.multiple_of(way * half + direction * quarter + start, step), step
                )
                own_part = slab[to, at, mine] if way == 0 else slab[at, to, mine]
                relay_out[way, direction, at, here] = relay_in[way, direction, at, here] + own_part
            return c

        lax.fori_loop(0, side * per_slab, add, 0)
        for hop_ in hops:
            joint_hop(*hop_).start()

    def second_copy(way, k):
        to, device = peer(1 - way, k)
        return pltpu.make_async_remote_copy(
            src_ref=first_sum.at[way, to], dst_ref=second_in.at[way, k],
            send_sem=q_send.at[way, k], recv_sem=q_recv.at[way, k],
            device_id=(device, n), device_id_type=MESH,
        )

    halves = [(way, k) for way in (0, 1) for k in range(1, side)]

    def first_total():
        for hop_ in hops:
            near_hop(*hop_).wait_recv()
            joint_hop(*hop_).wait_recv()
        per_slab = half // step

        def add(i, c):
            at = i // per_slab
            start = pl.multiple_of(lax.rem(i, per_slab) * step, step)
            here = pl.ds(start, step)
            for way in (0, 1):
                mine = pl.ds(pl.multiple_of(way * half + start, step), step)
                total = slab[own[0], at, mine] if way == 0 else slab[at, own[1], mine]
                first_sum[way, at, here] = (
                    total + first_in[way, 0, at, here] + first_in[way, 1, at, here]
                )
            return c

        lax.fori_loop(0, side * per_slab, add, 0)
        for way, k in halves:
            second_copy(way, k).start()

    planes = substrate.shape[0]
    part_rows = substrate.shape[1]
    inside = pl.ds(PAD, part_rows)
    last_w, last_n = n_wide - 1, n_narrow - 1
    wide_near = (lax.rem(w + last_w, n_wide), lax.rem(w + 1, n_wide))
    narrow_near = (lax.rem(n + last_n, n_narrow), lax.rem(n + 1, n_narrow))

    def part_x(field, e, side_):
        start = planes if side_ else DEEP
        return pltpu.make_async_remote_copy(
            src_ref=field.at[pl.ds(start, DEEP), inside], dst_ref=part_xr.at[e, 1 - side_],
            send_sem=p_send.at[e, side_], recv_sem=p_recv.at[e, 1 - side_],
            device_id=(wide_near[side_], n), device_id_type=MESH,
        )

    def part_y(field, e, side_):
        start = part_rows if side_ else PAD
        land = 0 if side_ else PAD + part_rows
        return pltpu.make_async_remote_copy(
            src_ref=field.at[:, pl.ds(start, PAD)], dst_ref=field.at[:, pl.ds(land, PAD)],
            send_sem=p_send.at[e, 2 + side_], recv_sem=p_recv.at[e, 3 - side_],
            device_id=(w, narrow_near[side_]), device_id_type=MESH,
        )

    def part_x_start(field, e):
        for i in (0, 1):
            part_x(field, e, i).start()

    def part_x_end(field, e):
        for i in (0, 1):
            part_x(field, e, i).wait_recv()
        field[0:DEEP, PAD:PAD + part_rows] = jnp.where(w == 0, 0.0, part_xr[e, 0])
        field[planes + DEEP:, PAD:PAD + part_rows] = jnp.where(w == last_w, 0.0, part_xr[e, 1])
        for i in (0, 1):
            part_y(field, e, i).start()

    def part_y_end(field, e):
        for i in (0, 1):
            part_y(field, e, i).wait_recv()

        @pl.when(n == 0)
        def _():
            field[:, 0:PAD] = jnp.zeros_like(field[:, 0:PAD])

        @pl.when(n == last_n)
        def _():
            field[:, PAD + part_rows:] = jnp.zeros_like(field[:, PAD + part_rows:])

        for i in (0, 1):
            part_x(field, e, i).wait_send()
            part_y(field, e, i).wait_send()

    def part_start():
        for way, k in halves:
            second_copy(way, k).wait_recv()
        per_half = planes // 2
        for way in (0, 1):
            mine = own[1 - way]
            for i in range(per_half):
                here = slice(i * part_rows, (i + 1) * part_rows)
                total = first_sum[way, mine, here]
                for k in range(1, side):
                    total = total + second_in[way, k, here]
                x = way * per_half + i
                tp[DEEP + x, PAD:PAD + part_rows] = substrate[x] + dissipation_factor * total
        part_x_start(tp, 0)

    barrier = pltpu.get_barrier_semaphore()

    def greet_n(k, c):
        pl.semaphore_signal(barrier, inc=1, device_id=(w, across(k)), device_id_type=MESH)
        return c

    def greet_w(k, c):
        pl.semaphore_signal(barrier, inc=1, device_id=(along(k), n), device_id_type=MESH)
        return c

    lax.fori_loop(1, n_narrow, greet_n, 0)
    lax.fori_loop(1, n_wide, greet_w, 0)

    lane = lax.broadcasted_iota(jnp.int32, (per * rows, 128), 1)
    low_half = lane < 64
    odd = lax.rem(n, 2)
    block = 16

    def later_half(count):
        lanes = lax.broadcasted_iota(jnp.int32, (count, 128), 1)
        return jnp.where(lanes < 64, odd, 1 - odd) == 1

    def swap(x):
        return pltpu.roll(x, 64, 1)

    def power(x, exponent):
        for _ in range(int(math.log2(exponent))):
            x = x * x
        return x

    def forward_copy(g, k):
        to = across(k)
        return pltpu.make_async_remote_copy(
            src_ref=zsend.at[to, pl.ds(g * per, per)],
            dst_ref=rbuf.at[pl.ds(g * per, per), pl.ds(pl.multiple_of(n * rows, rows), rows)],
            send_sem=nf_send.at[g, k],
            recv_sem=nf_recv.at[g, k],
            device_id=(w, to),
            device_id_type=MESH,
        )

    def forward_arrival(g, k):
        source = across(n_narrow - k)
        here = rbuf.at[pl.ds(g * per, per), pl.ds(pl.multiple_of(source * rows, rows), rows)]
        return pltpu.make_async_remote_copy(
            src_ref=here, dst_ref=here, send_sem=nf_send.at[g, k], recv_sem=nf_recv.at[g, k],
            device_id=(w, source), device_id_type=MESH,
        )

    loaded(0, 1)
    for g in range(GROUPS):
        lines = div[:, g].reshape(xps * rows, n_z)
        lines = dot_left(lines, fz_h[...], fz_l[...])
        for m in range(n_z // 128):
            e = lines[:per * rows, 128 * m:128 * (m + 1)]
            o = swap(lines[per * rows:, 128 * m:128 * (m + 1)])
            first = jnp.where(low_half, e, o)
            second = jnp.where(low_half, o, e)
            zsend[2 * m, g * per:(g + 1) * per] = first.reshape(per, rows, 128)
            zsend[2 * m + 1, g * per:(g + 1) * per] = second.reshape(per, rows, 128)
        if g == 0:
            pl.semaphore_wait(barrier, n_narrow - 1 + n_wide - 1)

        def launch(k, c):
            forward_copy(g, k).start()
            return c

        lax.fori_loop(1, n_narrow, launch, 0)
        if g == 0:
            for hop_ in hops:
                far_hop(*hop_).start()
            cp[DEEP:DEEP + planes, PAD:PAD + part_rows] = spread[...]
            part_x_start(cp, 1)

    for hop_ in hops:
        near_hop(*hop_).start()
    s = s_y[...] + s_z[n][0:1, :] + penalty
    root = jnp.sqrt(s * (1.0 + s))
    rtab[0] = 1.0 / (1.0 + 2.0 * s + 2.0 * root)
    rtab[1] = -1.0 / root

    def chunk(index):
        return pl.ds(pl.multiple_of(index * chunk_rows, chunk_rows), chunk_rows)

    def out_copy(g, k):
        to = along(k)
        return pltpu.make_async_remote_copy(
            src_ref=mom.at[g, chunk(to)], dst_ref=mrecv.at[g, w],
            send_sem=wf_send.at[g, k], recv_sem=wf_recv.at[g, k],
            device_id=(to, n), device_id_type=MESH,
        )

    def out_arrival(g, k):
        here = mrecv.at[g, along(n_wide - k)]
        return pltpu.make_async_remote_copy(
            src_ref=here, dst_ref=here, send_sem=wf_send.at[g, k], recv_sem=wf_recv.at[g, k],
            device_id=(along(n_wide - k), n), device_id_type=MESH,
        )

    def back_copy(g, k):
        to = along(k)
        return pltpu.make_async_remote_copy(
            src_ref=absend.at[g, to], dst_ref=ab.at[g, chunk(w)],
            send_sem=wb_send.at[g, k], recv_sem=wb_recv.at[g, k],
            device_id=(to, n), device_id_type=MESH,
        )

    def back_arrival(g, k):
        here = ab.at[g, chunk(along(n_wide - k))]
        return pltpu.make_async_remote_copy(
            src_ref=here, dst_ref=here, send_sem=wb_send.at[g, k], recv_sem=wb_recv.at[g, k],
            device_id=(along(n_wide - k), n), device_id_type=MESH,
        )

    def each(count, action):
        def body(k, c):
            action(k)
            return c

        lax.fori_loop(1, count, body, 0)

    for g in range(GROUPS):
        span = slice(g * per, (g + 1) * per)
        rbuf[span, pl.ds(pl.multiple_of(n * rows, rows), rows)] = zsend[n, span]
        if g == 0:
            part_x_end(cp, 1)
            loaded(4, 5)
        each(n_narrow, lambda k: forward_arrival(g, k).wait_recv())
        lines = jnp.concatenate([rbuf[i] for i in range(g * per, (g + 1) * per)], axis=1)
        lines = dot_right(cy_h[...], cy_l[...], lines)
        for i in range(per):
            ubuf[g * per + i] = lines[:, 128 * i:128 * (i + 1)]

        def moments(i, c):
            here = pl.ds(pl.multiple_of(i * block, block), block)
            r = rtab[0, here]
            f = ubuf[g * per, here]
            b = ubuf[g * per + per - 1, here]
            for k in range(1, per):
                f = f * r + ubuf[g * per + k, here]
                b = b * r + ubuf[g * per + per - 1 - k, here]
            halves_[g, 0, here] = f
            halves_[g, 1, here] = b
            rp = power(r, per)
            mom[g, here] = jnp.where(later_half(block), f + rp * swap(f), b + rp * swap(b))
            return c

        lax.fori_loop(0, n_y // block, moments, 0)
        each(n_wide, lambda k: out_copy(g, k).start())
        mrecv[g, w] = mom[g, chunk(w)]
        if g == 0:
            relay()

    q = power(rtab[0, chunk(w)], xps)
    closing = 1.0 / (1.0 - power(q, n_wide))
    for g in range(GROUPS):
        each(n_wide, lambda k: out_arrival(g, k).wait_recv())
        f = mrecv[g, 0]
        b = mrecv[g, n_wide - 1]
        for j in range(1, n_wide):
            f = f * q + mrecv[g, j]
            b = b * q + mrecv[g, n_wide - 1 - j]
        f = f * closing
        b = b * closing
        ahead, behind = [], []
        for j in range(n_wide):
            ahead.append(f)
            behind.append(b)
            f = f * q + mrecv[g, j]
            b = b * q + mrecv[g, n_wide - 1 - j]
        for j in range(n_wide):
            absend[g, j] = jnp.where(later_half(chunk_rows), ahead[j], behind[n_wide - 1 - j])
        each(n_wide, lambda k: back_copy(g, k).start())
        ab[g, chunk(w)] = absend[g, w]

    def backward_copy(g, k):
        to = across(k)
        return pltpu.make_async_remote_copy(
            src_ref=vsend.at[to, pl.ds(g * per, per)],
            dst_ref=zrecv.at[n, pl.ds(g * per, per)],
            send_sem=nb_send.at[g, k],
            recv_sem=nb_recv.at[g, k],
            device_id=(w, to),
            device_id_type=MESH,
        )

    def backward_arrival(g, k):
        source = across(n_narrow - k)
        here = zrecv.at[source, pl.ds(g * per, per)]
        return pltpu.make_async_remote_copy(
            src_ref=here, dst_ref=here, send_sem=nb_send.at[g, k], recv_sem=nb_recv.at[g, k],
            device_id=(w, source), device_id_type=MESH,
        )

    loaded(6, 7)
    for g in range(GROUPS):
        span = slice(g * per, (g + 1) * per)
        each(n_wide, lambda k: back_arrival(g, k).wait_recv())

        def solve(i, c):
            here = pl.ds(pl.multiple_of(i * block, block), block)
            later = later_half(block)
            r = rtab[0, here]
            scale = rtab[1, here]
            rp = power(r, per)
            mixed = ab[g, here]
            other = swap(mixed)
            f = jnp.where(later, mixed, other)
            b = jnp.where(later, other, mixed)
            f = jnp.where(later, rp * f + swap(halves_[g, 0, here]), f)
            b = jnp.where(later, b, rp * b + swap(halves_[g, 1, here]))
            behind = []
            for k in range(per - 1, -1, -1):
                rb = b * r
                behind.append(rb)
                b = rb + ubuf[g * per + k, here]
            for k in range(per):
                f = f * r + ubuf[g * per + k, here]
                ubuf[g * per + k, here] = scale * (f + behind[per - 1 - k])
            return c

        lax.fori_loop(0, n_y // block, solve, 0)
        lines = jnp.concatenate([ubuf[i] for i in range(g * per, (g + 1) * per)], axis=1)
        lines = dot_right(iy_h[...], iy_l[...], lines)
        for to in range(n_narrow):
            for i in range(per):
                vsend[to, g * per + i] = lines[to * rows:(to + 1) * rows, 128 * i:128 * (i + 1)]
        each(n_narrow, lambda k: backward_copy(g, k).start())
        zrecv[n, span] = vsend[n, span]

    first_total()
    part_y_end(cp, 1)
    loaded(2, 3)

    def x_halo(side):
        source = 2 * xps if side else 1
        return pltpu.make_async_remote_copy(
            src_ref=press.at[source], dst_ref=xrecv.at[1 - side],
            send_sem=h_send.at[side], recv_sem=h_recv.at[1 - side],
            device_id=(wide_near[side], n), device_id_type=MESH,
        )

    def y_halo_copy(side):
        return pltpu.make_async_remote_copy(
            src_ref=ysend.at[side], dst_ref=yrecv.at[1 - side],
            send_sem=h_send.at[2 + side], recv_sem=h_recv.at[3 - side],
            device_id=(w, narrow_near[side]), device_id_type=MESH,
        )

    for g in range(GROUPS):
        each(n_narrow, lambda k: backward_arrival(g, k).wait_recv())
        evens, odds = [], []
        for m in range(n_z // 128):
            first = zrecv[2 * m, g * per:(g + 1) * per].reshape(per * rows, 128)
            second = zrecv[2 * m + 1, g * per:(g + 1) * per].reshape(per * rows, 128)
            evens.append(jnp.where(low_half, first, second))
            odds.append(swap(jnp.where(low_half, second, first)))
        lines = jnp.concatenate(
            [jnp.concatenate(evens, axis=1), jnp.concatenate(odds, axis=1)], axis=0
        )
        lines = dot_left(lines, iz_h[...], iz_l[...])
        for i in range(xps):
            plane = lines[i * rows:(i + 1) * rows]
            x = 2 * i + g
            press[x + 1] = plane
            ysend[0, x] = plane[0]
            ysend[1, x] = plane[rows - 1]
        if g == 0:
            x_halo(0).start()
            part_start()
    x_halo(1).start()
    y_halo_copy(0).start()
    y_halo_copy(1).start()
    part_x_end(tp, 0)

    for way, k in halves:
        second_copy(way, k).wait_send()
    for hop_ in hops:
        far_hop(*hop_).wait_send()
        near_hop(*hop_).wait_send()
        joint_hop(*hop_).wait_send()
    for g in range(GROUPS):
        each(n_narrow, lambda k: forward_copy(g, k).wait_send())
        each(n_narrow, lambda k: backward_copy(g, k).wait_send())
        each(n_wide, lambda k: out_copy(g, k).wait_send())
        each(n_wide, lambda k: back_copy(g, k).wait_send())
    for side in (0, 1):
        x_halo(side).wait()
        y_halo_copy(side).wait()
    press[0] = xrecv[0]
    press[2 * xps + 1] = xrecv[1]
    y_halo[...] = yrecv[...]
    part_y_end(tp, 0)


def solve_pressure(divergence, slab, substrate, spread):
    n_wide, n_narrow = lax.axis_size("wide"), lax.axis_size("narrow")
    x_local, rows, n_z = divergence.shape
    n_y = rows * n_narrow
    xps = x_local // 2
    tables = [jnp.asarray(t) for t in pressure_tables(n_y, n_z, n_narrow)]
    dma = pltpu.SemaphoreType.DMA
    field = (xps, n_y, 128)
    turned = (n_narrow, xps, rows, 128)
    chunk_rows = n_y // n_wide
    side = math.isqrt(n_wide)
    planes, part_rows, depth = substrate.shape
    half = planes * part_rows // 2
    part = (planes + 2 * DEEP, part_rows + 2 * PAD, depth)
    any_space = pl.BlockSpec(memory_space=pl.ANY)
    return pl.pallas_call(
        functools.partial(pressure_kernel, n_wide, n_narrow),
        out_shape=[
            jax.ShapeDtypeStruct((x_local + 2, rows, n_z), F32),
            jax.ShapeDtypeStruct((2, x_local, n_z), F32),
            jax.ShapeDtypeStruct(part, F32),
            jax.ShapeDtypeStruct(part, F32),
        ],
        in_specs=[VM, VM, VM, VM] + [any_space] * 8 + [VM, VM],
        out_specs=[VM] * 4,
        scratch_shapes=[pltpu.VMEM(t.shape, BF16) for t in tables[:8]]
        + [
            pltpu.VMEM(turned, F32),
            pltpu.VMEM(field, F32),
            pltpu.VMEM(field, F32),
            pltpu.VMEM(turned, F32),
            pltpu.VMEM(turned, F32),
            pltpu.VMEM((2, n_y, 128), F32),
            pltpu.VMEM((GROUPS, 2, n_y, 128), F32),
            pltpu.VMEM((GROUPS, n_y, 128), F32),
            pltpu.VMEM((GROUPS, n_wide, chunk_rows, 128), F32),
            pltpu.VMEM((GROUPS, n_wide, chunk_rows, 128), F32),
            pltpu.VMEM((GROUPS, n_y, 128), F32),
            pltpu.VMEM((2, rows, n_z), F32),
            pltpu.VMEM((2, x_local, n_z), F32),
            pltpu.VMEM((2, x_local, n_z), F32),
            pltpu.VMEM((2, 2, side, half // 2, depth), F32),
            pltpu.VMEM((2, 2, side, half // 2, depth), F32),
            pltpu.VMEM((2, 2, side, half, depth), F32),
            pltpu.VMEM((2, side, half, depth), F32),
            pltpu.VMEM((2, side, half, depth), F32),
            pltpu.VMEM((2, 2, DEEP, part_rows, depth), F32),
            dma((GROUPS, n_narrow)),
            dma((GROUPS, n_narrow)),
            dma((GROUPS, n_narrow)),
            dma((GROUPS, n_narrow)),
            dma((GROUPS, n_wide)),
            dma((GROUPS, n_wide)),
            dma((GROUPS, n_wide)),
            dma((GROUPS, n_wide)),
            dma((4,)),
            dma((4,)),
            dma((2, 2, 3)),
            dma((2, 2, 3)),
            dma((2, side)),
            dma((2, side)),
            dma((2, 4)),
            dma((2, 4)),
            dma((8,)),
        ],
        compiler_params=pltpu.CompilerParams(
            collective_id=1, has_side_effects=True, vmem_limit_bytes=32 * 2**20
        ),
        name="pressure",
    )(
        divergence.reshape(xps, 2, rows, n_z),
        slab.reshape(side, side, 2 * half, depth),
        substrate, spread, *tables,
    )


def conduct(step, span, source, coefficient, target):
    planes, rows, depth = coefficient.shape
    lane = lax.broadcasted_iota(jnp.int32, (rows, depth), 1)

    def plane(x, c):
        p = source[x]
        around = source[x + 1] + source[x - 1] + pltpu.roll(p, 1, 0) + pltpu.roll(p, rows - 1, 0)
        around += jnp.where(lane == 0, 0.0, pltpu.roll(p, 1, 1))
        around += jnp.where(lane == depth - 1, 0.0, pltpu.roll(p, depth - 1, 1))
        new = p + coefficient[x] * (around - 6.0 * p)
        if step == STEPS - 1:
            target[x - DEEP] = new[PAD:rows - PAD]
        else:
            target[x] = new
        return c

    lax.fori_loop(*span, plane, 0, unroll=2)


def y_step(plane, before, after, ahead):
    rows = plane.shape[0]
    row = lax.broadcasted_iota(jnp.int32, plane.shape, 0)
    if ahead:
        return jnp.where(row == rows - 1, after, pltpu.roll(plane, rows - 1, 0))
    return jnp.where(row == 0, before, pltpu.roll(plane, 1, 0))


def project_kernel(lead, trail, y_halo, tp, cp, current, out, part, tq, tr):
    step = pl.program_id(0)
    planes, n_z = current.shape[1], current.shape[3]
    total = tp.shape[0]
    for i in range(2 * STEPS):

        @pl.when(step == i)
        def _():
            first, last = i // 2 + 1, total - i // 2 - 1
            span = (first, total // 2) if i % 2 == 0 else (total // 2, last)
            conduct(i // 2, span, (tp, tq, tr)[i // 2], cp, (tq, tr, part)[i // 2])

    block = [lead[0], lead[1], trail[0], trail[1]]
    for i in range(planes):
        x = step * planes + i
        p = block[i + 1]
        before = y_halo[0, pl.ds(x, 1)]
        after = y_halo[1, pl.ds(x, 1)]
        out[0, i] = current[0, i] - (block[i + 2] - block[i]) * 0.5
        out[1, i] = current[1, i] - 0.5 * (
            y_step(p, before, after, True) - y_step(p, before, after, False)
        )
        out[2, i] = current[2, i] - 0.5 * (pltpu.roll(p, n_z - 1, 1) - pltpu.roll(p, 1, 1))


def project(current, press, y_halo, tp, cp):
    _, x_local, rows, n_z = current.shape
    planes = 2
    spec = pl.BlockSpec((3, planes, rows, n_z), lambda i: (0, i, 0, 0))
    part = (tp.shape[0] - 2 * DEEP, tp.shape[1] - 2 * PAD, tp.shape[2])
    return pl.pallas_call(
        project_kernel,
        grid=(x_local // planes,),
        out_shape=[jax.ShapeDtypeStruct(current.shape, F32), jax.ShapeDtypeStruct(part, F32)],
        in_specs=[
            pl.BlockSpec((planes, rows, n_z), lambda i: (i, 0, 0)),
            pl.BlockSpec((planes, rows, n_z), lambda i: (i + 1, 0, 0)),
            VM, VM, VM, spec,
        ],
        out_specs=[spec, pl.BlockSpec(part, lambda i: (0, 0, 0))],
        scratch_shapes=[pltpu.VMEM(tp.shape, F32), pltpu.VMEM(tp.shape, F32)],
        compiler_params=pltpu.CompilerParams(vmem_limit_bytes=20 * 2**20),
        name="projection",
    )(press, press, y_halo, tp, cp, current)


def per_device(
    material_flow_vector,
    tool_push_density,
    tool_warmth_excess,
    substrate_warmth_excess,
    spread_coefficient,
    source_owner_sheet,
    source_part_line,
):
    current, divergence, heat = flow(material_flow_vector, tool_push_density, tool_warmth_excess)
    slab_ids = source_owner_sheet[:, 0]
    slab_count = lax.axis_size("wide")
    component_lines = substrate_warmth_excess.shape[0] * substrate_warmth_excess.shape[1]
    target = slab_ids * component_lines + source_part_line
    partial_value = slab_heat(target, heat, slab_count * component_lines)
    solved = solve_pressure(
        divergence, partial_value, substrate_warmth_excess, spread_coefficient
    )
    return tuple(project(current, *solved))


def solution(mesh):
    return jax.shard_map(
        per_device,
        mesh=mesh,
        in_specs=(
            P(None, "wide", "narrow", None),
            P(None, "wide", "narrow", None),
            P("wide", "narrow", None),
            P("wide", "narrow", None),
            P("wide", "narrow", None),
            P(("wide", "narrow"), None),
            P(("wide", "narrow")),
        ),
        out_specs=(P(None, "wide", "narrow", None), P("wide", "narrow", None)),
        check_vma=False,
    )
```

```python
import functools
import math

import jax
import jax.numpy as jnp
import ml_dtypes
import numpy as np
from jax import lax
from jax.experimental import pallas as pl
from jax.experimental.pallas import tpu as pltpu
from jax.sharding import PartitionSpec as P

STEPS = 3
MESH = pl.DeviceIdType.MESH
F32 = jnp.float32
BF16 = jnp.bfloat16
VM = pl.BlockSpec(memory_space=pltpu.VMEM)

time_step = 0.15
rate_base = 0.5
zener_energy = 4.0
stress_exponent = 5.0
penalty = 0.001
dissipation_factor = 0.1
GROUPS = 2
DEEP = STEPS


PAD = 8
STRIP = 8


def flow_kernel(
    n_wide, n_narrow,
    vel_in, push_in, warmth_in,
    mom, div, heat,
    velp, provp, mup0, mup1, lz, push,
    vel_ys, vel_yr, mu_ys0, mu_yr0, prov_ys, prov_yr, mu_ys1, mu_yr1, mom_ys, mom_yr, mom_xr,
    load_sem, h_send, h_recv,
):
    w = lax.axis_index("wide")
    n = lax.axis_index("narrow")
    _, planes, rows, n_z = vel_in.shape
    strips = rows // STRIP
    wide_to = (lax.rem(w + n_wide - 1, n_wide), lax.rem(w + 1, n_wide))
    narrow_to = (lax.rem(n + n_narrow - 1, n_narrow), lax.rem(n + 1, n_narrow))
    body = pl.ds(PAD, rows)

    barrier = pltpu.get_barrier_semaphore()
    for side in (0, 1):
        pl.semaphore_signal(barrier, inc=1, device_id=(wide_to[side], n), device_id_type=MESH)
        pl.semaphore_signal(barrier, inc=1, device_id=(w, narrow_to[side]), device_id_type=MESH)

    loads = [
        pltpu.make_async_copy(vel_in, velp.at[:, pl.ds(1, planes), body], load_sem.at[0]),
        pltpu.make_async_copy(push_in, push, load_sem.at[1]),
    ]
    for load in loads:
        load.start()

    def wide_copy(e, side, source, target):
        return pltpu.make_async_remote_copy(
            src_ref=source, dst_ref=target,
            send_sem=h_send.at[e, side], recv_sem=h_recv.at[e, 1 - side],
            device_id=(wide_to[side], n), device_id_type=MESH,
        )

    def narrow_copy(e, side, sends, lands):
        return pltpu.make_async_remote_copy(
            src_ref=sends.at[side], dst_ref=lands.at[1 - side],
            send_sem=h_send.at[e, 2 + side], recv_sem=h_recv.at[e, 3 - side],
            device_id=(w, narrow_to[side]), device_id_type=MESH,
        )

    def x_pair(e, field, lead=()):
        return [
            wide_copy(e, 0, field.at[lead + (1, body)], field.at[lead + (planes + 1, body)]),
            wide_copy(e, 1, field.at[lead + (planes, body)], field.at[lead + (0, body)]),
        ]

    def y_pair(e, sends, lands):
        return [narrow_copy(e, side, sends, lands) for side in (0, 1)]

    def all_x(action, first=0, last=None, unroll=1):
        def step(x, c):
            action(x)
            return c

        lax.fori_loop(first, planes if last is None else last, step, 0, unroll=unroll)

    def y_fill(field, lands, comps):
        def fill(x):
            here = pl.ds(x, 1)
            if comps is None:
                field[x + 1, PAD - 1:PAD] = lands[0, here]
                field[x + 1, PAD + rows:PAD + rows + 1] = lands[1, here]
                return
            for i, c in enumerate(comps):
                field[c, x + 1, PAD - 1:PAD] = lands[0, i, here]
                field[c, x + 1, PAD + rows:PAD + rows + 1] = lands[1, i, here]

        all_x(fill)

    def z_ahead(a):
        return pltpu.roll(a, n_z - 1, 1)

    def z_behind(a):
        return pltpu.roll(a, 1, 1)

    loads[0].wait()

    def vel_rows(x):
        for c in range(3):
            vel_ys[0, c, pl.ds(x, 1)] = velp[c, x + 1, PAD:PAD + 1]
            vel_ys[1, c, pl.ds(x, 1)] = velp[c, x + 1, PAD + rows - 1:PAD + rows]

    all_x(vel_rows)
    pl.semaphore_wait(barrier, 4)
    every = slice(None)
    vel_x = x_pair(0, velp, (every,))
    vel_y = y_pair(0, vel_ys, vel_yr)
    for copy in vel_x + vel_y:
        copy.start()

    def zener_log(x):
        lz[x] = (zener_energy / stress_exponent) * (1.0 / warmth_in[x] - 1.0)

    all_x(zener_log)
    loads[1].wait()

    def excess(src, x, r):
        here = slice(PAD + STRIP * r, PAD + STRIP * (r + 1))
        up = slice(PAD + STRIP * r + 1, PAD + STRIP * (r + 1) + 1)
        down = slice(PAD + STRIP * r - 1, PAD + STRIP * (r + 1) - 1)
        dx = [src[c, x + 2, here] - src[c, x, here] for c in range(3)]
        dy = [src[c, x + 1, up] - src[c, x + 1, down] for c in range(3)]
        mid = [src[c, x + 1, here] for c in range(3)]
        dz = [z_ahead(m) - z_behind(m) for m in mid]
        xy, xz, yz = dy[0] + dx[1], dz[0] + dx[2], dz[1] + dy[2]
        diagonal = dx[0] * dx[0] + dy[1] * dy[1] + dz[2] * dz[2]
        return 0.5 * diagonal + 0.25 * (xy * xy + xz * xz + yz * yz)

    def mu_plane(src, mup, ys, with_heat):
        def plane(x, which):
            for r in which:
                part = slice(STRIP * r, STRIP * (r + 1))
                extra = excess(src, x, r)
                rate_sq = extra + rate_base**2
                v = jnp.exp((0.5 / stress_exponent) * jnp.log(rate_sq) + lz[x, part])
                mu = jnp.log(v + jnp.sqrt(v * v + 1.0)) * lax.rsqrt(rate_sq) * (1.0 / 3.0)
                mup[x + 1, PAD + STRIP * r:PAD + STRIP * (r + 1)] = mu
                if r == 0:
                    ys[0, pl.ds(x, 1)] = mu[0:1]
                if r == strips - 1:
                    ys[1, pl.ds(x, 1)] = mu[STRIP - 1:]
                if with_heat:
                    h = mu * extra
                    to = pl.ds(pl.multiple_of(x * rows + STRIP * r, STRIP), STRIP)
                    for m in range(n_z // 128):
                        heat[m, to] = h[:, 128 * m:128 * (m + 1)]

        return plane

    def advance_plane(mup, final):
        def plane(x, which):
            for r in which:
                part = slice(STRIP * r, STRIP * (r + 1))
                here = slice(PAD + STRIP * r, PAD + STRIP * (r + 1))
                up = slice(PAD + STRIP * r + 1, PAD + STRIP * (r + 1) + 1)
                down = slice(PAD + STRIP * r - 1, PAD + STRIP * (r + 1) - 1)
                m = mup[x + 1, here]
                m_xp = m + mup[x + 2, here]
                m_xm = m + mup[x, here]
                m_yp = m + mup[x + 1, up]
                m_ym = m + mup[x + 1, down]
                m_z = m + z_ahead(m)
                for c in range(3):
                    u = velp[c, x + 1, here]
                    flux = m_z * (z_ahead(u) - u)
                    total = flux - z_behind(flux)
                    total += m_xp * (velp[c, x + 2, here] - u) - m_xm * (u - velp[c, x, here])
                    total += m_yp * (velp[c, x + 1, up] - u) - m_ym * (u - velp[c, x + 1, down])
                    new = u + (0.5 * time_step) * total + time_step * push[c, x, part]
                    provp[c, x + 1, here] = new
                    if final:
                        mom[c, x, part] = new
                        if c == 1:
                            if r == 0:
                                mom_ys[0, pl.ds(x, 1)] = new[0:1]
                            if r == strips - 1:
                                mom_ys[1, pl.ds(x, 1)] = new[STRIP - 1:]
                    else:
                        if r == 0:
                            prov_ys[0, c, pl.ds(x, 1)] = new[0:1]
                        if r == strips - 1:
                            prov_ys[1, c, pl.ds(x, 1)] = new[STRIP - 1:]

        return plane

    def stage(action, arriving_x, arriving_y, fill, fill_x=None):
        all_x(lambda x: action(x, range(1, strips - 1)), 1, planes - 1, 2)
        for copy in arriving_y:
            copy.wait_recv()
        fill()
        all_x(lambda x: action(x, (0, strips - 1)), 1, planes - 1, 2)
        for copy in arriving_x:
            copy.wait_recv()
        if fill_x is not None:
            fill_x()
        all_x(lambda i: action(i * (planes - 1), range(strips)), 0, 2)

    stage(mu_plane(velp, mup0, mu_ys0, False), vel_x, vel_y,
          lambda: y_fill(velp, vel_yr, (0, 1, 2)))
    mu_x0 = x_pair(1, mup0)
    mu_y0 = y_pair(1, mu_ys0, mu_yr0)
    for copy in mu_x0 + mu_y0:
        copy.start()
    stage(advance_plane(mup0, False), mu_x0, mu_y0, lambda: y_fill(mup0, mu_yr0, None))
    prov_x = x_pair(2, provp, (every,))
    prov_y = y_pair(2, prov_ys, prov_yr)
    for copy in prov_x + prov_y:
        copy.start()
    stage(mu_plane(provp, mup1, mu_ys1, True), prov_x, prov_y,
          lambda: y_fill(provp, prov_yr, (0, 1, 2)))
    mu_x1 = x_pair(3, mup1)
    mu_y1 = y_pair(3, mu_ys1, mu_yr1)
    for copy in mu_x1 + mu_y1:
        copy.start()
    for copy in prov_x + prov_y:
        copy.wait_send()
    stage(advance_plane(mup1, True), mu_x1, mu_y1, lambda: y_fill(mup1, mu_yr1, None))
    mom_x = [
        wide_copy(4, 0, mom.at[0, 0], mom_xr.at[1]),
        wide_copy(4, 1, mom.at[0, planes - 1], mom_xr.at[0]),
    ]
    mom_y = y_pair(4, mom_ys, mom_yr)
    for copy in mom_x + mom_y:
        copy.start()
    for copy in vel_x + vel_y + mu_x0 + mu_y0 + mu_x1 + mu_y1:
        copy.wait_send()

    def fill_rows():
        def fill(x):
            here = pl.ds(x, 1)
            provp[1, x + 1, PAD - 1:PAD] = mom_yr[0, here]
            provp[1, x + 1, PAD + rows:PAD + rows + 1] = mom_yr[1, here]

        all_x(fill)

    def div_plane(x, which):
        for r in which:
            part = slice(STRIP * r, STRIP * (r + 1))
            here = slice(PAD + STRIP * r, PAD + STRIP * (r + 1))
            up = slice(PAD + STRIP * r + 1, PAD + STRIP * (r + 1) + 1)
            down = slice(PAD + STRIP * r - 1, PAD + STRIP * (r + 1) - 1)
            u = provp[2, x + 1, here]
            total = provp[0, x + 2, here] - provp[0, x, here]
            total += provp[1, x + 1, up] - provp[1, x + 1, down]
            div[x, part] = 0.5 * (total + (z_ahead(u) - z_behind(u)))

    def fill_planes():
        provp[0, 0, body] = mom_xr[0]
        provp[0, planes + 1, body] = mom_xr[1]

    stage(div_plane, mom_x, mom_y, fill_rows, fill_planes)
    for copy in mom_x + mom_y:
        copy.wait_send()


def flow(velocity, push, warmth):
    n_wide, n_narrow = lax.axis_size("wide"), lax.axis_size("narrow")
    _, planes, rows, n_z = velocity.shape
    padded = (planes + 2, PAD + rows + PAD, n_z)
    line = (2, planes, n_z)
    lines = (2, 3, planes, n_z)
    any_space = pl.BlockSpec(memory_space=pl.ANY)
    shapes = [(3,) + padded, (3,) + padded, padded, padded, (planes, rows, n_z), velocity.shape]
    shapes += [lines, lines, line, line, lines, lines, line, line, line, line, (2, rows, n_z)]
    dma = pltpu.SemaphoreType.DMA
    return pl.pallas_call(
        functools.partial(flow_kernel, n_wide, n_narrow),
        out_shape=[
            jax.ShapeDtypeStruct(velocity.shape, F32),
            jax.ShapeDtypeStruct((planes, rows, n_z), F32),
            jax.ShapeDtypeStruct((n_z // 128, planes * rows, 128), F32),
        ],
        in_specs=[any_space, any_space, VM],
        out_specs=[VM] * 3,
        scratch_shapes=[pltpu.VMEM(shape, F32) for shape in shapes]
        + [dma((2,)), dma((5, 4)), dma((5, 4))],
        compiler_params=pltpu.CompilerParams(
            collective_id=2, has_side_effects=True, vmem_limit_bytes=48 * 2**20
        ),
        name="flow",
    )(velocity, push, warmth)


def gather_kernel(target, heat, out, other):
    out[...] = jnp.zeros_like(out)
    other[...] = jnp.zeros_like(other)
    depth = heat.shape[0]

    def cell(i, c):
        for m in range(depth):
            into = out if m % 2 == 0 else other
            row = pl.ds(target[i * depth + m], 1)
            into[row] = into[row] + heat[m, pl.ds(i, 1)]
        return c

    lax.fori_loop(0, heat.shape[1], cell, 0, unroll=4)
    step = 256

    def join(i, c):
        here = pl.ds(pl.multiple_of(i * step, step), step)
        out[here] = out[here] + other[here]
        return c

    lax.fori_loop(0, out.shape[0] // step, join, 0)


def slab_heat(target, heat, lines):
    return pl.pallas_call(
        gather_kernel,
        out_shape=jax.ShapeDtypeStruct((lines, 128), F32),
        in_specs=[pl.BlockSpec(memory_space=pltpu.SMEM), VM],
        out_specs=VM,
        scratch_shapes=[pltpu.VMEM((lines, 128), F32)],
        compiler_params=pltpu.CompilerParams(vmem_limit_bytes=24 * 2**20),
        name="slab_heat",
    )(target, heat)


def real_basis(length):
    cells = np.arange(length, dtype=np.float64)
    rows = [np.full(length, 1.0 / math.sqrt(length)), (-1.0) ** cells / math.sqrt(length)]
    waves = [0, length // 2]
    for k in range(1, length // 2):
        angle = 2.0 * math.pi * k * cells / length
        rows.append(np.cos(angle) * math.sqrt(2.0 / length))
        rows.append(np.sin(angle) * math.sqrt(2.0 / length))
        waves += [k, k]
    waves = np.array(waves)
    symbol = np.sin(2.0 * math.pi * (waves % (length // 2)) / length) ** 2
    return np.stack(rows), symbol


def split_table(table):
    high = table.astype(np.float32).astype(ml_dtypes.bfloat16)
    low = (table - high.astype(np.float64)).astype(np.float32).astype(ml_dtypes.bfloat16)
    return [high, low]


def pressure_tables(n_y, n_z, n_narrow):
    basis_z, symbol_z = real_basis(n_z)
    basis_y, symbol_y = real_basis(n_y)
    forward = basis_z.T
    tables = []
    for table in (forward, forward.T, basis_y, basis_y.T):
        tables += split_table(np.ascontiguousarray(table))
    s_y = np.broadcast_to(symbol_y[:, None], (n_y, 128)).astype(np.float32)
    s_z = np.tile(symbol_z.reshape(n_narrow, 1, 64), (1, 8, 2)).astype(np.float32)
    return tables + [s_y, s_z]


def split_value(x):
    high = x.astype(BF16)
    return high, (x - high.astype(F32)).astype(BF16)


def dot_left(x, high, low):
    x_high, x_low = split_value(x)
    dot = functools.partial(jnp.dot, preferred_element_type=F32)
    return dot(x_high, high) + (dot(x_high, low) + dot(x_low, high))


def dot_right(high, low, x):
    x_high, x_low = split_value(x)
    dot = functools.partial(jnp.dot, preferred_element_type=F32)
    return dot(high, x_high) + (dot(low, x_high) + dot(high, x_low))


def pressure_kernel(
    n_wide, n_narrow,
    div, slab, substrate, spread, *rest,
):
    table_refs, rest = rest[:8], rest[8:]
    s_y, s_z, press, y_halo, tp, cp = rest[:6]
    tables, rest = rest[6:14], rest[14:]
    (
        zsend, rbuf, ubuf, vsend, zrecv, rtab, halves_, mom, mrecv, absend, ab, xrecv, yrecv, ysend,
        relay_in, relay_out, first_in, first_sum, second_in, part_xr,
        nf_send, nf_recv, nb_send, nb_recv, wf_send, wf_recv, wb_send, wb_recv, h_send, h_recv,
        f_send, f_recv, q_send, q_recv, p_send, p_recv, table_sem,
    ) = rest
    fz_h, fz_l, iz_h, iz_l, cy_h, cy_l, iy_h, iy_l = tables
    loads = [
        pltpu.make_async_copy(table_refs[i], tables[i], table_sem.at[i]) for i in range(8)
    ]

    def loaded(*which):
        for i in which:
            loads[i].wait()

    for i in (0, 1, 4, 5, 6, 7, 2, 3):
        loads[i].start()
    w = lax.axis_index("wide")
    n = lax.axis_index("narrow")
    xps, _, rows, n_z = div.shape
    n_y = s_y.shape[0]
    per = xps // 2
    chunk_rows = n_y // n_wide

    def across(k):
        return lax.rem(n + k, n_narrow)

    def along(k):
        return lax.rem(w + k, n_wide)

    side = math.isqrt(n_wide)
    half = slab.shape[2] // 2
    own = (w // side, lax.rem(w, side))

    def peer(way, k):
        to = lax.rem(own[way] + k, side)
        return (to, to * side + own[1] if way == 0 else own[0] * side + to)

    quarter = half // 2

    def chunk_rows_of(way, to, part, start=0, size=None):
        at = pl.ds(way * half + part * quarter + start, quarter if size is None else size)
        return slab.at[to, :, at] if way == 0 else slab.at[:, to, at]

    def hop(way, direction, source, target, slot):
        _, device = peer(way, 1 if direction == 0 else side - 1)
        return pltpu.make_async_remote_copy(
            src_ref=source, dst_ref=target,
            send_sem=f_send.at[way, direction, slot], recv_sem=f_recv.at[way, direction, slot],
            device_id=(device, n), device_id_type=MESH,
        )

    def next_to(way, direction):
        return peer(way, 1 if direction == 0 else side - 1)[0]

    def far_hop(way, direction):
        source = chunk_rows_of(way, peer(way, 2)[0], direction)
        return hop(way, direction, source, relay_in.at[way, direction], 0)

    def near_hop(way, direction):
        source = chunk_rows_of(way, next_to(way, direction), 1 - direction)
        target = first_in.at[way, direction, :, pl.ds((1 - direction) * quarter, quarter)]
        return hop(way, direction, source, target, 1)

    def joint_hop(way, direction):
        target = first_in.at[way, direction, :, pl.ds(direction * quarter, quarter)]
        return hop(way, direction, relay_out.at[way, direction], target, 2)

    hops = [(way, direction) for way in (0, 1) for direction in (0, 1)]
    step = 32

    def relay():
        for hop_ in hops:
            far_hop(*hop_).wait_recv()
        per_slab = quarter // step

        def add(i, c):
            at = i // per_slab
            start = pl.multiple_of(lax.rem(i, per_slab) * step, step)
            here = pl.ds(start, step)
            for way, direction in hops:
                to = next_to(way, direction)
                mine = pl.ds(
                    pl.multiple_of(way * half + direction * quarter + start, step), step
                )
                own_part = slab[to, at, mine] if way == 0 else slab[at, to, mine]
                relay_out[way, direction, at, here] = relay_in[way, direction, at, here] + own_part
            return c

        lax.fori_loop(0, side * per_slab, add, 0)
        for hop_ in hops:
            joint_hop(*hop_).start()

    def second_copy(way, k):
        to, device = peer(1 - way, k)
        return pltpu.make_async_remote_copy(
            src_ref=first_sum.at[way, to], dst_ref=second_in.at[way, k],
            send_sem=q_send.at[way, k], recv_sem=q_recv.at[way, k],
            device_id=(device, n), device_id_type=MESH,
        )

    halves = [(way, k) for way in (0, 1) for k in range(1, side)]

    def first_total():
        for hop_ in hops:
            near_hop(*hop_).wait_recv()
            joint_hop(*hop_).wait_recv()
        per_slab = half // step

        def add(i, c):
            at = i // per_slab
            start = pl.multiple_of(lax.rem(i, per_slab) * step, step)
            here = pl.ds(start, step)
            for way in (0, 1):
                mine = pl.ds(pl.multiple_of(way * half + start, step), step)
                total = slab[own[0], at, mine] if way == 0 else slab[at, own[1], mine]
                first_sum[way, at, here] = (
                    total + first_in[way, 0, at, here] + first_in[way, 1, at, here]
                )
            return c

        lax.fori_loop(0, side * per_slab, add, 0)
        for way, k in halves:
            second_copy(way, k).start()

    planes = substrate.shape[0]
    part_rows = substrate.shape[1]
    inside = pl.ds(PAD, part_rows)
    last_w, last_n = n_wide - 1, n_narrow - 1
    wide_near = (lax.rem(w + last_w, n_wide), lax.rem(w + 1, n_wide))
    narrow_near = (lax.rem(n + last_n, n_narrow), lax.rem(n + 1, n_narrow))

    def part_x(field, e, side_):
        start = planes if side_ else DEEP
        return pltpu.make_async_remote_copy(
            src_ref=field.at[pl.ds(start, DEEP), inside], dst_ref=part_xr.at[e, 1 - side_],
            send_sem=p_send.at[e, side_], recv_sem=p_recv.at[e, 1 - side_],
            device_id=(wide_near[side_], n), device_id_type=MESH,
        )

    def part_y(field, e, side_):
        start = part_rows if side_ else PAD
        land = 0 if side_ else PAD + part_rows
        return pltpu.make_async_remote_copy(
            src_ref=field.at[:, pl.ds(start, PAD)], dst_ref=field.at[:, pl.ds(land, PAD)],
            send_sem=p_send.at[e, 2 + side_], recv_sem=p_recv.at[e, 3 - side_],
            device_id=(w, narrow_near[side_]), device_id_type=MESH,
        )

    def part_x_start(field, e):
        for i in (0, 1):
            part_x(field, e, i).start()

    def part_x_end(field, e):
        for i in (0, 1):
            part_x(field, e, i).wait_recv()
        field[0:DEEP, PAD:PAD + part_rows] = jnp.where(w == 0, 0.0, part_xr[e, 0])
        field[planes + DEEP:, PAD:PAD + part_rows] = jnp.where(w == last_w, 0.0, part_xr[e, 1])
        for i in (0, 1):
            part_y(field, e, i).start()

    def part_y_end(field, e):
        for i in (0, 1):
            part_y(field, e, i).wait_recv()

        @pl.when(n == 0)
        def _():
            field[:, 0:PAD] = jnp.zeros_like(field[:, 0:PAD])

        @pl.when(n == last_n)
        def _():
            field[:, PAD + part_rows:] = jnp.zeros_like(field[:, PAD + part_rows:])

        for i in (0, 1):
            part_x(field, e, i).wait_send()
            part_y(field, e, i).wait_send()

    def part_start():
        for way, k in halves:
            second_copy(way, k).wait_recv()
        per_half = planes // 2
        for way in (0, 1):
            mine = own[1 - way]
            for i in range(per_half):
                here = slice(i * part_rows, (i + 1) * part_rows)
                total = first_sum[way, mine, here]
                for k in range(1, side):
                    total = total + second_in[way, k, here]
                x = way * per_half + i
                tp[DEEP + x, PAD:PAD + part_rows] = substrate[x] + dissipation_factor * total
        part_x_start(tp, 0)

    barrier = pltpu.get_barrier_semaphore()

    def greet_n(k, c):
        pl.semaphore_signal(barrier, inc=1, device_id=(w, across(k)), device_id_type=MESH)
        return c

    def greet_w(k, c):
        pl.semaphore_signal(barrier, inc=1, device_id=(along(k), n), device_id_type=MESH)
        return c

    lax.fori_loop(1, n_narrow, greet_n, 0)
    lax.fori_loop(1, n_wide, greet_w, 0)

    lane = lax.broadcasted_iota(jnp.int32, (per * rows, 128), 1)
    low_half = lane < 64
    odd = lax.rem(n, 2)
    block = 16

    def later_half(count):
        lanes = lax.broadcasted_iota(jnp.int32, (count, 128), 1)
        return jnp.where(lanes < 64, odd, 1 - odd) == 1

    def swap(x):
        return pltpu.roll(x, 64, 1)

    def power(x, exponent):
        for _ in range(int(math.log2(exponent))):
            x = x * x
        return x

    def forward_copy(g, k):
        to = across(k)
        return pltpu.make_async_remote_copy(
            src_ref=zsend.at[to, pl.ds(g * per, per)],
            dst_ref=rbuf.at[pl.ds(g * per, per), pl.ds(pl.multiple_of(n * rows, rows), rows)],
            send_sem=nf_send.at[g, k],
            recv_sem=nf_recv.at[g, k],
            device_id=(w, to),
            device_id_type=MESH,
        )

    def forward_arrival(g, k):
        source = across(n_narrow - k)
        here = rbuf.at[pl.ds(g * per, per), pl.ds(pl.multiple_of(source * rows, rows), rows)]
        return pltpu.make_async_remote_copy(
            src_ref=here, dst_ref=here, send_sem=nf_send.at[g, k], recv_sem=nf_recv.at[g, k],
            device_id=(w, source), device_id_type=MESH,
        )

    loaded(0, 1)
    for g in range(GROUPS):
        lines = div[:, g].reshape(xps * rows, n_z)
        lines = dot_left(lines, fz_h[...], fz_l[...])
        for m in range(n_z // 128):
            e = lines[:per * rows, 128 * m:128 * (m + 1)]
            o = swap(lines[per * rows:, 128 * m:128 * (m + 1)])
            first = jnp.where(low_half, e, o)
            second = jnp.where(low_half, o, e)
            zsend[2 * m, g * per:(g + 1) * per] = first.reshape(per, rows, 128)
            zsend[2 * m + 1, g * per:(g + 1) * per] = second.reshape(per, rows, 128)
        if g == 0:
            pl.semaphore_wait(barrier, n_narrow - 1 + n_wide - 1)

        def launch(k, c):
            forward_copy(g, k).start()
            return c

        lax.fori_loop(1, n_narrow, launch, 0)
        if g == 0:
            for hop_ in hops:
                far_hop(*hop_).start()
            cp[DEEP:DEEP + planes, PAD:PAD + part_rows] = spread[...]
            part_x_start(cp, 1)

    for hop_ in hops:
        near_hop(*hop_).start()
    s = s_y[...] + s_z[n][0:1, :] + penalty
    root = jnp.sqrt(s * (1.0 + s))
    rtab[0] = 1.0 / (1.0 + 2.0 * s + 2.0 * root)
    rtab[1] = -1.0 / root

    def chunk(index):
        return pl.ds(pl.multiple_of(index * chunk_rows, chunk_rows), chunk_rows)

    def out_copy(g, k):
        to = along(k)
        return pltpu.make_async_remote_copy(
            src_ref=mom.at[g, chunk(to)], dst_ref=mrecv.at[g, w],
            send_sem=wf_send.at[g], recv_sem=wf_recv.at[g],
            device_id=(to, n), device_id_type=MESH,
        )

    def all_out(g):
        here = mrecv.at[g, pl.ds(0, n_wide - 1)]
        return pltpu.make_async_remote_copy(
            src_ref=here, dst_ref=here, send_sem=wf_send.at[g], recv_sem=wf_recv.at[g],
            device_id=(along(1), n), device_id_type=MESH,
        )

    def back_copy(g, k):
        to = along(k)
        return pltpu.make_async_remote_copy(
            src_ref=absend.at[g, to], dst_ref=ab.at[g, chunk(w)],
            send_sem=wb_send.at[g], recv_sem=wb_recv.at[g],
            device_id=(to, n), device_id_type=MESH,
        )

    def all_back(g):
        here = ab.at[g, pl.ds(0, (n_wide - 1) * chunk_rows)]
        return pltpu.make_async_remote_copy(
            src_ref=here, dst_ref=here, send_sem=wb_send.at[g], recv_sem=wb_recv.at[g],
            device_id=(along(1), n), device_id_type=MESH,
        )

    def each(count, action):
        def body(k, c):
            action(k)
            return c

        lax.fori_loop(1, count, body, 0)

    for g in range(GROUPS):
        span = slice(g * per, (g + 1) * per)
        rbuf[span, pl.ds(pl.multiple_of(n * rows, rows), rows)] = zsend[n, span]
        if g == 0:
            part_x_end(cp, 1)
            loaded(4, 5)
        each(n_narrow, lambda k: forward_arrival(g, k).wait_recv())
        lines = jnp.concatenate([rbuf[i] for i in range(g * per, (g + 1) * per)], axis=1)
        lines = dot_right(cy_h[...], cy_l[...], lines)
        for i in range(per):
            ubuf[g * per + i] = lines[:, 128 * i:128 * (i + 1)]

        def moments(i, c):
            here = pl.ds(pl.multiple_of(i * block, block), block)
            r = rtab[0, here]
            f = ubuf[g * per, here]
            b = ubuf[g * per + per - 1, here]
            for k in range(1, per):
                f = f * r + ubuf[g * per + k, here]
                b = b * r + ubuf[g * per + per - 1 - k, here]
            halves_[g, 0, here] = f
            halves_[g, 1, here] = b
            rp = power(r, per)
            mom[g, here] = jnp.where(later_half(block), f + rp * swap(f), b + rp * swap(b))
            return c

        lax.fori_loop(0, n_y // block, moments, 0)
        each(n_wide, lambda k: out_copy(g, k).start())
        mrecv[g, w] = mom[g, chunk(w)]
        if g == 0:
            relay()

    q = power(rtab[0, chunk(w)], xps)
    closing = 1.0 / (1.0 - power(q, n_wide))
    for g in range(GROUPS):
        all_out(g).wait_recv()
        f = mrecv[g, 0]
        b = mrecv[g, n_wide - 1]
        for j in range(1, n_wide):
            f = f * q + mrecv[g, j]
            b = b * q + mrecv[g, n_wide - 1 - j]
        f = f * closing
        b = b * closing
        ahead, behind = [], []
        for j in range(n_wide):
            ahead.append(f)
            behind.append(b)
            f = f * q + mrecv[g, j]
            b = b * q + mrecv[g, n_wide - 1 - j]
        for j in range(n_wide):
            absend[g, j] = jnp.where(later_half(chunk_rows), ahead[j], behind[n_wide - 1 - j])
        each(n_wide, lambda k: back_copy(g, k).start())
        ab[g, chunk(w)] = absend[g, w]

    def backward_copy(g, k):
        to = across(k)
        return pltpu.make_async_remote_copy(
            src_ref=vsend.at[to, pl.ds(g * per, per)],
            dst_ref=zrecv.at[n, pl.ds(g * per, per)],
            send_sem=nb_send.at[g, k],
            recv_sem=nb_recv.at[g, k],
            device_id=(w, to),
            device_id_type=MESH,
        )

    def backward_arrival(g, k):
        source = across(n_narrow - k)
        here = zrecv.at[source, pl.ds(g * per, per)]
        return pltpu.make_async_remote_copy(
            src_ref=here, dst_ref=here, send_sem=nb_send.at[g, k], recv_sem=nb_recv.at[g, k],
            device_id=(w, source), device_id_type=MESH,
        )

    loaded(6, 7)
    for g in range(GROUPS):
        span = slice(g * per, (g + 1) * per)
        all_back(g).wait_recv()

        def solve(i, c):
            here = pl.ds(pl.multiple_of(i * block, block), block)
            later = later_half(block)
            r = rtab[0, here]
            scale = rtab[1, here]
            rp = power(r, per)
            mixed = ab[g, here]
            other = swap(mixed)
            f = jnp.where(later, mixed, other)
            b = jnp.where(later, other, mixed)
            f = jnp.where(later, rp * f + swap(halves_[g, 0, here]), f)
            b = jnp.where(later, b, rp * b + swap(halves_[g, 1, here]))
            behind = []
            for k in range(per - 1, -1, -1):
                rb = b * r
                behind.append(rb)
                b = rb + ubuf[g * per + k, here]
            for k in range(per):
                f = f * r + ubuf[g * per + k, here]
                ubuf[g * per + k, here] = scale * (f + behind[per - 1 - k])
            return c

        lax.fori_loop(0, n_y // block, solve, 0)
        lines = jnp.concatenate([ubuf[i] for i in range(g * per, (g + 1) * per)], axis=1)
        lines = dot_right(iy_h[...], iy_l[...], lines)
        for to in range(n_narrow):
            for i in range(per):
                vsend[to, g * per + i] = lines[to * rows:(to + 1) * rows, 128 * i:128 * (i + 1)]
        each(n_narrow, lambda k: backward_copy(g, k).start())
        zrecv[n, span] = vsend[n, span]

    first_total()
    part_y_end(cp, 1)
    loaded(2, 3)

    def x_halo(side):
        source = 2 * xps if side else 1
        return pltpu.make_async_remote_copy(
            src_ref=press.at[source], dst_ref=xrecv.at[1 - side],
            send_sem=h_send.at[side], recv_sem=h_recv.at[1 - side],
            device_id=(wide_near[side], n), device_id_type=MESH,
        )

    def y_halo_copy(side):
        return pltpu.make_async_remote_copy(
            src_ref=ysend.at[side], dst_ref=yrecv.at[1 - side],
            send_sem=h_send.at[2 + side], recv_sem=h_recv.at[3 - side],
            device_id=(w, narrow_near[side]), device_id_type=MESH,
        )

    for g in range(GROUPS):
        each(n_narrow, lambda k: backward_arrival(g, k).wait_recv())
        evens, odds = [], []
        for m in range(n_z // 128):
            first = zrecv[2 * m, g * per:(g + 1) * per].reshape(per * rows, 128)
            second = zrecv[2 * m + 1, g * per:(g + 1) * per].reshape(per * rows, 128)
            evens.append(jnp.where(low_half, first, second))
            odds.append(swap(jnp.where(low_half, second, first)))
        lines = jnp.concatenate(
            [jnp.concatenate(evens, axis=1), jnp.concatenate(odds, axis=1)], axis=0
        )
        lines = dot_left(lines, iz_h[...], iz_l[...])
        for i in range(xps):
            plane = lines[i * rows:(i + 1) * rows]
            x = 2 * i + g
            press[x + 1] = plane
            ysend[0, x] = plane[0]
            ysend[1, x] = plane[rows - 1]
        if g == 0:
            x_halo(0).start()
            part_start()
    x_halo(1).start()
    y_halo_copy(0).start()
    y_halo_copy(1).start()
    part_x_end(tp, 0)

    for way, k in halves:
        second_copy(way, k).wait_send()
    for hop_ in hops:
        far_hop(*hop_).wait_send()
        near_hop(*hop_).wait_send()
        joint_hop(*hop_).wait_send()
    for g in range(GROUPS):
        each(n_narrow, lambda k: forward_copy(g, k).wait_send())
        each(n_narrow, lambda k: backward_copy(g, k).wait_send())
        all_out(g).wait_send()
        all_back(g).wait_send()
    for side in (0, 1):
        x_halo(side).wait()
        y_halo_copy(side).wait()
    press[0] = xrecv[0]
    press[2 * xps + 1] = xrecv[1]
    y_halo[...] = yrecv[...]
    part_y_end(tp, 0)


def solve_pressure(divergence, slab, substrate, spread):
    n_wide, n_narrow = lax.axis_size("wide"), lax.axis_size("narrow")
    x_local, rows, n_z = divergence.shape
    n_y = rows * n_narrow
    xps = x_local // 2
    tables = [jnp.asarray(t) for t in pressure_tables(n_y, n_z, n_narrow)]
    dma = pltpu.SemaphoreType.DMA
    field = (xps, n_y, 128)
    turned = (n_narrow, xps, rows, 128)
    chunk_rows = n_y // n_wide
    side = math.isqrt(n_wide)
    planes, part_rows, depth = substrate.shape
    half = planes * part_rows // 2
    part = (planes + 2 * DEEP, part_rows + 2 * PAD, depth)
    any_space = pl.BlockSpec(memory_space=pl.ANY)
    return pl.pallas_call(
        functools.partial(pressure_kernel, n_wide, n_narrow),
        out_shape=[
            jax.ShapeDtypeStruct((x_local + 2, rows, n_z), F32),
            jax.ShapeDtypeStruct((2, x_local, n_z), F32),
            jax.ShapeDtypeStruct(part, F32),
            jax.ShapeDtypeStruct(part, F32),
        ],
        in_specs=[VM, VM, VM, VM] + [any_space] * 8 + [VM, VM],
        out_specs=[VM] * 4,
        scratch_shapes=[pltpu.VMEM(t.shape, BF16) for t in tables[:8]]
        + [
            pltpu.VMEM(turned, F32),
            pltpu.VMEM(field, F32),
            pltpu.VMEM(field, F32),
            pltpu.VMEM(turned, F32),
            pltpu.VMEM(turned, F32),
            pltpu.VMEM((2, n_y, 128), F32),
            pltpu.VMEM((GROUPS, 2, n_y, 128), F32),
            pltpu.VMEM((GROUPS, n_y, 128), F32),
            pltpu.VMEM((GROUPS, n_wide, chunk_rows, 128), F32),
            pltpu.VMEM((GROUPS, n_wide, chunk_rows, 128), F32),
            pltpu.VMEM((GROUPS, n_y, 128), F32),
            pltpu.VMEM((2, rows, n_z), F32),
            pltpu.VMEM((2, x_local, n_z), F32),
            pltpu.VMEM((2, x_local, n_z), F32),
            pltpu.VMEM((2, 2, side, half // 2, depth), F32),
            pltpu.VMEM((2, 2, side, half // 2, depth), F32),
            pltpu.VMEM((2, 2, side, half, depth), F32),
            pltpu.VMEM((2, side, half, depth), F32),
            pltpu.VMEM((2, side, half, depth), F32),
            pltpu.VMEM((2, 2, DEEP, part_rows, depth), F32),
            dma((GROUPS, n_narrow)),
            dma((GROUPS, n_narrow)),
            dma((GROUPS, n_narrow)),
            dma((GROUPS, n_narrow)),
            dma((GROUPS,)),
            dma((GROUPS,)),
            dma((GROUPS,)),
            dma((GROUPS,)),
            dma((4,)),
            dma((4,)),
            dma((2, 2, 3)),
            dma((2, 2, 3)),
            dma((2, side)),
            dma((2, side)),
            dma((2, 4)),
            dma((2, 4)),
            dma((8,)),
        ],
        compiler_params=pltpu.CompilerParams(
            collective_id=1, has_side_effects=True, vmem_limit_bytes=32 * 2**20
        ),
        name="pressure",
    )(
        divergence.reshape(xps, 2, rows, n_z),
        slab.reshape(side, side, 2 * half, depth),
        substrate, spread, *tables,
    )


def conduct(step, span, source, coefficient, target):
    planes, rows, depth = coefficient.shape
    lane = lax.broadcasted_iota(jnp.int32, (rows, depth), 1)

    def plane(x, c):
        p = source[x]
        around = source[x + 1] + source[x - 1] + pltpu.roll(p, 1, 0) + pltpu.roll(p, rows - 1, 0)
        around += jnp.where(lane == 0, 0.0, pltpu.roll(p, 1, 1))
        around += jnp.where(lane == depth - 1, 0.0, pltpu.roll(p, depth - 1, 1))
        new = p + coefficient[x] * (around - 6.0 * p)
        if step == STEPS - 1:
            target[x - DEEP] = new[PAD:rows - PAD]
        else:
            target[x] = new
        return c

    lax.fori_loop(*span, plane, 0, unroll=2)


def y_step(plane, before, after, ahead):
    rows = plane.shape[0]
    row = lax.broadcasted_iota(jnp.int32, plane.shape, 0)
    if ahead:
        return jnp.where(row == rows - 1, after, pltpu.roll(plane, rows - 1, 0))
    return jnp.where(row == 0, before, pltpu.roll(plane, 1, 0))


def project_kernel(lead, trail, y_halo, tp, cp, current, out, part, tq, tr):
    step = pl.program_id(0)
    planes, n_z = current.shape[1], current.shape[3]
    total = tp.shape[0]
    for i in range(2 * STEPS):

        @pl.when(step == i)
        def _():
            first, last = i // 2 + 1, total - i // 2 - 1
            span = (first, total // 2) if i % 2 == 0 else (total // 2, last)
            conduct(i // 2, span, (tp, tq, tr)[i // 2], cp, (tq, tr, part)[i // 2])

    block = [lead[0], lead[1], trail[0], trail[1]]
    for i in range(planes):
        x = step * planes + i
        p = block[i + 1]
        before = y_halo[0, pl.ds(x, 1)]
        after = y_halo[1, pl.ds(x, 1)]
        out[0, i] = current[0, i] - (block[i + 2] - block[i]) * 0.5
        out[1, i] = current[1, i] - 0.5 * (
            y_step(p, before, after, True) - y_step(p, before, after, False)
        )
        out[2, i] = current[2, i] - 0.5 * (pltpu.roll(p, n_z - 1, 1) - pltpu.roll(p, 1, 1))


def project(current, press, y_halo, tp, cp):
    _, x_local, rows, n_z = current.shape
    planes = 2
    spec = pl.BlockSpec((3, planes, rows, n_z), lambda i: (0, i, 0, 0))
    part = (tp.shape[0] - 2 * DEEP, tp.shape[1] - 2 * PAD, tp.shape[2])
    return pl.pallas_call(
        project_kernel,
        grid=(x_local // planes,),
        out_shape=[jax.ShapeDtypeStruct(current.shape, F32), jax.ShapeDtypeStruct(part, F32)],
        in_specs=[
            pl.BlockSpec((planes, rows, n_z), lambda i: (i, 0, 0)),
            pl.BlockSpec((planes, rows, n_z), lambda i: (i + 1, 0, 0)),
            VM, VM, VM, spec,
        ],
        out_specs=[spec, pl.BlockSpec(part, lambda i: (0, 0, 0))],
        scratch_shapes=[pltpu.VMEM(tp.shape, F32), pltpu.VMEM(tp.shape, F32)],
        compiler_params=pltpu.CompilerParams(vmem_limit_bytes=20 * 2**20),
        name="projection",
    )(press, press, y_halo, tp, cp, current)


def per_device(
    material_flow_vector,
    tool_push_density,
    tool_warmth_excess,
    substrate_warmth_excess,
    spread_coefficient,
    source_owner_sheet,
    source_part_line,
):
    current, divergence, heat = flow(material_flow_vector, tool_push_density, tool_warmth_excess)
    slab_ids = source_owner_sheet[:, 0]
    slab_count = lax.axis_size("wide")
    component_lines = substrate_warmth_excess.shape[0] * substrate_warmth_excess.shape[1]
    target = slab_ids * component_lines + source_part_line
    partial_value = slab_heat(target, heat, slab_count * component_lines)
    solved = solve_pressure(
        divergence, partial_value, substrate_warmth_excess, spread_coefficient
    )
    return tuple(project(current, *solved))


def solution(mesh):
    return jax.shard_map(
        per_device,
        mesh=mesh,
        in_specs=(
            P(None, "wide", "narrow", None),
            P(None, "wide", "narrow", None),
            P("wide", "narrow", None),
            P("wide", "narrow", None),
            P("wide", "narrow", None),
            P(("wide", "narrow"), None),
            P(("wide", "narrow")),
        ),
        out_specs=(P(None, "wide", "narrow", None), P("wide", "narrow", None)),
        check_vma=False,
    )
```

```python
import functools
import math

import jax
import jax.numpy as jnp
import ml_dtypes
import numpy as np
from jax import lax
from jax.experimental import pallas as pl
from jax.experimental.pallas import tpu as pltpu
from jax.sharding import PartitionSpec as P

STEPS = 3
MESH = pl.DeviceIdType.MESH
F32 = jnp.float32
BF16 = jnp.bfloat16
VM = pl.BlockSpec(memory_space=pltpu.VMEM)

time_step = 0.15
rate_base = 0.5
zener_energy = 4.0
stress_exponent = 5.0
penalty = 0.001
dissipation_factor = 0.1
GROUPS = 2
DEEP = STEPS


PAD = 8
STRIP = 8


def flow_kernel(
    n_wide, n_narrow,
    vel_in, push_in, warmth_in,
    mom, div, heat,
    velp, provp, mup0, mup1, lz, push,
    vel_ys, vel_yr, mu_ys0, mu_yr0, prov_ys, prov_yr, mu_ys1, mu_yr1, mom_ys, mom_yr, mom_xr,
    load_sem, h_send, h_recv,
):
    w = lax.axis_index("wide")
    n = lax.axis_index("narrow")
    _, planes, rows, n_z = vel_in.shape
    strips = rows // STRIP
    wide_to = (lax.rem(w + n_wide - 1, n_wide), lax.rem(w + 1, n_wide))
    narrow_to = (lax.rem(n + n_narrow - 1, n_narrow), lax.rem(n + 1, n_narrow))
    body = pl.ds(PAD, rows)

    barrier = pltpu.get_barrier_semaphore()
    for side in (0, 1):
        pl.semaphore_signal(barrier, inc=1, device_id=(wide_to[side], n), device_id_type=MESH)
        pl.semaphore_signal(barrier, inc=1, device_id=(w, narrow_to[side]), device_id_type=MESH)

    loads = [
        pltpu.make_async_copy(vel_in, velp.at[:, pl.ds(1, planes), body], load_sem.at[0]),
        pltpu.make_async_copy(push_in, push, load_sem.at[1]),
    ]
    for load in loads:
        load.start()

    def wide_copy(e, side, source, target):
        return pltpu.make_async_remote_copy(
            src_ref=source, dst_ref=target,
            send_sem=h_send.at[e, side], recv_sem=h_recv.at[e, 1 - side],
            device_id=(wide_to[side], n), device_id_type=MESH,
        )

    def narrow_copy(e, side, sends, lands):
        return pltpu.make_async_remote_copy(
            src_ref=sends.at[side], dst_ref=lands.at[1 - side],
            send_sem=h_send.at[e, 2 + side], recv_sem=h_recv.at[e, 3 - side],
            device_id=(w, narrow_to[side]), device_id_type=MESH,
        )

    def x_pair(e, field, lead=()):
        return [
            wide_copy(e, 0, field.at[lead + (1, body)], field.at[lead + (planes + 1, body)]),
            wide_copy(e, 1, field.at[lead + (planes, body)], field.at[lead + (0, body)]),
        ]

    def y_pair(e, sends, lands):
        return [narrow_copy(e, side, sends, lands) for side in (0, 1)]

    def all_x(action, first=0, last=None, unroll=1):
        def step(x, c):
            action(x)
            return c

        lax.fori_loop(first, planes if last is None else last, step, 0, unroll=unroll)

    def y_fill(field, lands, comps):
        def fill(x):
            here = pl.ds(x, 1)
            if comps is None:
                field[x + 1, PAD - 1:PAD] = lands[0, here]
                field[x + 1, PAD + rows:PAD + rows + 1] = lands[1, here]
                return
            for i, c in enumerate(comps):
                field[c, x + 1, PAD - 1:PAD] = lands[0, i, here]
                field[c, x + 1, PAD + rows:PAD + rows + 1] = lands[1, i, here]

        all_x(fill)

    def z_ahead(a):
        return pltpu.roll(a, n_z - 1, 1)

    def z_behind(a):
        return pltpu.roll(a, 1, 1)

    loads[0].wait()

    def vel_rows(x):
        for c in range(3):
            vel_ys[0, c, pl.ds(x, 1)] = velp[c, x + 1, PAD:PAD + 1]
            vel_ys[1, c, pl.ds(x, 1)] = velp[c, x + 1, PAD + rows - 1:PAD + rows]

    all_x(vel_rows)
    pl.semaphore_wait(barrier, 4)
    every = slice(None)
    vel_x = x_pair(0, velp, (every,))
    vel_y = y_pair(0, vel_ys, vel_yr)
    for copy in vel_x + vel_y:
        copy.start()

    def zener_log(x):
        lz[x] = (zener_energy / stress_exponent) * (1.0 / warmth_in[x] - 1.0)

    all_x(zener_log, unroll=2)
    loads[1].wait()

    def excess(src, x, r):
        here = slice(PAD + STRIP * r, PAD + STRIP * (r + 1))
        up = slice(PAD + STRIP * r + 1, PAD + STRIP * (r + 1) + 1)
        down = slice(PAD + STRIP * r - 1, PAD + STRIP * (r + 1) - 1)
        dx = [src[c, x + 2, here] - src[c, x, here] for c in range(3)]
        dy = [src[c, x + 1, up] - src[c, x + 1, down] for c in range(3)]
        mid = [src[c, x + 1, here] for c in range(3)]
        dz = [z_ahead(m) - z_behind(m) for m in mid]
        xy, xz, yz = dy[0] + dx[1], dz[0] + dx[2], dz[1] + dy[2]
        diagonal = dx[0] * dx[0] + dy[1] * dy[1] + dz[2] * dz[2]
        return 0.5 * diagonal + 0.25 * (xy * xy + xz * xz + yz * yz)

    def mu_plane(src, mup, ys, with_heat):
        def plane(x, which):
            for r in which:
                part = slice(STRIP * r, STRIP * (r + 1))
                extra = excess(src, x, r)
                rate_sq = extra + rate_base**2
                v = jnp.exp((0.5 / stress_exponent) * jnp.log(rate_sq) + lz[x, part])
                mu = jnp.log(v + jnp.sqrt(v * v + 1.0)) * lax.rsqrt(rate_sq) * (1.0 / 3.0)
                mup[x + 1, PAD + STRIP * r:PAD + STRIP * (r + 1)] = mu
                if r == 0:
                    ys[0, pl.ds(x, 1)] = mu[0:1]
                if r == strips - 1:
                    ys[1, pl.ds(x, 1)] = mu[STRIP - 1:]
                if with_heat:
                    h = mu * extra
                    to = pl.ds(pl.multiple_of(x * rows + STRIP * r, STRIP), STRIP)
                    for m in range(n_z // 128):
                        heat[m, to] = h[:, 128 * m:128 * (m + 1)]

        return plane

    def advance_plane(mup, final):
        def plane(x, which):
            for r in which:
                part = slice(STRIP * r, STRIP * (r + 1))
                here = slice(PAD + STRIP * r, PAD + STRIP * (r + 1))
                up = slice(PAD + STRIP * r + 1, PAD + STRIP * (r + 1) + 1)
                down = slice(PAD + STRIP * r - 1, PAD + STRIP * (r + 1) - 1)
                m = mup[x + 1, here]
                m_xp = m + mup[x + 2, here]
                m_xm = m + mup[x, here]
                m_yp = m + mup[x + 1, up]
                m_ym = m + mup[x + 1, down]
                m_z = m + z_ahead(m)
                for c in range(3):
                    u = velp[c, x + 1, here]
                    flux = m_z * (z_ahead(u) - u)
                    total = flux - z_behind(flux)
                    total += m_xp * (velp[c, x + 2, here] - u) - m_xm * (u - velp[c, x, here])
                    total += m_yp * (velp[c, x + 1, up] - u) - m_ym * (u - velp[c, x + 1, down])
                    new = u + (0.5 * time_step) * total + time_step * push[c, x, part]
                    provp[c, x + 1, here] = new
                    if final:
                        mom[c, x, part] = new
                        if c == 1:
                            if r == 0:
                                mom_ys[0, pl.ds(x, 1)] = new[0:1]
                            if r == strips - 1:
                                mom_ys[1, pl.ds(x, 1)] = new[STRIP - 1:]
                    else:
                        if r == 0:
                            prov_ys[0, c, pl.ds(x, 1)] = new[0:1]
                        if r == strips - 1:
                            prov_ys[1, c, pl.ds(x, 1)] = new[STRIP - 1:]

        return plane

    def stage(action, arriving_x, arriving_y, fill, fill_x=None):
        all_x(lambda x: action(x, range(1, strips - 1)), 1, planes - 1, 2)
        for copy in arriving_y:
            copy.wait_recv()
        fill()
        all_x(lambda x: action(x, (0, strips - 1)), 1, planes - 1, 2)
        for copy in arriving_x:
            copy.wait_recv()
        if fill_x is not None:
            fill_x()
        all_x(lambda i: action(i * (planes - 1), range(strips)), 0, 2)

    stage(mu_plane(velp, mup0, mu_ys0, False), vel_x, vel_y,
          lambda: y_fill(velp, vel_yr, (0, 1, 2)))
    mu_x0 = x_pair(1, mup0)
    mu_y0 = y_pair(1, mu_ys0, mu_yr0)
    for copy in mu_x0 + mu_y0:
        copy.start()
    stage(advance_plane(mup0, False), mu_x0, mu_y0, lambda: y_fill(mup0, mu_yr0, None))
    prov_x = x_pair(2, provp, (every,))
    prov_y = y_pair(2, prov_ys, prov_yr)
    for copy in prov_x + prov_y:
        copy.start()
    stage(mu_plane(provp, mup1, mu_ys1, True), prov_x, prov_y,
          lambda: y_fill(provp, prov_yr, (0, 1, 2)))
    mu_x1 = x_pair(3, mup1)
    mu_y1 = y_pair(3, mu_ys1, mu_yr1)
    for copy in mu_x1 + mu_y1:
        copy.start()
    for copy in prov_x + prov_y:
        copy.wait_send()
    stage(advance_plane(mup1, True), mu_x1, mu_y1, lambda: y_fill(mup1, mu_yr1, None))
    mom_x = [
        wide_copy(4, 0, mom.at[0, 0], mom_xr.at[1]),
        wide_copy(4, 1, mom.at[0, planes - 1], mom_xr.at[0]),
    ]
    mom_y = y_pair(4, mom_ys, mom_yr)
    for copy in mom_x + mom_y:
        copy.start()
    for copy in vel_x + vel_y + mu_x0 + mu_y0 + mu_x1 + mu_y1:
        copy.wait_send()

    def fill_rows():
        def fill(x):
            here = pl.ds(x, 1)
            provp[1, x + 1, PAD - 1:PAD] = mom_yr[0, here]
            provp[1, x + 1, PAD + rows:PAD + rows + 1] = mom_yr[1, here]

        all_x(fill)

    def div_plane(x, which):
        for r in which:
            part = slice(STRIP * r, STRIP * (r + 1))
            here = slice(PAD + STRIP * r, PAD + STRIP * (r + 1))
            up = slice(PAD + STRIP * r + 1, PAD + STRIP * (r + 1) + 1)
            down = slice(PAD + STRIP * r - 1, PAD + STRIP * (r + 1) - 1)
            u = provp[2, x + 1, here]
            total = provp[0, x + 2, here] - provp[0, x, here]
            total += provp[1, x + 1, up] - provp[1, x + 1, down]
            div[x, part] = 0.5 * (total + (z_ahead(u) - z_behind(u)))

    def fill_planes():
        provp[0, 0, body] = mom_xr[0]
        provp[0, planes + 1, body] = mom_xr[1]

    stage(div_plane, mom_x, mom_y, fill_rows, fill_planes)
    for copy in mom_x + mom_y:
        copy.wait_send()


def flow(velocity, push, warmth):
    n_wide, n_narrow = lax.axis_size("wide"), lax.axis_size("narrow")
    _, planes, rows, n_z = velocity.shape
    padded = (planes + 2, PAD + rows + PAD, n_z)
    line = (2, planes, n_z)
    lines = (2, 3, planes, n_z)
    any_space = pl.BlockSpec(memory_space=pl.ANY)
    shapes = [(3,) + padded, (3,) + padded, padded, padded, (planes, rows, n_z), velocity.shape]
    shapes += [lines, lines, line, line, lines, lines, line, line, line, line, (2, rows, n_z)]
    dma = pltpu.SemaphoreType.DMA
    return pl.pallas_call(
        functools.partial(flow_kernel, n_wide, n_narrow),
        out_shape=[
            jax.ShapeDtypeStruct(velocity.shape, F32),
            jax.ShapeDtypeStruct((planes, rows, n_z), F32),
            jax.ShapeDtypeStruct((n_z // 128, planes * rows, 128), F32),
        ],
        in_specs=[any_space, any_space, VM],
        out_specs=[VM] * 3,
        scratch_shapes=[pltpu.VMEM(shape, F32) for shape in shapes]
        + [dma((2,)), dma((5, 4)), dma((5, 4))],
        compiler_params=pltpu.CompilerParams(
            collective_id=2, has_side_effects=True, vmem_limit_bytes=48 * 2**20
        ),
        name="flow",
    )(velocity, push, warmth)


def gather_kernel(target, heat, out, other):
    out[...] = jnp.zeros_like(out)
    other[...] = jnp.zeros_like(other)
    depth = heat.shape[0]

    def cell(i, c):
        for m in range(depth):
            into = out if m % 2 == 0 else other
            row = pl.ds(target[i * depth + m], 1)
            into[row] = into[row] + heat[m, pl.ds(i, 1)]
        return c

    lax.fori_loop(0, heat.shape[1], cell, 0, unroll=8)
    step = 256

    def join(i, c):
        here = pl.ds(pl.multiple_of(i * step, step), step)
        out[here] = out[here] + other[here]
        return c

    lax.fori_loop(0, out.shape[0] // step, join, 0)


def slab_heat(target, heat, lines):
    return pl.pallas_call(
        gather_kernel,
        out_shape=jax.ShapeDtypeStruct((lines, 128), F32),
        in_specs=[pl.BlockSpec(memory_space=pltpu.SMEM), VM],
        out_specs=VM,
        scratch_shapes=[pltpu.VMEM((lines, 128), F32)],
        compiler_params=pltpu.CompilerParams(vmem_limit_bytes=24 * 2**20),
        name="slab_heat",
    )(target, heat)


def real_basis(length):
    cells = np.arange(length, dtype=np.float64)
    rows = [np.full(length, 1.0 / math.sqrt(length)), (-1.0) ** cells / math.sqrt(length)]
    waves = [0, length // 2]
    for k in range(1, length // 2):
        angle = 2.0 * math.pi * k * cells / length
        rows.append(np.cos(angle) * math.sqrt(2.0 / length))
        rows.append(np.sin(angle) * math.sqrt(2.0 / length))
        waves += [k, k]
    waves = np.array(waves)
    symbol = np.sin(2.0 * math.pi * (waves % (length // 2)) / length) ** 2
    return np.stack(rows), symbol


def split_table(table):
    high = table.astype(np.float32).astype(ml_dtypes.bfloat16)
    low = (table - high.astype(np.float64)).astype(np.float32).astype(ml_dtypes.bfloat16)
    return [high, low]


def pressure_tables(n_y, n_z, n_narrow):
    basis_z, symbol_z = real_basis(n_z)
    basis_y, symbol_y = real_basis(n_y)
    forward = basis_z.T
    tables = []
    for table in (forward, forward.T, basis_y, basis_y.T):
        tables += split_table(np.ascontiguousarray(table))
    s_y = np.broadcast_to(symbol_y[:, None], (n_y, 128)).astype(np.float32)
    s_z = np.tile(symbol_z.reshape(n_narrow, 1, 64), (1, 8, 2)).astype(np.float32)
    return tables + [s_y, s_z]


def split_value(x):
    high = x.astype(BF16)
    return high, (x - high.astype(F32)).astype(BF16)


def dot_left(x, high, low):
    x_high, x_low = split_value(x)
    dot = functools.partial(jnp.dot, preferred_element_type=F32)
    return dot(x_high, high) + (dot(x_high, low) + dot(x_low, high))


def dot_right(high, low, x):
    x_high, x_low = split_value(x)
    dot = functools.partial(jnp.dot, preferred_element_type=F32)
    return dot(high, x_high) + (dot(low, x_high) + dot(high, x_low))


def pressure_kernel(
    n_wide, n_narrow,
    div, slab, substrate, spread, *rest,
):
    table_refs, rest = rest[:8], rest[8:]
    s_y, s_z, press, y_halo, tp, cp = rest[:6]
    tables, rest = rest[6:14], rest[14:]
    (
        zsend, rbuf, ubuf, vsend, zrecv, rtab, halves_, mom, mrecv, absend, ab, xrecv, yrecv, ysend,
        relay_in, relay_out, first_in, first_sum, second_in, part_xr,
        nf_send, nf_recv, nb_send, nb_recv, wf_send, wf_recv, wb_send, wb_recv, h_send, h_recv,
        f_send, f_recv, q_send, q_recv, p_send, p_recv, table_sem,
    ) = rest
    fz_h, fz_l, iz_h, iz_l, cy_h, cy_l, iy_h, iy_l = tables
    loads = [
        pltpu.make_async_copy(table_refs[i], tables[i], table_sem.at[i]) for i in range(8)
    ]

    def loaded(*which):
        for i in which:
            loads[i].wait()

    for i in (0, 1, 4, 5, 6, 7, 2, 3):
        loads[i].start()
    w = lax.axis_index("wide")
    n = lax.axis_index("narrow")
    xps, _, rows, n_z = div.shape
    n_y = s_y.shape[0]
    per = xps // 2
    chunk_rows = n_y // n_wide

    def across(k):
        return lax.rem(n + k, n_narrow)

    def along(k):
        return lax.rem(w + k, n_wide)

    side = math.isqrt(n_wide)
    half = slab.shape[2] // 2
    own = (w // side, lax.rem(w, side))

    def peer(way, k):
        to = lax.rem(own[way] + k, side)
        return (to, to * side + own[1] if way == 0 else own[0] * side + to)

    quarter = half // 2

    def chunk_rows_of(way, to, part, start=0, size=None):
        at = pl.ds(way * half + part * quarter + start, quarter if size is None else size)
        return slab.at[to, :, at] if way == 0 else slab.at[:, to, at]

    def hop(way, direction, source, target, slot):
        _, device = peer(way, 1 if direction == 0 else side - 1)
        return pltpu.make_async_remote_copy(
            src_ref=source, dst_ref=target,
            send_sem=f_send.at[way, direction, slot], recv_sem=f_recv.at[way, direction, slot],
            device_id=(device, n), device_id_type=MESH,
        )

    def next_to(way, direction):
        return peer(way, 1 if direction == 0 else side - 1)[0]

    def far_hop(way, direction):
        source = chunk_rows_of(way, peer(way, 2)[0], direction)
        return hop(way, direction, source, relay_in.at[way, direction], 0)

    def near_hop(way, direction):
        source = chunk_rows_of(way, next_to(way, direction), 1 - direction)
        target = first_in.at[way, direction, :, pl.ds((1 - direction) * quarter, quarter)]
        return hop(way, direction, source, target, 1)

    def joint_hop(way, direction):
        target = first_in.at[way, direction, :, pl.ds(direction * quarter, quarter)]
        return hop(way, direction, relay_out.at[way, direction], target, 2)

    hops = [(way, direction) for way in (0, 1) for direction in (0, 1)]
    step = 32

    def relay():
        for hop_ in hops:
            far_hop(*hop_).wait_recv()
        per_slab = quarter // step

        def add(i, c):
            at = i // per_slab
            start = pl.multiple_of(lax.rem(i, per_slab) * step, step)
            here = pl.ds(start, step)
            for way, direction in hops:
                to = next_to(way, direction)
                mine = pl.ds(
                    pl.multiple_of(way * half + direction * quarter + start, step), step
                )
                own_part = slab[to, at, mine] if way == 0 else slab[at, to, mine]
                relay_out[way, direction, at, here] = relay_in[way, direction, at, here] + own_part
            return c

        lax.fori_loop(0, side * per_slab, add, 0)
        for hop_ in hops:
            joint_hop(*hop_).start()

    def second_copy(way, k):
        to, device = peer(1 - way, k)
        return pltpu.make_async_remote_copy(
            src_ref=first_sum.at[way, to], dst_ref=second_in.at[way, k],
            send_sem=q_send.at[way, k], recv_sem=q_recv.at[way, k],
            device_id=(device, n), device_id_type=MESH,
        )

    halves = [(way, k) for way in (0, 1) for k in range(1, side)]

    def first_total():
        for hop_ in hops:
            near_hop(*hop_).wait_recv()
            joint_hop(*hop_).wait_recv()
        per_slab = half // step

        def add(i, c):
            at = i // per_slab
            start = pl.multiple_of(lax.rem(i, per_slab) * step, step)
            here = pl.ds(start, step)
            for way in (0, 1):
                mine = pl.ds(pl.multiple_of(way * half + start, step), step)
                total = slab[own[0], at, mine] if way == 0 else slab[at, own[1], mine]
                first_sum[way, at, here] = (
                    total + first_in[way, 0, at, here] + first_in[way, 1, at, here]
                )
            return c

        lax.fori_loop(0, side * per_slab, add, 0)
        for way, k in halves:
            second_copy(way, k).start()

    planes = substrate.shape[0]
    part_rows = substrate.shape[1]
    inside = pl.ds(PAD, part_rows)
    last_w, last_n = n_wide - 1, n_narrow - 1
    wide_near = (lax.rem(w + last_w, n_wide), lax.rem(w + 1, n_wide))
    narrow_near = (lax.rem(n + last_n, n_narrow), lax.rem(n + 1, n_narrow))

    def part_x(field, e, side_):
        start = planes if side_ else DEEP
        return pltpu.make_async_remote_copy(
            src_ref=field.at[pl.ds(start, DEEP), inside], dst_ref=part_xr.at[e, 1 - side_],
            send_sem=p_send.at[e, side_], recv_sem=p_recv.at[e, 1 - side_],
            device_id=(wide_near[side_], n), device_id_type=MESH,
        )

    def part_y(field, e, side_):
        start = part_rows if side_ else PAD
        land = 0 if side_ else PAD + part_rows
        return pltpu.make_async_remote_copy(
            src_ref=field.at[:, pl.ds(start, PAD)], dst_ref=field.at[:, pl.ds(land, PAD)],
            send_sem=p_send.at[e, 2 + side_], recv_sem=p_recv.at[e, 3 - side_],
            device_id=(w, narrow_near[side_]), device_id_type=MESH,
        )

    def part_x_start(field, e):
        for i in (0, 1):
            part_x(field, e, i).start()

    def part_x_end(field, e):
        for i in (0, 1):
            part_x(field, e, i).wait_recv()
        field[0:DEEP, PAD:PAD + part_rows] = jnp.where(w == 0, 0.0, part_xr[e, 0])
        field[planes + DEEP:, PAD:PAD + part_rows] = jnp.where(w == last_w, 0.0, part_xr[e, 1])
        for i in (0, 1):
            part_y(field, e, i).start()

    def part_y_end(field, e):
        for i in (0, 1):
            part_y(field, e, i).wait_recv()

        @pl.when(n == 0)
        def _():
            field[:, 0:PAD] = jnp.zeros_like(field[:, 0:PAD])

        @pl.when(n == last_n)
        def _():
            field[:, PAD + part_rows:] = jnp.zeros_like(field[:, PAD + part_rows:])

        for i in (0, 1):
            part_x(field, e, i).wait_send()
            part_y(field, e, i).wait_send()

    def part_start():
        for way, k in halves:
            second_copy(way, k).wait_recv()
        per_half = planes // 2
        for way in (0, 1):
            mine = own[1 - way]
            for i in range(per_half):
                here = slice(i * part_rows, (i + 1) * part_rows)
                total = first_sum[way, mine, here]
                for k in range(1, side):
                    total = total + second_in[way, k, here]
                x = way * per_half + i
                tp[DEEP + x, PAD:PAD + part_rows] = substrate[x] + dissipation_factor * total
        part_x_start(tp, 0)

    barrier = pltpu.get_barrier_semaphore()

    def greet_n(k, c):
        pl.semaphore_signal(barrier, inc=1, device_id=(w, across(k)), device_id_type=MESH)
        return c

    def greet_w(k, c):
        pl.semaphore_signal(barrier, inc=1, device_id=(along(k), n), device_id_type=MESH)
        return c

    lax.fori_loop(1, n_narrow, greet_n, 0)
    lax.fori_loop(1, n_wide, greet_w, 0)

    lane = lax.broadcasted_iota(jnp.int32, (per * rows, 128), 1)
    low_half = lane < 64
    odd = lax.rem(n, 2)
    block = 16

    def later_half(count):
        lanes = lax.broadcasted_iota(jnp.int32, (count, 128), 1)
        return jnp.where(lanes < 64, odd, 1 - odd) == 1

    def swap(x):
        return pltpu.roll(x, 64, 1)

    def power(x, exponent):
        for _ in range(int(math.log2(exponent))):
            x = x * x
        return x

    def forward_copy(g, k):
        to = across(k)
        return pltpu.make_async_remote_copy(
            src_ref=zsend.at[to, pl.ds(g * per, per)],
            dst_ref=rbuf.at[pl.ds(g * per, per), pl.ds(pl.multiple_of(n * rows, rows), rows)],
            send_sem=nf_send.at[g, k],
            recv_sem=nf_recv.at[g, k],
            device_id=(w, to),
            device_id_type=MESH,
        )

    def forward_arrival(g, k):
        source = across(n_narrow - k)
        here = rbuf.at[pl.ds(g * per, per), pl.ds(pl.multiple_of(source * rows, rows), rows)]
        return pltpu.make_async_remote_copy(
            src_ref=here, dst_ref=here, send_sem=nf_send.at[g, k], recv_sem=nf_recv.at[g, k],
            device_id=(w, source), device_id_type=MESH,
        )

    loaded(0, 1)
    for g in range(GROUPS):
        lines = div[:, g].reshape(xps * rows, n_z)
        lines = dot_left(lines, fz_h[...], fz_l[...])
        for m in range(n_z // 128):
            e = lines[:per * rows, 128 * m:128 * (m + 1)]
            o = swap(lines[per * rows:, 128 * m:128 * (m + 1)])
            first = jnp.where(low_half, e, o)
            second = jnp.where(low_half, o, e)
            zsend[2 * m, g * per:(g + 1) * per] = first.reshape(per, rows, 128)
            zsend[2 * m + 1, g * per:(g + 1) * per] = second.reshape(per, rows, 128)
        if g == 0:
            pl.semaphore_wait(barrier, n_narrow - 1 + n_wide - 1)

        def launch(k, c):
            forward_copy(g, k).start()
            return c

        lax.fori_loop(1, n_narrow, launch, 0)
        if g == 0:
            for hop_ in hops:
                far_hop(*hop_).start()
            cp[DEEP:DEEP + planes, PAD:PAD + part_rows] = spread[...]
            part_x_start(cp, 1)

    for hop_ in hops:
        near_hop(*hop_).start()
    s = s_y[...] + s_z[n][0:1, :] + penalty
    root = jnp.sqrt(s * (1.0 + s))
    rtab[0] = 1.0 / (1.0 + 2.0 * s + 2.0 * root)
    rtab[1] = -1.0 / root

    def chunk(index):
        return pl.ds(pl.multiple_of(index * chunk_rows, chunk_rows), chunk_rows)

    def out_copy(g, k):
        to = along(k)
        return pltpu.make_async_remote_copy(
            src_ref=mom.at[g, chunk(to)], dst_ref=mrecv.at[g, w],
            send_sem=wf_send.at[g], recv_sem=wf_recv.at[g],
            device_id=(to, n), device_id_type=MESH,
        )

    def all_out(g):
        here = mrecv.at[g, pl.ds(0, n_wide - 1)]
        return pltpu.make_async_remote_copy(
            src_ref=here, dst_ref=here, send_sem=wf_send.at[g], recv_sem=wf_recv.at[g],
            device_id=(along(1), n), device_id_type=MESH,
        )

    def back_copy(g, k):
        to = along(k)
        return pltpu.make_async_remote_copy(
            src_ref=absend.at[g, to], dst_ref=ab.at[g, chunk(w)],
            send_sem=wb_send.at[g], recv_sem=wb_recv.at[g],
            device_id=(to, n), device_id_type=MESH,
        )

    def all_back(g):
        here = ab.at[g, pl.ds(0, (n_wide - 1) * chunk_rows)]
        return pltpu.make_async_remote_copy(
            src_ref=here, dst_ref=here, send_sem=wb_send.at[g], recv_sem=wb_recv.at[g],
            device_id=(along(1), n), device_id_type=MESH,
        )

    def each(count, action):
        def body(k, c):
            action(k)
            return c

        lax.fori_loop(1, count, body, 0)

    for g in range(GROUPS):
        span = slice(g * per, (g + 1) * per)
        rbuf[span, pl.ds(pl.multiple_of(n * rows, rows), rows)] = zsend[n, span]
        if g == 0:
            part_x_end(cp, 1)
            loaded(4, 5)
        each(n_narrow, lambda k: forward_arrival(g, k).wait_recv())
        lines = jnp.concatenate([rbuf[i] for i in range(g * per, (g + 1) * per)], axis=1)
        lines = dot_right(cy_h[...], cy_l[...], lines)
        for i in range(per):
            ubuf[g * per + i] = lines[:, 128 * i:128 * (i + 1)]

        def moments(i, c):
            here = pl.ds(pl.multiple_of(i * block, block), block)
            r = rtab[0, here]
            f = ubuf[g * per, here]
            b = ubuf[g * per + per - 1, here]
            for k in range(1, per):
                f = f * r + ubuf[g * per + k, here]
                b = b * r + ubuf[g * per + per - 1 - k, here]
            halves_[g, 0, here] = f
            halves_[g, 1, here] = b
            rp = power(r, per)
            mom[g, here] = jnp.where(later_half(block), f + rp * swap(f), b + rp * swap(b))
            return c

        lax.fori_loop(0, n_y // block, moments, 0, unroll=2)
        each(n_wide, lambda k: out_copy(g, k).start())
        mrecv[g, w] = mom[g, chunk(w)]
        if g == 0:
            relay()

    q = power(rtab[0, chunk(w)], xps)
    closing = 1.0 / (1.0 - power(q, n_wide))
    for g in range(GROUPS):
        all_out(g).wait_recv()
        f = mrecv[g, 0]
        b = mrecv[g, n_wide - 1]
        for j in range(1, n_wide):
            f = f * q + mrecv[g, j]
            b = b * q + mrecv[g, n_wide - 1 - j]
        f = f * closing
        b = b * closing
        ahead, behind = [], []
        for j in range(n_wide):
            ahead.append(f)
            behind.append(b)
            f = f * q + mrecv[g, j]
            b = b * q + mrecv[g, n_wide - 1 - j]
        for j in range(n_wide):
            absend[g, j] = jnp.where(later_half(chunk_rows), ahead[j], behind[n_wide - 1 - j])
        each(n_wide, lambda k: back_copy(g, k).start())
        ab[g, chunk(w)] = absend[g, w]

    def backward_copy(g, k):
        to = across(k)
        return pltpu.make_async_remote_copy(
            src_ref=vsend.at[to, pl.ds(g * per, per)],
            dst_ref=zrecv.at[n, pl.ds(g * per, per)],
            send_sem=nb_send.at[g, k],
            recv_sem=nb_recv.at[g, k],
            device_id=(w, to),
            device_id_type=MESH,
        )

    def backward_arrival(g, k):
        source = across(n_narrow - k)
        here = zrecv.at[source, pl.ds(g * per, per)]
        return pltpu.make_async_remote_copy(
            src_ref=here, dst_ref=here, send_sem=nb_send.at[g, k], recv_sem=nb_recv.at[g, k],
            device_id=(w, source), device_id_type=MESH,
        )

    loaded(6, 7)
    for g in range(GROUPS):
        span = slice(g * per, (g + 1) * per)
        all_back(g).wait_recv()

        def solve(i, c):
            here = pl.ds(pl.multiple_of(i * block, block), block)
            later = later_half(block)
            r = rtab[0, here]
            scale = rtab[1, here]
            rp = power(r, per)
            mixed = ab[g, here]
            other = swap(mixed)
            f = jnp.where(later, mixed, other)
            b = jnp.where(later, other, mixed)
            f = jnp.where(later, rp * f + swap(halves_[g, 0, here]), f)
            b = jnp.where(later, b, rp * b + swap(halves_[g, 1, here]))
            behind = []
            for k in range(per - 1, -1, -1):
                rb = b * r
                behind.append(rb)
                b = rb + ubuf[g * per + k, here]
            for k in range(per):
                f = f * r + ubuf[g * per + k, here]
                ubuf[g * per + k, here] = scale * (f + behind[per - 1 - k])
            return c

        lax.fori_loop(0, n_y // block, solve, 0, unroll=2)
        lines = jnp.concatenate([ubuf[i] for i in range(g * per, (g + 1) * per)], axis=1)
        lines = dot_right(iy_h[...], iy_l[...], lines)
        for to in range(n_narrow):
            for i in range(per):
                vsend[to, g * per + i] = lines[to * rows:(to + 1) * rows, 128 * i:128 * (i + 1)]
        each(n_narrow, lambda k: backward_copy(g, k).start())
        zrecv[n, span] = vsend[n, span]

    first_total()
    part_y_end(cp, 1)
    loaded(2, 3)

    def x_halo(side):
        source = 2 * xps if side else 1
        return pltpu.make_async_remote_copy(
            src_ref=press.at[source], dst_ref=xrecv.at[1 - side],
            send_sem=h_send.at[side], recv_sem=h_recv.at[1 - side],
            device_id=(wide_near[side], n), device_id_type=MESH,
        )

    def y_halo_copy(side):
        return pltpu.make_async_remote_copy(
            src_ref=ysend.at[side], dst_ref=yrecv.at[1 - side],
            send_sem=h_send.at[2 + side], recv_sem=h_recv.at[3 - side],
            device_id=(w, narrow_near[side]), device_id_type=MESH,
        )

    for g in range(GROUPS):
        each(n_narrow, lambda k: backward_arrival(g, k).wait_recv())
        evens, odds = [], []
        for m in range(n_z // 128):
            first = zrecv[2 * m, g * per:(g + 1) * per].reshape(per * rows, 128)
            second = zrecv[2 * m + 1, g * per:(g + 1) * per].reshape(per * rows, 128)
            evens.append(jnp.where(low_half, first, second))
            odds.append(swap(jnp.where(low_half, second, first)))
        lines = jnp.concatenate(
            [jnp.concatenate(evens, axis=1), jnp.concatenate(odds, axis=1)], axis=0
        )
        lines = dot_left(lines, iz_h[...], iz_l[...])
        for i in range(xps):
            plane = lines[i * rows:(i + 1) * rows]
            x = 2 * i + g
            press[x + 1] = plane
            ysend[0, x] = plane[0]
            ysend[1, x] = plane[rows - 1]
        if g == 0:
            x_halo(0).start()
            part_start()
    x_halo(1).start()
    y_halo_copy(0).start()
    y_halo_copy(1).start()
    part_x_end(tp, 0)

    for way, k in halves:
        second_copy(way, k).wait_send()
    for hop_ in hops:
        far_hop(*hop_).wait_send()
        near_hop(*hop_).wait_send()
        joint_hop(*hop_).wait_send()
    for g in range(GROUPS):
        each(n_narrow, lambda k: forward_copy(g, k).wait_send())
        each(n_narrow, lambda k: backward_copy(g, k).wait_send())
        all_out(g).wait_send()
        all_back(g).wait_send()
    for side in (0, 1):
        x_halo(side).wait()
        y_halo_copy(side).wait()
    press[0] = xrecv[0]
    press[2 * xps + 1] = xrecv[1]
    y_halo[...] = yrecv[...]
    part_y_end(tp, 0)


def solve_pressure(divergence, slab, substrate, spread):
    n_wide, n_narrow = lax.axis_size("wide"), lax.axis_size("narrow")
    x_local, rows, n_z = divergence.shape
    n_y = rows * n_narrow
    xps = x_local // 2
    tables = [jnp.asarray(t) for t in pressure_tables(n_y, n_z, n_narrow)]
    dma = pltpu.SemaphoreType.DMA
    field = (xps, n_y, 128)
    turned = (n_narrow, xps, rows, 128)
    chunk_rows = n_y // n_wide
    side = math.isqrt(n_wide)
    planes, part_rows, depth = substrate.shape
    half = planes * part_rows // 2
    part = (planes + 2 * DEEP, part_rows + 2 * PAD, depth)
    any_space = pl.BlockSpec(memory_space=pl.ANY)
    return pl.pallas_call(
        functools.partial(pressure_kernel, n_wide, n_narrow),
        out_shape=[
            jax.ShapeDtypeStruct((x_local + 2, rows, n_z), F32),
            jax.ShapeDtypeStruct((2, x_local, n_z), F32),
            jax.ShapeDtypeStruct(part, F32),
            jax.ShapeDtypeStruct(part, F32),
        ],
        in_specs=[VM, VM, VM, VM] + [any_space] * 8 + [VM, VM],
        out_specs=[VM] * 4,
        scratch_shapes=[pltpu.VMEM(t.shape, BF16) for t in tables[:8]]
        + [
            pltpu.VMEM(turned, F32),
            pltpu.VMEM(field, F32),
            pltpu.VMEM(field, F32),
            pltpu.VMEM(turned, F32),
            pltpu.VMEM(turned, F32),
            pltpu.VMEM((2, n_y, 128), F32),
            pltpu.VMEM((GROUPS, 2, n_y, 128), F32),
            pltpu.VMEM((GROUPS, n_y, 128), F32),
            pltpu.VMEM((GROUPS, n_wide, chunk_rows, 128), F32),
            pltpu.VMEM((GROUPS, n_wide, chunk_rows, 128), F32),
            pltpu.VMEM((GROUPS, n_y, 128), F32),
            pltpu.VMEM((2, rows, n_z), F32),
            pltpu.VMEM((2, x_local, n_z), F32),
            pltpu.VMEM((2, x_local, n_z), F32),
            pltpu.VMEM((2, 2, side, half // 2, depth), F32),
            pltpu.VMEM((2, 2, side, half // 2, depth), F32),
            pltpu.VMEM((2, 2, side, half, depth), F32),
            pltpu.VMEM((2, side, half, depth), F32),
            pltpu.VMEM((2, side, half, depth), F32),
            pltpu.VMEM((2, 2, DEEP, part_rows, depth), F32),
            dma((GROUPS, n_narrow)),
            dma((GROUPS, n_narrow)),
            dma((GROUPS, n_narrow)),
            dma((GROUPS, n_narrow)),
            dma((GROUPS,)),
            dma((GROUPS,)),
            dma((GROUPS,)),
            dma((GROUPS,)),
            dma((4,)),
            dma((4,)),
            dma((2, 2, 3)),
            dma((2, 2, 3)),
            dma((2, side)),
            dma((2, side)),
            dma((2, 4)),
            dma((2, 4)),
            dma((8,)),
        ],
        compiler_params=pltpu.CompilerParams(
            collective_id=1, has_side_effects=True, vmem_limit_bytes=32 * 2**20
        ),
        name="pressure",
    )(
        divergence.reshape(xps, 2, rows, n_z),
        slab.reshape(side, side, 2 * half, depth),
        substrate, spread, *tables,
    )


def conduct(step, span, source, coefficient, target):
    planes, rows, depth = coefficient.shape
    lane = lax.broadcasted_iota(jnp.int32, (rows, depth), 1)

    def plane(x, c):
        p = source[x]
        around = source[x + 1] + source[x - 1] + pltpu.roll(p, 1, 0) + pltpu.roll(p, rows - 1, 0)
        around += jnp.where(lane == 0, 0.0, pltpu.roll(p, 1, 1))
        around += jnp.where(lane == depth - 1, 0.0, pltpu.roll(p, depth - 1, 1))
        new = p + coefficient[x] * (around - 6.0 * p)
        if step == STEPS - 1:
            target[x - DEEP] = new[PAD:rows - PAD]
        else:
            target[x] = new
        return c

    lax.fori_loop(*span, plane, 0, unroll=2)


def y_step(plane, before, after, ahead):
    rows = plane.shape[0]
    row = lax.broadcasted_iota(jnp.int32, plane.shape, 0)
    if ahead:
        return jnp.where(row == rows - 1, after, pltpu.roll(plane, rows - 1, 0))
    return jnp.where(row == 0, before, pltpu.roll(plane, 1, 0))


def project_kernel(lead, trail, y_halo, tp, cp, current, out, part, tq, tr):
    step = pl.program_id(0)
    planes, n_z = current.shape[1], current.shape[3]
    total = tp.shape[0]
    for i in range(2 * STEPS):

        @pl.when(step == i)
        def _():
            first, last = i // 2 + 1, total - i // 2 - 1
            span = (first, total // 2) if i % 2 == 0 else (total // 2, last)
            conduct(i // 2, span, (tp, tq, tr)[i // 2], cp, (tq, tr, part)[i // 2])

    block = [lead[0], lead[1], trail[0], trail[1]]
    for i in range(planes):
        x = step * planes + i
        p = block[i + 1]
        before = y_halo[0, pl.ds(x, 1)]
        after = y_halo[1, pl.ds(x, 1)]
        out[0, i] = current[0, i] - (block[i + 2] - block[i]) * 0.5
        out[1, i] = current[1, i] - 0.5 * (
            y_step(p, before, after, True) - y_step(p, before, after, False)
        )
        out[2, i] = current[2, i] - 0.5 * (pltpu.roll(p, n_z - 1, 1) - pltpu.roll(p, 1, 1))


def project(current, press, y_halo, tp, cp):
    _, x_local, rows, n_z = current.shape
    planes = 2
    spec = pl.BlockSpec((3, planes, rows, n_z), lambda i: (0, i, 0, 0))
    part = (tp.shape[0] - 2 * DEEP, tp.shape[1] - 2 * PAD, tp.shape[2])
    return pl.pallas_call(
        project_kernel,
        grid=(x_local // planes,),
        out_shape=[jax.ShapeDtypeStruct(current.shape, F32), jax.ShapeDtypeStruct(part, F32)],
        in_specs=[
            pl.BlockSpec((planes, rows, n_z), lambda i: (i, 0, 0)),
            pl.BlockSpec((planes, rows, n_z), lambda i: (i + 1, 0, 0)),
            VM, VM, VM, spec,
        ],
        out_specs=[spec, pl.BlockSpec(part, lambda i: (0, 0, 0))],
        scratch_shapes=[pltpu.VMEM(tp.shape, F32), pltpu.VMEM(tp.shape, F32)],
        compiler_params=pltpu.CompilerParams(vmem_limit_bytes=20 * 2**20),
        name="projection",
    )(press, press, y_halo, tp, cp, current)


def per_device(
    material_flow_vector,
    tool_push_density,
    tool_warmth_excess,
    substrate_warmth_excess,
    spread_coefficient,
    source_owner_sheet,
    source_part_line,
):
    current, divergence, heat = flow(material_flow_vector, tool_push_density, tool_warmth_excess)
    slab_ids = source_owner_sheet[:, 0]
    slab_count = lax.axis_size("wide")
    component_lines = substrate_warmth_excess.shape[0] * substrate_warmth_excess.shape[1]
    target = slab_ids * component_lines + source_part_line
    partial_value = slab_heat(target, heat, slab_count * component_lines)
    solved = solve_pressure(
        divergence, partial_value, substrate_warmth_excess, spread_coefficient
    )
    return tuple(project(current, *solved))


def solution(mesh):
    return jax.shard_map(
        per_device,
        mesh=mesh,
        in_specs=(
            P(None, "wide", "narrow", None),
            P(None, "wide", "narrow", None),
            P("wide", "narrow", None),
            P("wide", "narrow", None),
            P("wide", "narrow", None),
            P(("wide", "narrow"), None),
            P(("wide", "narrow")),
        ),
        out_specs=(P(None, "wide", "narrow", None), P("wide", "narrow", None)),
        check_vma=False,
    )
```
